32 devices in a mesh: chan: 16 (over z, x, core), tm: 2 (over y).
Axes of the slice: x: 2, y: 2, z: 4, core: 2. Of those that a mesh axis runs over, the one named last changes fastest.
Arguments:
- spectra: bfloat16 [16, 512, 2, 2048], P('tm', 'chan'), may hold values from -74 to 74
- src_block: int32 [2], replicated, may hold values from 0 to 15
- quality: int32 [512], P('chan'), may hold values 0 or 1
Outputs:
- stacked: float32 [32, 2, 512, 512], P('tm', None, 'chan')
The draws below stay inside these ranges and needn't reach their ends.
All inputs are finite; a program needn't handle non-finite values. No bound on the sum of `quality` on one device may be relied on, other than what follows from the above.
Results may differ from the reference program's by a relative error of at most 0.0054.
Values may be sent and summed in bfloat16 or wider, within the bound.
No kernel may reach another device: no remote copies, remote signals or barrier semaphores. Data moves between devices by JAX's collectives and lax.ppermute only.
A program may use at most 64 MiB of HBM per device.

```python
import math
import jax
import jax.numpy as jnp
from jax import lax

F = 2048
LAG = 512
STEPS = 2
CH_DEV = 32
W_DEV = 8
CHANNELS = 512
WINDOWS = 16
N_CHAN = 16
N_TM = 2


def draw_spectra(key, part):
    first_key, second_key, third_key = jax.random.split(key, 3)
    base_values = jnp.clip(jax.random.normal(first_key, (WINDOWS, CHANNELS, 2, F), jnp.float32), -6.0, 6.0)
    levels = jnp.exp(jax.random.uniform(second_key, (WINDOWS, CHANNELS, 1, 1), jnp.float32, -1.5, 1.5))
    colours = jnp.exp(jax.random.uniform(third_key, (1, 1, 1, F), jnp.float32, -1.0, 1.0))
    return (base_values * levels * colours).astype(jnp.bfloat16)


def touch_ends(values, own_key, least, high):
    longest = values.shape.index(max(values.shape))
    spots = []
    for shift in (0, 1):
        where = [jax.random.randint(jax.random.fold_in(own_key, axis), (), 0, length) for axis, length in enumerate(values.shape)]
        where[longest] = (where[longest] + shift) % values.shape[longest]
        spots.append(tuple(where))
    return values.at[spots[0]].set(least).at[spots[1]].set(high)


def setup_inputs(seed: int = 0) -> dict:
    streams_of = jax.random.split(jax.random.key(seed), 4)
    return {
        "spectra": draw_spectra(jax.random.fold_in(streams_of[3], 71), 0),
        "src_block": jax.random.randint(streams_of[1], (STEPS,), 0, N_CHAN).astype(jnp.int32),
        "quality": touch_ends((jax.random.randint(streams_of[2], (CHANNELS,), 0, 10) < 9).astype(jnp.int32), jax.random.fold_in(streams_of[2], 1), 0, 1),
    }


def normalize(masked):
    mean_power = lax.optimization_barrier(jnp.mean(masked * masked, axis=(2, 3), keepdims=True))
    return (masked / jnp.sqrt(mean_power + 1e-06)).astype(jnp.bfloat16)

def lag_table(num_bins, num_lags, windows):
    freq_bins = jnp.arange(num_bins, dtype=jnp.int32)[:, None]
    shifts = jnp.arange(num_lags, dtype=jnp.int32)[None, :] - num_lags // 2
    phases = jnp.mod(freq_bins * shifts, 2 * num_bins).astype(jnp.float32) * (math.pi / num_bins)
    scaling = 1.0 / math.sqrt(2.0 * num_bins * windows)
    return jnp.concatenate([jnp.cos(phases) * scaling, -jnp.sin(phases) * scaling], 0).astype(jnp.bfloat16)

def reference(spectra, src_block, quality):
    masked = spectra.astype(jnp.float32) * quality.astype(jnp.float32)[None, :, None, None]
    whitened = normalize(masked)
    lag_weights = lag_table(F, LAG, WINDOWS).astype(jnp.float32)
    groups = whitened.reshape(N_TM, W_DEV, CHANNELS, 2, F)
    blk_size = CH_DEV * min(N_CHAN, 16)
    num_blocks = CHANNELS // blk_size
    results = []
    for step_index in range(STEPS):
        first_row = (src_block[step_index] * CH_DEV).astype(jnp.int32)
        stacked = jnp.zeros((CH_DEV, CHANNELS, LAG), jnp.float32)
        for group_index in range(N_TM):
            window_group = groups[group_index]
            source = lax.dynamic_slice_in_dim(window_group, first_row, CH_DEV, 1).astype(jnp.float32)

            def one_block(receivers):
                receivers = receivers.astype(jnp.float32)
                hp = lax.Precision.HIGHEST
                real_part = jnp.einsum('wsf,wcf->scf', source[:, :, 0], receivers[:, :, 0], precision=hp) + jnp.einsum('wsf,wcf->scf', source[:, :, 1], receivers[:, :, 1], precision=hp)
                imag_part = jnp.einsum('wsf,wcf->scf', source[:, :, 0], receivers[:, :, 1], precision=hp) - jnp.einsum('wsf,wcf->scf', source[:, :, 1], receivers[:, :, 0], precision=hp)
                cross_spec = jnp.concatenate([real_part, imag_part], -1).astype(jnp.bfloat16).astype(jnp.float32)
                return jnp.einsum('scg,gl->scl', cross_spec, lag_weights, precision=hp)
            blocked = window_group.reshape(W_DEV, num_blocks, blk_size, 2, F).transpose(1, 0, 2, 3, 4)
            mapped = lax.map(one_block, blocked)
            stacked = stacked + mapped.transpose(1, 0, 2, 3).reshape(CH_DEV, CHANNELS, LAG)
        results.append(stacked)
    return jnp.stack(results, 1)
```

```python
import math

import jax
import jax.numpy as jnp
from jax import lax
from jax.experimental import pallas as pl
from jax.experimental.pallas import tpu as pltpu
from jax.sharding import PartitionSpec as P

LAG = 512
STEPS = 2
BINS = 256
LANES = 128
PACK = 16


def lag_table(num_bins, num_lags, windows):
    freq_bins = jnp.arange(num_bins, dtype=jnp.int32)[:, None]
    shifts = jnp.arange(num_lags, dtype=jnp.int32)[None, :] - num_lags // 2
    phases = jnp.mod(freq_bins * shifts, 2 * num_bins).astype(jnp.float32) * (math.pi / num_bins)
    scaling = 1.0 / math.sqrt(2.0 * num_bins * windows)
    return jnp.stack([jnp.cos(phases) * scaling, -jnp.sin(phases) * scaling], 0).astype(
        jnp.bfloat16
    )


def lags_kernel(place, own_ref, other_ref, rcv_ref, table_ref, out_ref, src, cross, total):
    rows, _, bins = own_ref.shape
    windows, _, channels, _ = rcv_ref.shape
    block = pl.program_id(0)
    own_half = place[1]

    @pl.when(block == 0)
    def _():
        total[...] = jnp.zeros_like(total)

    src[:rows] = own_ref[...].astype(jnp.float32)
    src[rows:] = other_ref[...].astype(jnp.float32)

    def section(index, carry):
        lane = pl.multiple_of((index // (channels // PACK)) * LANES, LANES)
        chan = pl.multiple_of((index % (channels // PACK)) * PACK, PACK)
        received = [
            [
                rcv_ref[w, part, pl.ds(chan, PACK), pl.ds(lane, LANES)].astype(jnp.float32)
                for part in range(2)
            ]
            for w in range(windows)
        ]

        def source(s, inner):
            re = im = None
            for w in range(windows):
                s_re = src[s, pl.ds(2 * w, 1), pl.ds(lane, LANES)]
                s_im = src[s, pl.ds(2 * w + 1, 1), pl.ds(lane, LANES)]
                c_re, c_im = received[w]
                re_w = s_re * c_re + s_im * c_im
                im_w = s_re * c_im - s_im * c_re
                re = re_w if re is None else re + re_w
                im = im_w if im is None else im + im_w
            row = (s + own_half * rows) % (2 * rows)
            cross[row, pl.ds(chan, PACK), pl.ds(lane, LANES)] = re.astype(jnp.bfloat16)
            cross[row, pl.ds(chan, PACK), pl.ds(lane + bins, LANES)] = im.astype(jnp.bfloat16)
            return inner

        return lax.fori_loop(0, 2 * rows, source, carry, unroll=4)

    lax.fori_loop(0, (bins // LANES) * (channels // PACK), section, 0)
    total[...] += jnp.dot(
        cross[...].reshape(2 * rows * channels, 2 * bins),
        table_ref[...].reshape(2 * bins, LAG),
        preferred_element_type=jnp.float32,
    )

    @pl.when(block == pl.num_programs(0) - 1)
    def _():
        out_ref[...] = total[...].reshape(out_ref.shape).astype(out_ref.dtype)


def lags(place, own, other, receivers, table, dtype):
    windows, _, channels, num_bins = receivers.shape
    rows = own.shape[0] // 2
    source = pl.BlockSpec((rows, 2 * windows, BINS), lambda i, p: (p[0], 0, i))
    return pl.pallas_call(
        lags_kernel,
        grid_spec=pltpu.PrefetchScalarGridSpec(
            num_scalar_prefetch=1,
            grid=(num_bins // BINS,),
            in_specs=[
                source,
                source,
                pl.BlockSpec((windows, 2, channels, BINS), lambda i, p: (0, 0, 0, i)),
                pl.BlockSpec((2, BINS, LAG), lambda i, p: (0, i, 0)),
            ],
            out_specs=pl.BlockSpec((2 * rows, channels, LAG), lambda i, p: (0, 0, 0)),
            scratch_shapes=[
                pltpu.VMEM((2 * rows, 2 * windows, BINS), jnp.float32),
                pltpu.VMEM((2 * rows, channels, 2 * BINS), jnp.bfloat16),
                pltpu.VMEM((2 * rows * channels, LAG), jnp.float32),
            ],
        ),
        out_shape=jax.ShapeDtypeStruct((2 * rows, channels, LAG), dtype),
        compiler_params=pltpu.CompilerParams(vmem_limit_bytes=32 * 1024 * 1024),
        cost_estimate=pl.CostEstimate(
            flops=2 * (2 * rows) * channels * 2 * num_bins * LAG * 4,
            bytes_accessed=12 * 1024 * 1024,
            transcendentals=0,
        ),
    )(place, own, other, receivers, table)


def per_device(spectra, src_block, quality):
    windows, channels, _, num_bins = spectra.shape
    tm = lax.axis_size("tm")
    chan = lax.axis_size("chan")
    me = lax.axis_index("chan")
    core = me % 2
    my_tm = lax.axis_index("tm")
    siblings = [(i, i ^ 1) for i in range(chan)]
    same_core = [list(range(c, chan, 2)) for c in range(2)]
    partners = [(i, i ^ 1) for i in range(tm)]

    masked = spectra.astype(jnp.float32) * quality.astype(jnp.float32)[None, :, None, None]
    power = jnp.mean(masked * masked, axis=(2, 3), keepdims=True)
    white = (masked / jnp.sqrt(power + 1e-06)).astype(jnp.bfloat16)
    receivers = white.transpose(0, 2, 1, 3)
    rows = channels // 4
    halves = (
        white.reshape(windows, 2, 2, rows, 2, num_bins)
        .transpose(2, 1, 3, 0, 4, 5)
        .reshape(2, 2 * rows, 2 * windows, num_bins)
    )
    mine = lax.dynamic_index_in_dim(halves, core, 0, keepdims=False)
    given = lax.ppermute(
        lax.dynamic_index_in_dim(halves, 1 - core, 0, keepdims=False), "chan", siblings
    )
    table = lag_table(num_bins, LAG, windows * tm)

    own = []
    for step in range(STEPS):
        owner = src_block[step]
        part = jnp.where(owner == me, mine, jnp.where(owner == (me ^ 1), given, 0))
        own.append(lax.psum(part, "chan", axis_index_groups=same_core))
    other = [lax.ppermute(part, "chan", siblings) for part in own]
    outs = []
    for step in range(STEPS):
        args = (own[step], other[step], receivers, table)
        sent = lags(jnp.stack([1 - my_tm, core]), *args, jnp.bfloat16)
        come = lax.ppermute(sent, "tm", partners)
        kept = lags(jnp.stack([my_tm, core]), *args, jnp.float32)
        outs.append(kept + come.astype(jnp.float32))
    return jnp.stack(outs, 1)


def solution(mesh):
    return jax.shard_map(
        per_device,
        mesh=mesh,
        in_specs=(P("tm", "chan", None, None), P(), P("chan")),
        out_specs=P("tm", None, "chan", None),
        check_vma=False,
    )
```

```python
import math

import jax
import jax.numpy as jnp
import numpy as np
from jax import lax
from jax.experimental import pallas as pl
from jax.experimental.pallas import tpu as pltpu
from jax.sharding import PartitionSpec as P

LAG = 512
STEPS = 2
BINS = 256
LANES = 128
LINE = 4


def lag_table(num_bins, num_lags, windows):
    freq_bins = np.arange(num_bins, dtype=np.int64)[:, None]
    shifts = np.arange(num_lags, dtype=np.int64)[None, :] - num_lags // 2
    phases = np.mod(freq_bins * shifts, 2 * num_bins).astype(np.float32) * np.float32(
        math.pi / num_bins
    )
    scaling = np.float32(1.0 / math.sqrt(2.0 * num_bins * windows))
    table = np.stack([np.cos(phases) * scaling, -np.sin(phases) * scaling], 0)
    return jnp.asarray(table.astype(jnp.bfloat16))


def tree_sum(terms):
    while len(terms) > 1:
        terms = [terms[i] + terms[i + 1] for i in range(0, len(terms), 2)]
    return terms[0]


def lags_kernel(place, own_ref, mate_ref, other_ref, rcv_ref, table_ref, out_ref, src, cross, total):
    rows = own_ref.shape[0]
    sources = 4 * rows
    windows, _, channels, bins = rcv_ref.shape
    block = pl.program_id(0)
    core, column, row_xor = place[0], place[1], place[2]

    @pl.when(block == 0)
    def _():
        total[...] = jnp.zeros_like(total)

    src[:rows] = own_ref[...].astype(jnp.float32)
    src[rows : 2 * rows] = mate_ref[...].astype(jnp.float32)
    src[2 * rows :] = other_ref[...].astype(jnp.float32)

    def section(index, carry):
        lane = pl.multiple_of(index * LANES, LANES)
        received = [
            [rcv_ref[w, part, :, pl.ds(lane, LANES)] for part in range(2)] for w in range(windows)
        ]

        def source(s, inner):
            sent = [
                jnp.broadcast_to(
                    src[s, pl.ds(i, 1), pl.ds(lane, LANES)], (channels, LANES)
                ).astype(jnp.bfloat16)
                for i in range(2 * windows)
            ]
            re = []
            im = []
            for w in range(windows):
                s_re, s_im = sent[2 * w], sent[2 * w + 1]
                c_re, c_im = received[w]
                re.append(s_re * c_re + s_im * c_im)
                im.append(s_re * c_im - s_im * c_re)
            half = (s // (2 * rows)) ^ core
            side = ((s // rows) % 2) ^ column
            row = (half * 2 + side) * rows + ((s % rows) ^ row_xor)
            cross[row, :, pl.ds(lane, LANES)] = tree_sum(re)
            cross[row, :, pl.ds(lane + bins, LANES)] = tree_sum(im)
            return inner

        return lax.fori_loop(0, sources, source, carry, unroll=4)

    lax.fori_loop(0, bins // LANES, section, 0)
    total[...] += jnp.dot(
        cross[...].reshape(sources * channels, 2 * bins),
        table_ref[...].reshape(2 * bins, LAG),
        preferred_element_type=jnp.float32,
    )

    @pl.when(block == pl.num_programs(0) - 1)
    def _():
        out_ref[...] = total[...].reshape(out_ref.shape).astype(out_ref.dtype)


def lags(place, own, mate, other, receivers, table, dtype):
    windows, _, channels, num_bins = receivers.shape
    rows = own.shape[0]
    sources = 4 * rows
    source = lambda count: pl.BlockSpec((count, 2 * windows, BINS), lambda i, p: (0, 0, i))
    return pl.pallas_call(
        lags_kernel,
        grid_spec=pltpu.PrefetchScalarGridSpec(
            num_scalar_prefetch=1,
            grid=(num_bins // BINS,),
            in_specs=[
                source(rows),
                source(rows),
                source(2 * rows),
                pl.BlockSpec((windows, 2, channels, BINS), lambda i, p: (0, 0, 0, i)),
                pl.BlockSpec((2, BINS, LAG), lambda i, p: (0, i, 0)),
            ],
            out_specs=pl.BlockSpec((sources, channels, LAG), lambda i, p: (0, 0, 0)),
            scratch_shapes=[
                pltpu.VMEM((sources, 2 * windows, BINS), jnp.float32),
                pltpu.VMEM((sources, channels, 2 * BINS), jnp.bfloat16),
                pltpu.VMEM((sources * channels, LAG), jnp.float32),
            ],
        ),
        out_shape=jax.ShapeDtypeStruct((sources, channels, LAG), dtype),
        compiler_params=pltpu.CompilerParams(vmem_limit_bytes=24 * 1024 * 1024),
        cost_estimate=pl.CostEstimate(
            flops=2 * sources * channels * 2 * num_bins * LAG * 4,
            bytes_accessed=8 * 1024 * 1024,
            transcendentals=0,
        ),
    )(place, own, mate, other, receivers, table)


def per_device(spectra, src_block, quality):
    windows, channels, _, num_bins = spectra.shape
    tm = lax.axis_size("tm")
    chan = lax.axis_size("chan")
    me = lax.axis_index("chan")
    my_tm = lax.axis_index("tm")
    core, column, row = me % 2, (me // 2) % 2, (me // 4) % LINE
    swap = lambda value, bits: lax.ppermute(value, "chan", [(i, i ^ bits) for i in range(chan)])
    pick = lambda value, index: lax.dynamic_index_in_dim(value, index, 0, keepdims=False)

    masked = spectra.astype(jnp.float32) * quality.astype(jnp.float32)[None, :, None, None]
    power = jnp.mean(masked * masked, axis=(2, 3), keepdims=True)
    white = (masked / jnp.sqrt(power + 1e-06)).astype(jnp.bfloat16)
    receivers = white.transpose(0, 2, 1, 3)
    block = white.transpose(1, 0, 2, 3).reshape(tm, 2, 2, LINE, -1, 2 * windows, num_bins)
    by_core = block.transpose(1, 0, 2, 3, 4, 5, 6)
    mine = pick(by_core, core)
    given = swap(pick(by_core, 1 - core), 1)
    table = lag_table(num_bins, LAG, windows * tm)
    place = jnp.stack([core, column, row])

    def unit(step, part):
        owner = src_block[step]
        have = jnp.where(owner % 2 == core, pick(mine, part), pick(given, part))
        if chan > 4 * LINE:
            low = 4 * LINE
            groups = [list(range(i, chan, low)) for i in range(low)]
            have = jnp.where(owner // 2 == me // 2, have, 0)
            have = lax.psum(have, "chan", axis_index_groups=groups)
        quarter = jnp.where(
            (owner // 2) % 2 == column, pick(have, column), swap(pick(have, 1 - column), 2)
        )
        far = row ^ ((owner // 4) % LINE)
        piece = pick(quarter, row)
        for d in range(1, LINE):
            piece = jnp.where(far == d, swap(pick(quarter, row ^ d), 4 * d), piece)
        own = jnp.concatenate([piece] + [swap(piece, 4 * d) for d in range(1, LINE)], 0)
        mate = swap(own, 2)
        other = swap(jnp.concatenate([own, mate], 0), 1)
        return own, mate, other

    sources = [[unit(step, part) for part in (1 - my_tm, my_tm)] for step in range(STEPS)]
    partners = [(i, i ^ 1) for i in range(tm)]
    outs = []
    for step in range(STEPS):
        sent = lags(place, *sources[step][0], receivers, table, jnp.bfloat16)
        come = lax.ppermute(sent, "tm", partners)
        kept = lags(place, *sources[step][1], receivers, table, jnp.float32)
        outs.append(kept + come.astype(jnp.float32))
    return jnp.stack(outs, 1)


def solution(mesh):
    return jax.shard_map(
        per_device,
        mesh=mesh,
        in_specs=(P("tm", "chan", None, None), P(), P("chan")),
        out_specs=P("tm", None, "chan", None),
        check_vma=False,
    )
```

```python
import math

import jax
import jax.numpy as jnp
import numpy as np
from jax import lax
from jax.experimental import pallas as pl
from jax.experimental.pallas import tpu as pltpu
from jax.sharding import PartitionSpec as P

LAG = 512
STEPS = 2
LANES = 128
PACK = 16
BLOCKS = 8


def lag_table(num_bins, num_lags, windows):
    freq_bins = np.arange(num_bins, dtype=np.int64)[:, None]
    shifts = np.arange(num_lags, dtype=np.int64)[None, :] - num_lags // 2
    phases = np.mod(freq_bins * shifts, 2 * num_bins).astype(np.float32) * np.float32(
        math.pi / num_bins
    )
    scaling = np.float32(1.0 / math.sqrt(2.0 * num_bins * windows))
    table = np.stack([np.cos(phases) * scaling, -np.sin(phases) * scaling], 0)
    table = table.reshape(2, BLOCKS, -1, num_lags).transpose(1, 0, 2, 3)
    return jnp.asarray(table.reshape(BLOCKS, -1, num_lags).astype(jnp.bfloat16))


def tree_sum(terms):
    while len(terms) > 1:
        terms = [terms[i] + terms[i + 1] for i in range(0, len(terms), 2)]
    return terms[0]


def lags_kernel(place, own_ref, other_ref, rcv_ref, table_ref, out_ref, src, cross, total):
    half, windows, _, _, bins = own_ref.shape
    channels = rcv_ref.shape[2]
    sources = out_ref.shape[0]
    order = place[0]
    first = pl.multiple_of(place[1] * sources, sources)

    total[...] = jnp.zeros_like(total)
    cross[1] = jnp.zeros_like(cross[1])

    def product(index):
        total[...] += jnp.dot(
            cross[index % 2].reshape(sources * channels, 2 * bins),
            table_ref[index ^ order],
            preferred_element_type=jnp.float32,
        )

    def spectra(index, ref, entry):
        slot = index % 2
        for w in range(windows):
            for part in range(2):
                src[2 * w + part] = ref[entry, w, part, pl.ds(first, sources), :].astype(
                    jnp.float32
                )
        for lane in range(0, bins, LANES):
            here = pl.multiple_of((index ^ order) * bins + lane, LANES)
            groups = range(0, channels, PACK)
            received = [
                [
                    [rcv_ref[w, part, pl.ds(chan, PACK), pl.ds(here, LANES)] for chan in groups]
                    for part in range(2)
                ]
                for w in range(windows)
            ]
            for s in range(sources):
                sent = [
                    jnp.broadcast_to(
                        src[i, pl.ds(s, 1), pl.ds(lane, LANES)], (PACK, LANES)
                    ).astype(jnp.bfloat16)
                    for i in range(2 * windows)
                ]
                for g, chan in enumerate(groups):
                    re = []
                    im = []
                    for w in range(windows):
                        s_re, s_im = sent[2 * w], sent[2 * w + 1]
                        c_re, c_im = received[w][0][g], received[w][1][g]
                        re.append(s_re * c_re + s_im * c_im)
                        im.append(s_re * c_im - s_im * c_re)
                    rows = pl.ds(chan, PACK)
                    cross[slot, s, rows, pl.ds(lane, LANES)] = tree_sum(re)
                    cross[slot, s, rows, pl.ds(bins + lane, LANES)] = tree_sum(im)

    for ref, start in ((own_ref, 0), (other_ref, half)):

        def body(entry, carry, ref=ref, start=start):
            index = entry + start
            spectra(index, ref, entry)
            product(index - 1 + 2 * (index == 0))
            return carry

        lax.fori_loop(0, half, body, 0)
    product(2 * half - 1)
    out_ref[...] = total[...].reshape(out_ref.shape).astype(out_ref.dtype)


def lags(order, part, own, other, receivers, table, dtype):
    half, windows, _, _, bins = own.shape
    channels = receivers.shape[2]
    sources = PACK
    vmem = pl.BlockSpec(memory_space=pltpu.VMEM)
    return pl.pallas_call(
        lags_kernel,
        in_specs=[pl.BlockSpec(memory_space=pltpu.SMEM)] + [vmem] * 4,
        out_specs=vmem,
        scratch_shapes=[
            pltpu.VMEM((2 * windows, sources, bins), jnp.float32),
            pltpu.VMEM((2, sources, channels, 2 * bins), jnp.bfloat16),
            pltpu.VMEM((sources * channels, LAG), jnp.float32),
        ],
        out_shape=jax.ShapeDtypeStruct((sources, channels, LAG), dtype),
        compiler_params=pltpu.CompilerParams(vmem_limit_bytes=24 * 1024 * 1024),
        cost_estimate=pl.CostEstimate(
            flops=2 * sources * channels * 4 * half * bins * LAG * 4,
            bytes_accessed=8 * 1024 * 1024,
            transcendentals=0,
        ),
    )(jnp.stack([order, part]), own, other, receivers, table)


def per_device(spectra, src_block, quality):
    windows, channels, _, num_bins = spectra.shape
    tm = lax.axis_size("tm")
    chan = lax.axis_size("chan")
    me = lax.axis_index("chan")
    my_tm = lax.axis_index("tm")
    bit = lambda value, place: (value >> place) & 1
    swap = lambda value, place: lax.ppermute(
        value, "chan", [(i, i ^ (1 << place)) for i in range(chan)]
    )

    masked = spectra.astype(jnp.float32) * quality.astype(jnp.float32)[None, :, None, None]
    power = jnp.mean(masked * masked, axis=(2, 3), keepdims=True)
    receivers = (masked / jnp.sqrt(power + 1e-06)).astype(jnp.bfloat16).transpose(0, 2, 1, 3)
    table = lag_table(num_bins, LAG, windows * tm)
    order = bit(me, 0) * 4 + bit(me, 1) * 2 + bit(me, 2)

    def part_of(value, which):
        width = value.shape[3] // 2
        return lax.dynamic_slice_in_dim(value, which * width, width, 3)

    mine = part_of(receivers, bit(me, 0))
    given = swap(part_of(receivers, 1 - bit(me, 0)), 0)

    def block(owner):
        have = jnp.where(bit(owner, 0) == bit(me, 0), mine, given)
        if chan > 16:
            groups = [list(range(i, chan, 16)) for i in range(16)]
            have = jnp.where(owner // 2 == me // 2, have, 0)
            have = lax.psum(have, "chan", axis_index_groups=groups)
        for place in (1, 2):
            here = bit(me, place)
            come = swap(part_of(have, 1 - here), place)
            have = jnp.where(bit(owner, place) == here, part_of(have, here), come)
        have = jnp.where(bit(owner, 3) == bit(me, 3), have, swap(have, 3))[None]
        for place in (2, 1):
            have = jnp.concatenate([have, swap(have, place)], 0)
        return have, swap(have, 0)

    sources = [block(src_block[step]) for step in range(STEPS)]
    partners = [(i, i ^ 1) for i in range(tm)]
    outs = []
    for step in range(STEPS):
        sent = lags(order, 1 - my_tm, *sources[step], receivers, table, jnp.bfloat16)
        come = lax.ppermute(sent, "tm", partners)
        kept = lags(order, my_tm, *sources[step], receivers, table, jnp.float32)
        outs.append(kept + come.astype(jnp.float32))
    return jnp.stack(outs, 1)


def solution(mesh):
    return jax.shard_map(
        per_device,
        mesh=mesh,
        in_specs=(P("tm", "chan", None, None), P(), P("chan")),
        out_specs=P("tm", None, "chan", None),
        check_vma=False,
    )
```

```python
import math

import jax
import jax.numpy as jnp
import numpy as np
from jax import lax
from jax.experimental import pallas as pl
from jax.experimental.pallas import tpu as pltpu
from jax.sharding import PartitionSpec as P

LAG = 512
STEPS = 2
LANES = 128
PACK = 16
BLOCKS = 8


def lag_table(num_bins, num_lags, windows):
    freq_bins = np.arange(num_bins, dtype=np.int64)[:, None]
    shifts = np.arange(num_lags, dtype=np.int64)[None, :] - num_lags // 2
    phases = np.mod(freq_bins * shifts, 2 * num_bins).astype(np.float32) * np.float32(
        math.pi / num_bins
    )
    scaling = np.float32(1.0 / math.sqrt(2.0 * num_bins * windows))
    table = np.stack([np.cos(phases) * scaling, -np.sin(phases) * scaling], 0)
    table = table.reshape(2, BLOCKS, -1, num_lags).transpose(1, 0, 2, 3)
    return jnp.asarray(table.reshape(BLOCKS, -1, num_lags).astype(jnp.bfloat16))


def lags_kernel(
    place, own_ref, other_ref, scale_ref, rcv_ref, table_ref, out_ref, src, even, odd, total
):
    half, windows, _, _, bins = own_ref.shape
    channels = rcv_ref.shape[2]
    sources = out_ref.shape[0]
    order = place[0]
    first = pl.multiple_of(place[1] * sources, sources)
    groups = range(0, channels, PACK)

    def widen(w, carry):
        scale = scale_ref[w, pl.ds(first, sources), :]
        for ref, start in ((own_ref, 0), (other_ref, half)):
            for entry in range(half):
                for part in range(2):
                    for lane in range(0, bins, LANES):
                        lanes = pl.ds(lane, LANES)
                        raw = ref[entry, w, part, pl.ds(first, sources), lanes]
                        src[start + entry, 2 * w + part, :, lanes] = (
                            raw.astype(jnp.float32) * scale
                        )
        return carry

    lax.fori_loop(0, windows, widen, 0)
    total[...] = jnp.zeros_like(total)
    odd[...] = jnp.zeros_like(odd)

    def product(index, cross):
        total[...] += jnp.dot(
            cross[...].reshape(sources * channels, 2 * bins),
            table_ref[index ^ order],
            preferred_element_type=jnp.float32,
        )

    def spectra(index, cross):
        for lane in range(0, bins, LANES):
            here = pl.multiple_of((index ^ order) * bins + lane, LANES)
            lanes = pl.ds(lane, LANES)
            received = [
                [
                    [rcv_ref[w, part, pl.ds(chan, PACK), pl.ds(here, LANES)] for chan in groups]
                    for part in range(2)
                ]
                for w in range(windows)
            ]
            for s in range(sources):

                def summed(low, high):
                    if high - low > 1:
                        middle = (low + high) // 2
                        left, right = summed(low, middle), summed(middle, high)
                        return [a + b for a, b in zip(left, right)]
                    s_re, s_im = [
                        jnp.broadcast_to(src[index, 2 * low + part, pl.ds(s, 1), lanes], (PACK, LANES))
                        .astype(jnp.bfloat16)
                        for part in range(2)
                    ]
                    values = []
                    for c_re, c_im in zip(*received[low]):
                        values.append(s_re * c_re + s_im * c_im)
                        values.append(s_re * c_im - s_im * c_re)
                    return values

                values = summed(0, windows)
                for g, chan in enumerate(groups):
                    rows = pl.ds(chan, PACK)
                    cross[s, rows, pl.ds(lane, LANES)] = values[2 * g]
                    cross[s, rows, pl.ds(bins + lane, LANES)] = values[2 * g + 1]

    def body(pair, carry):
        index = 2 * pair
        product(jnp.maximum(index - 1, 0), odd)
        spectra(index, even)
        product(index, even)
        spectra(index + 1, odd)
        return carry

    lax.fori_loop(0, half, body, 0)
    product(2 * half - 1, odd)
    out_ref[...] = total[...].reshape(out_ref.shape).astype(out_ref.dtype)


def lags(order, part, own, other, scale, receivers, table, dtype):
    half, windows, _, _, bins = own.shape
    channels = receivers.shape[2]
    sources = PACK
    vmem = pl.BlockSpec(memory_space=pltpu.VMEM)
    return pl.pallas_call(
        lags_kernel,
        in_specs=[pl.BlockSpec(memory_space=pltpu.SMEM)] + [vmem] * 5,
        out_specs=vmem,
        scratch_shapes=[
            pltpu.VMEM((2 * half, 2 * windows, sources, bins), jnp.float32),
            pltpu.VMEM((sources, channels, 2 * bins), jnp.bfloat16),
            pltpu.VMEM((sources, channels, 2 * bins), jnp.bfloat16),
            pltpu.VMEM((sources * channels, LAG), jnp.float32),
        ],
        out_shape=jax.ShapeDtypeStruct((sources, channels, LAG), dtype),
        compiler_params=pltpu.CompilerParams(vmem_limit_bytes=24 * 1024 * 1024),
        cost_estimate=pl.CostEstimate(
            flops=2 * sources * channels * 4 * half * bins * LAG * 4,
            bytes_accessed=8 * 1024 * 1024,
            transcendentals=0,
        ),
    )(jnp.stack([order, part]), own, other, scale, receivers, table)


def per_device(spectra, src_block, quality):
    windows, channels, _, num_bins = spectra.shape
    tm = lax.axis_size("tm")
    chan = lax.axis_size("chan")
    me = lax.axis_index("chan")
    my_tm = lax.axis_index("tm")
    bit = lambda value, place: (value >> place) & 1
    swap = lambda value, place: lax.ppermute(
        value, "chan", [(i, i ^ (1 << place)) for i in range(chan)]
    )

    raw = spectra.transpose(0, 2, 1, 3)
    usable = quality.astype(jnp.float32)[None, :]
    wide = raw.astype(jnp.float32)
    power = jnp.mean(wide * wide, axis=(1, 3)) * usable
    scale = usable / jnp.sqrt(power + 1e-06)
    receivers = (wide * scale[:, None, :, None]).astype(jnp.bfloat16)
    scales = lax.psum(
        jnp.stack([jnp.where(src_block[step] == me, scale, 0) for step in range(STEPS)]), "chan"
    )
    scales = jnp.broadcast_to(scales[..., None], scales.shape + (LANES,))
    table = lag_table(num_bins, LAG, windows * tm)
    order = bit(me, 0) * 4 + bit(me, 1) * 2 + bit(me, 2)

    def part_of(value, which):
        width = value.shape[3] // 2
        return lax.dynamic_slice_in_dim(value, which * width, width, 3)

    mine = part_of(raw, bit(me, 0))
    given = swap(part_of(raw, 1 - bit(me, 0)), 0)

    def block(owner):
        have = jnp.where(bit(owner, 0) == bit(me, 0), mine, given)
        if chan > 16:
            groups = [list(range(i, chan, 16)) for i in range(16)]
            have = jnp.where(owner // 2 == me // 2, have, 0)
            have = lax.psum(have, "chan", axis_index_groups=groups)
        for place in (1, 2):
            here = bit(me, place)
            come = swap(part_of(have, 1 - here), place)
            have = jnp.where(bit(owner, place) == here, part_of(have, here), come)
        have = jnp.where(bit(owner, 3) == bit(me, 3), have, swap(have, 3))[None]
        for place in (2, 1):
            have = jnp.concatenate([have, swap(have, place)], 0)
        return have, swap(have, 0)

    sources = [block(src_block[step]) for step in range(STEPS)]
    partners = [(i, i ^ 1) for i in range(tm)]
    outs = []
    for step in range(STEPS):
        sent = lags(order, 1 - my_tm, *sources[step], scales[step], receivers, table, jnp.bfloat16)
        come = lax.ppermute(sent, "tm", partners)
        kept = lags(order, my_tm, *sources[step], scales[step], receivers, table, jnp.float32)
        outs.append(kept + come.astype(jnp.float32))
    return jnp.stack(outs, 1)


def solution(mesh):
    return jax.shard_map(
        per_device,
        mesh=mesh,
        in_specs=(P("tm", "chan", None, None), P(), P("chan")),
        out_specs=P("tm", None, "chan", None),
        check_vma=False,
    )
```

```python
from functools import partial
import math

import jax
import jax.numpy as jnp
import numpy as np
from jax import lax
from jax.experimental import pallas as pl
from jax.experimental.pallas import tpu as pltpu
from jax.sharding import PartitionSpec as P

LAG = 512
STEPS = 2
LANES = 128
PACK = 16
BLOCKS = 8


def lag_table(num_bins, num_lags, windows):
    freq_bins = np.arange(num_bins, dtype=np.int64)[:, None]
    shifts = np.arange(num_lags, dtype=np.int64)[None, :] - num_lags // 2
    phases = np.mod(freq_bins * shifts, 2 * num_bins).astype(np.float32) * np.float32(
        math.pi / num_bins
    )
    scaling = np.float32(1.0 / math.sqrt(2.0 * num_bins * windows))
    table = np.stack([np.cos(phases) * scaling, -np.sin(phases) * scaling], 0)
    table = table.reshape(2, BLOCKS, -1, num_lags).transpose(1, 0, 2, 3)
    return jnp.asarray(table.reshape(BLOCKS, -1, num_lags).astype(jnp.bfloat16))


def lags_kernel(place, own_ref, other_ref, rcv_ref, table_ref, *refs, resumed, rounded):
    acc_ref, out_ref, src, even, odd = (refs if resumed else (None,) + refs)[:5]
    total = refs[-1] if rounded else out_ref
    blocks, windows, _, _, bins = own_ref.shape
    channels = rcv_ref.shape[2]
    sources = src.shape[2]
    order, first_block = place[0], place[2]
    first = pl.multiple_of(place[1] * sources, sources)
    groups = range(0, channels, PACK)

    def widen(w, carry):
        for start, ref in ((0, own_ref), (blocks, other_ref)):
            for entry in range(blocks):
                for part in range(2):
                    value = ref[entry, w, part, pl.ds(first, sources), :]
                    src[start + entry, 2 * w + part] = value.astype(jnp.float32)
        return carry

    lax.fori_loop(0, windows, widen, 0)

    def block_of(index):
        return (first_block + index % blocks + BLOCKS // 2 * (index // blocks)) ^ order

    def products(index, cross):
        def piece(row, column):
            rows = pl.ds(row * channels, sources // 2 * channels)
            columns = pl.ds(column, LAG // 2)
            share = jnp.dot(
                cross[pl.ds(row, sources // 2)].reshape(-1, 2 * bins),
                table_ref[block_of(index), :, columns],
                preferred_element_type=jnp.float32,
            )
            if index > 0:
                share += total[rows, columns]
            elif resumed:
                share += acc_ref[rows, columns]
            total[rows, columns] = share

        return [
            lambda row=row, column=column: piece(row, column)
            for row in range(0, sources, sources // 2)
            for column in range(0, LAG, LAG // 2)
        ]

    def spectra(index, cross):
        def group(lane, low_source):
            here = pl.multiple_of(block_of(index) * bins + lane, LANES)
            lanes = pl.ds(lane, LANES)
            received = [
                [
                    [rcv_ref[w, part, pl.ds(chan, PACK), pl.ds(here, LANES)] for chan in groups]
                    for part in range(2)
                ]
                for w in range(windows)
            ]
            for s in range(low_source, low_source + 4):

                def summed(low, high):
                    if high - low > 1:
                        middle = (low + high) // 2
                        left, right = summed(low, middle), summed(middle, high)
                        return [a + b for a, b in zip(left, right)]
                    s_re, s_im = [
                        jnp.broadcast_to(
                            src[index, 2 * low + part, pl.ds(s, 1), lanes], (PACK, LANES)
                        ).astype(jnp.bfloat16)
                        for part in range(2)
                    ]
                    values = []
                    for c_re, c_im in zip(*received[low]):
                        values.append(s_re * c_re + s_im * c_im)
                        values.append(s_re * c_im - s_im * c_re)
                    return values

                values = summed(0, windows)
                for g, chan in enumerate(groups):
                    rows = pl.ds(chan, PACK)
                    cross[s, rows, pl.ds(lane, LANES)] = values[2 * g]
                    cross[s, rows, pl.ds(bins + lane, LANES)] = values[2 * g + 1]

        return [
            lambda lane=lane, s=s: group(lane, s)
            for lane in range(0, bins, LANES)
            for s in range(0, sources, 4)
        ]

    slots = (even, odd)
    for index in range(2 * blocks + 1):
        beside = products(index - 1, slots[(index - 1) % 2]) if index > 0 else []
        work = spectra(index, slots[index % 2]) if index < 2 * blocks else []
        every = max(1, len(work) // 4)
        for at in range(max(len(work), len(beside) * every)):
            if at % every == 0 and at // every < len(beside):
                beside[at // every]()
            if at < len(work):
                work[at]()
    if rounded:
        out_ref[...] = total[...].astype(out_ref.dtype)


@partial(jax.jit, static_argnames="rounded")
def lags(place, own, other, receivers, table, acc=None, rounded=False):
    blocks, windows, _, _, bins = own.shape
    channels = receivers.shape[2]
    sources = PACK
    vmem = pl.BlockSpec(memory_space=pltpu.VMEM)
    resumed = acc is not None
    shape = (sources * channels, LAG)
    slot = pltpu.VMEM((sources, channels, 2 * bins), jnp.bfloat16)
    return pl.pallas_call(
        partial(lags_kernel, resumed=resumed, rounded=rounded),
        in_specs=[pl.BlockSpec(memory_space=pltpu.SMEM)] + [vmem] * (5 if resumed else 4),
        out_specs=vmem,
        scratch_shapes=[
            pltpu.VMEM((2 * blocks, 2 * windows, sources, bins), jnp.float32),
            slot,
            slot,
        ]
        + ([pltpu.VMEM(shape, jnp.float32)] if rounded else []),
        out_shape=jax.ShapeDtypeStruct(shape, jnp.bfloat16 if rounded else jnp.float32),
        compiler_params=pltpu.CompilerParams(vmem_limit_bytes=24 * 1024 * 1024),
        cost_estimate=pl.CostEstimate(
            flops=2 * sources * channels * 4 * blocks * bins * LAG * 4,
            bytes_accessed=8 * 1024 * 1024,
            transcendentals=0,
        ),
    )(place, own, other, receivers, table, *([acc] if resumed else []))


def after(value, *others):
    return lax.optimization_barrier((value,) + others)[0]


def per_device(spectra, src_block, quality):
    windows, channels, _, num_bins = spectra.shape
    tm = lax.axis_size("tm")
    chan = lax.axis_size("chan")
    me = lax.axis_index("chan")
    my_tm = lax.axis_index("tm")
    bit = lambda value, place: (value >> place) & 1
    swap = lambda value, place: lax.ppermute(
        value, "chan", [(i, i ^ (1 << place)) for i in range(chan)]
    )

    def part_of(value, which):
        width = value.shape[3] // 2
        return lax.dynamic_slice_in_dim(value, which * width, width, 3)

    raw = spectra.transpose(0, 2, 1, 3)
    mine = part_of(raw, bit(me, 0))
    given = swap(part_of(raw, 1 - bit(me, 0)), 0)
    usable = quality.astype(jnp.float32)[None, :]
    wide = raw.astype(jnp.float32)
    power = jnp.mean(wide * wide, axis=(1, 3)) * usable
    scale = usable / jnp.sqrt(power + 1e-06)
    given_scale = swap(scale, 0)
    receivers = (wide * scale[:, None, :, None]).astype(jnp.bfloat16)
    table = lag_table(num_bins, LAG, windows * tm)

    def white(value, factor):
        return (value.astype(jnp.float32) * factor[:, None, :, None]).astype(jnp.bfloat16)

    def scatter(owner, first, second):
        here = bit(owner, 0) == bit(me, 0)
        factor = jnp.where(here, scale, given_scale)
        choose = lambda which: white(
            jnp.where(here, part_of(mine, which), part_of(given, which)), factor
        )
        if chan > 16:
            groups = [list(range(i, chan, 16)) for i in range(16)]
            have = white(jnp.where(here, mine, given), factor)
            have = jnp.where(owner // 2 == me // 2, have, 0)
            have = lax.psum(have, "chan", axis_index_groups=groups)
            choose = lambda which: part_of(have, which)
        side = bit(me, first)
        come = swap(choose(1 - side), first)
        have = jnp.where(bit(owner, first) == side, choose(side), come)
        side = bit(me, second)
        come = swap(part_of(have, 1 - side), second)
        have = jnp.where(bit(owner, second) == side, part_of(have, side), come)
        return jnp.where(bit(owner, 3) == bit(me, 3), have, swap(have, 3))[None]

    def gather(have, place):
        return jnp.concatenate([have, swap(have, place)], 0)

    order = lambda first, second: bit(me, 0) * 4 + bit(me, first) * 2 + bit(me, second)

    def lag(place, near, far, **more):
        return lags(jnp.stack(place), near, far, receivers, table, **more)

    partners = [(i, i ^ 1) for i in range(tm)]
    send, keep = 1 - my_tm, my_tm
    zero, two = jnp.int32(0), jnp.int32(2)

    begun0 = scatter(src_block[0], 1, 2)
    begun1 = scatter(src_block[1], 2, 1)
    order0, order1 = order(1, 2), order(2, 1)

    near0 = gather(begun0, 2)
    far0 = swap(near0, 1)
    near0s = swap(near0, 0)
    send0 = lag([order0, send, zero], near0, near0s)
    begun1 = after(begun1, send0)
    near1 = gather(begun1, 1)
    keep0 = lag([order0, keep, zero], near0, near0s)
    far0 = after(far0, keep0)
    far0s = swap(far0, 0)
    send0 = lag([order0, send, two], far0, far0s, acc=send0, rounded=True)
    come0 = lax.ppermute(send0, "tm", partners)
    far1 = swap(near1, 2)
    near1s = swap(after(near1, send0), 0)
    keep0 = lag([order0, keep, two], far0, far0s, acc=keep0)
    send1 = lag([order1, send, zero], near1, near1s)
    keep1 = lag([order1, keep, zero], near1, near1s)
    far1 = after(far1, keep0, send1, keep1)
    far1s = swap(far1, 0)
    send1 = lag([order1, send, two], far1, far1s, acc=send1, rounded=True)
    come1 = lax.ppermute(send1, "tm", partners)
    keep1 = lag([order1, keep, two], far1, far1s, acc=keep1)
    outs = [keep0 + come0.astype(jnp.float32), keep1 + come1.astype(jnp.float32)]
    return jnp.stack([out.reshape(-1, channels, LAG) for out in outs], 1)


def solution(mesh):
    return jax.shard_map(
        per_device,
        mesh=mesh,
        in_specs=(P("tm", "chan", None, None), P(), P("chan")),
        out_specs=P("tm", None, "chan", None),
        check_vma=False,
    )
```

```python
from functools import partial
import math

import jax
import jax.numpy as jnp
import numpy as np
from jax import lax
from jax.experimental import pallas as pl
from jax.experimental.pallas import tpu as pltpu
from jax.sharding import PartitionSpec as P

LAG = 512
STEPS = 2
LANES = 128
PACK = 16
BLOCKS = 8


def lag_table(num_bins, num_lags, windows):
    freq_bins = np.arange(num_bins, dtype=np.int64)[:, None]
    shifts = np.arange(num_lags, dtype=np.int64)[None, :] - num_lags // 2
    phases = np.mod(freq_bins * shifts, 2 * num_bins).astype(np.float32) * np.float32(
        math.pi / num_bins
    )
    scaling = np.float32(1.0 / math.sqrt(2.0 * num_bins * windows))
    table = np.concatenate([np.cos(phases) * scaling, -np.sin(phases) * scaling], 0)
    return jnp.asarray(table.astype(jnp.bfloat16))


def cross_kernel(place, near_ref, far_ref, rcv_ref, *refs, step, resumed):
    cross_ref, src = refs[1:] if resumed else refs
    blocks, _, windows, _, sources, bins = near_ref.shape
    channels = rcv_ref.shape[2]
    num_bins = rcv_ref.shape[3]
    order, first_block = place[0], place[1]
    groups = range(0, channels, PACK)
    chunks = bins // LANES

    def widen(w, carry):
        for start, ref in ((0, near_ref), (blocks, far_ref)):
            for entry in range(blocks):
                for part in range(2):
                    value = ref[entry, step, w, part].astype(jnp.float32)
                    for low in range(0, sources, 8):
                        src[start + entry, low // 8, 2 * w + part] = value[low : low + 8]
        return carry

    lax.fori_loop(0, windows, widen, 0)

    def body(at, carry):
        low = at % (sources // 8)
        chunk = at // (sources // 8)
        entry = chunk // chunks
        lane = (chunk % chunks) * LANES
        block = (first_block + entry % blocks + BLOCKS // 2 * (entry // blocks)) ^ order
        here = pl.multiple_of(block * bins + lane, LANES)
        lanes = pl.ds(pl.multiple_of(lane, LANES), LANES)
        received = [
            [
                [rcv_ref[w, part, pl.ds(chan, PACK), pl.ds(here, LANES)] for chan in groups]
                for part in range(2)
            ]
            for w in range(windows)
        ]
        for s in range(8):

            def summed(first, last):
                if last - first > 1:
                    middle = (first + last) // 2
                    left, right = summed(first, middle), summed(middle, last)
                    return [a + b for a, b in zip(left, right)]
                s_re, s_im = [
                    jnp.broadcast_to(
                        src[entry, low, 2 * first + part, pl.ds(s, 1), lanes], (PACK, LANES)
                    ).astype(jnp.bfloat16)
                    for part in range(2)
                ]
                values = []
                for c_re, c_im in zip(*received[first]):
                    values.append(s_re * c_re + s_im * c_im)
                    values.append(s_re * c_im - s_im * c_re)
                return values

            values = summed(0, windows)
            for g, chan in enumerate(groups):
                rows = pl.ds(chan, PACK)
                there = pl.multiple_of(num_bins + here, LANES)
                cross_ref[low * 8 + s, rows, pl.ds(here, LANES)] = values[2 * g]
                cross_ref[low * 8 + s, rows, pl.ds(there, LANES)] = values[2 * g + 1]
        return carry

    lax.fori_loop(0, 2 * blocks * chunks * (sources // 8), body, 0)


@partial(jax.jit, static_argnames="step")
def cross_spectra(place, near, far, receivers, begun=None, *, step):
    blocks, _, windows, _, sources, bins = near.shape
    channels, num_bins = receivers.shape[2:]
    vmem = pl.BlockSpec(memory_space=pltpu.VMEM)
    resumed = begun is not None
    return pl.pallas_call(
        partial(cross_kernel, step=step, resumed=resumed),
        in_specs=[pl.BlockSpec(memory_space=pltpu.SMEM)] + [vmem] * (4 if resumed else 3),
        out_specs=vmem,
        scratch_shapes=[
            pltpu.VMEM((2 * blocks, sources // 8, 2 * windows, 8, bins), jnp.float32)
        ],
        out_shape=jax.ShapeDtypeStruct((sources, channels, 2 * num_bins), jnp.bfloat16),
        input_output_aliases={4: 0} if resumed else {},
        compiler_params=pltpu.CompilerParams(vmem_limit_bytes=16 * 1024 * 1024),
        cost_estimate=pl.CostEstimate(
            flops=sources * channels * 2 * blocks * bins * windows * 400,
            bytes_accessed=8 * 1024 * 1024,
            transcendentals=0,
        ),
    )(place, near, far, receivers, *([begun] if resumed else []))


def after(value, *others):
    return lax.optimization_barrier((value,) + others)[0]


def per_device(spectra, src_block, quality):
    windows, channels, _, num_bins = spectra.shape
    tm = lax.axis_size("tm")
    chan = lax.axis_size("chan")
    me = lax.axis_index("chan")
    my_tm = lax.axis_index("tm")
    kept = channels // tm
    bit = lambda value, place: (value >> place) & 1
    swap = lambda value, place: lax.ppermute(
        value, "chan", [(i, i ^ (1 << place)) for i in range(chan)]
    )

    def part_of(value, which):
        width = value.shape[-1] // 2
        return lax.dynamic_slice_in_dim(value, which * width, width, value.ndim - 1)

    def rows_of(value, which):
        return lax.dynamic_slice_in_dim(value, which * kept, kept, value.ndim - 2)

    raw = lax.optimization_barrier(spectra.transpose(0, 2, 1, 3))
    mine = part_of(raw, bit(me, 0))
    given = swap(part_of(raw, 1 - bit(me, 0)), 0)
    usable = quality.astype(jnp.float32)[None, :]
    wide = raw.astype(jnp.float32)
    power = jnp.mean(wide * wide, axis=(1, 3)) * usable
    scale = usable / jnp.sqrt(power + 1e-06)
    given_scale = swap(scale, 0)
    receivers = (wide * scale[:, None, :, None]).astype(jnp.bfloat16)
    table = lag_table(num_bins, LAG, windows * tm)

    def scatter(part, first, second):
        def chosen(which, *others):
            own, sib = after(mine, *others), after(given, *others)
            out = []
            for step in range(STEPS):
                here = bit(src_block[step], 0) == bit(me, 0)
                factor = jnp.where(here, scale, given_scale)
                value = jnp.where(here, part_of(own, which), part_of(sib, which))
                value = value.astype(jnp.float32) * factor[:, None, :, None]
                value = rows_of(value.astype(jnp.bfloat16), part)
                if chan > 16:
                    groups = [list(range(i, chan, 16)) for i in range(16)]
                    value = jnp.where(src_block[step] // 2 // 8 == me // 16, value, 0)
                    value = lax.psum(value, "chan", axis_index_groups=groups)
                out.append(value)
            return jnp.stack(out)

        def select(place, own, come):
            here = [bit(src_block[step], place) == bit(me, place) for step in range(STEPS)]
            return jnp.stack([jnp.where(h, own[k], come[k]) for k, h in enumerate(here)])

        side = bit(me, first)
        come = swap(chosen(1 - side), first)
        have = select(first, chosen(side, come), come)
        side = bit(me, second)
        come = swap(part_of(have, 1 - side), second)
        have = select(second, part_of(have, side), come)
        return select(3, have, swap(have, 3))[None]

    def gather(have, place):
        return jnp.concatenate([have, swap(have, place)], 0)

    def order(first, second):
        return bit(me, 0) * 4 + bit(me, first) * 2 + bit(me, second)

    def lags(cross):
        return jnp.dot(
            cross.reshape(kept * channels, 2 * num_bins),
            table,
            preferred_element_type=jnp.float32,
        )

    steps = range(STEPS)
    send_order, keep_order = order(1, 2), order(2, 1)
    begins = lambda which: jnp.stack([which, jnp.int32(0)])
    resumes = lambda which: jnp.stack([which, jnp.int32(2)])

    send = scatter(1 - my_tm, 1, 2)
    keep = scatter(my_tm, 2, 1)
    send = gather(send, 2)
    more = swap(send, 1)
    send_sib = swap(send, 0)
    sent = [
        cross_spectra(begins(send_order), send, send_sib, receivers, step=step) for step in steps
    ]
    more = after(more, *sent)
    keep = gather(keep, 1)
    more_sib = swap(more, 0)
    partners = [(i, i ^ 1) for i in range(tm)]
    come = []
    for step in steps:
        cross = cross_spectra(
            resumes(send_order), more, more_sib, receivers, sent[step], step=step
        )
        come.append(lax.ppermute(lags(cross).astype(jnp.bfloat16), "tm", partners))
    more = swap(keep, 2)
    keep_sib = swap(keep, 0)
    held = [
        cross_spectra(begins(keep_order), keep, keep_sib, receivers, step=step) for step in steps
    ]
    more = after(more, *held)
    more_sib = swap(more, 0)
    outs = []
    for step in steps:
        cross = cross_spectra(
            resumes(keep_order), more, more_sib, receivers, held[step], step=step
        )
        total = lags(cross) + come[step].astype(jnp.float32)
        outs.append(total.reshape(kept, channels, LAG))
    return jnp.stack(outs, 1)


def solution(mesh):
    return jax.shard_map(
        per_device,
        mesh=mesh,
        in_specs=(P("tm", "chan", None, None), P(), P("chan")),
        out_specs=P("tm", None, "chan", None),
        check_vma=False,
    )
```

```python
from functools import partial
import math

import jax
import jax.numpy as jnp
import numpy as np
from jax import lax
from jax.experimental import pallas as pl
from jax.experimental.pallas import tpu as pltpu
from jax.sharding import PartitionSpec as P

LAG = 512
STEPS = 2
LANES = 128
PACK = 16
BLOCKS = 8


def lag_table(num_bins, num_lags, windows):
    freq_bins = np.arange(num_bins, dtype=np.int64)[:, None]
    shifts = np.arange(num_lags, dtype=np.int64)[None, :] - num_lags // 2
    phases = np.mod(freq_bins * shifts, 2 * num_bins).astype(np.float32) * np.float32(
        math.pi / num_bins
    )
    scaling = np.float32(1.0 / math.sqrt(2.0 * num_bins * windows))
    table = np.concatenate([np.cos(phases) * scaling, -np.sin(phases) * scaling], 0)
    return jnp.asarray(table.astype(jnp.bfloat16))


def cross_kernel(place, near_ref, far_ref, rcv_ref, *refs, step, resumed):
    cross_ref, src = refs[1:] if resumed else refs
    blocks, _, windows, _, sources, bins = near_ref.shape
    channels = rcv_ref.shape[2]
    num_bins = rcv_ref.shape[3]
    order, first_block = place[0], place[1]
    groups = range(0, channels, PACK)
    chunks = bins // LANES

    def widen(w, carry):
        for start, ref in ((0, near_ref), (blocks, far_ref)):
            for entry in range(blocks):
                for part in range(2):
                    value = ref[entry, step, w, part].astype(jnp.float32)
                    for low in range(0, sources, 8):
                        src[start + entry, low // 8, 2 * w + part] = value[low : low + 8]
        return carry

    lax.fori_loop(0, windows, widen, 0)

    def body(at, carry):
        low = at % (sources // 8)
        chunk = at // (sources // 8)
        entry = chunk // chunks
        lane = (chunk % chunks) * LANES
        block = (first_block + entry % blocks + BLOCKS // 2 * (entry // blocks)) ^ order
        here = pl.multiple_of(block * bins + lane, LANES)
        lanes = pl.ds(pl.multiple_of(lane, LANES), LANES)
        there = pl.multiple_of(num_bins + here, LANES)

        def summed(first, last, pair):
            if last - first > 1:
                middle = (first + last) // 2
                left, right = summed(first, middle, pair), summed(middle, last, pair)
                return [a + b for a, b in zip(left, right)]
            sent = [
                [
                    jnp.broadcast_to(
                        src[entry, low, 2 * first + part, pl.ds(s, 1), lanes], (PACK, LANES)
                    ).astype(jnp.bfloat16)
                    for part in range(2)
                ]
                for s in pair
            ]
            values = []
            for chan in groups:
                c_re, c_im = [
                    rcv_ref[first, part, pl.ds(chan, PACK), pl.ds(here, LANES)]
                    for part in range(2)
                ]
                for s_re, s_im in sent:
                    values.append(s_re * c_re + s_im * c_im)
                    values.append(s_re * c_im - s_im * c_re)
            return values

        for s in range(0, 8, 2):
            values = iter(summed(0, windows, (s, s + 1)))
            for chan in groups:
                for row in (s, s + 1):
                    for lane_of in (here, there):
                        cross_ref[low * 8 + row, pl.ds(chan, PACK), pl.ds(lane_of, LANES)] = next(
                            values
                        )
        return carry

    lax.fori_loop(0, 2 * blocks * chunks * (sources // 8), body, 0)


@partial(jax.jit, static_argnames="step")
def cross_spectra(place, near, far, receivers, begun=None, *, step):
    blocks, _, windows, _, sources, bins = near.shape
    channels, num_bins = receivers.shape[2:]
    vmem = pl.BlockSpec(memory_space=pltpu.VMEM)
    resumed = begun is not None
    return pl.pallas_call(
        partial(cross_kernel, step=step, resumed=resumed),
        in_specs=[pl.BlockSpec(memory_space=pltpu.SMEM)] + [vmem] * (4 if resumed else 3),
        out_specs=vmem,
        scratch_shapes=[
            pltpu.VMEM((2 * blocks, sources // 8, 2 * windows, 8, bins), jnp.float32)
        ],
        out_shape=jax.ShapeDtypeStruct((sources, channels, 2 * num_bins), jnp.bfloat16),
        input_output_aliases={4: 0} if resumed else {},
        compiler_params=pltpu.CompilerParams(vmem_limit_bytes=16 * 1024 * 1024),
        cost_estimate=pl.CostEstimate(
            flops=sources * channels * 2 * blocks * bins * windows * 8,
            bytes_accessed=sources * channels * 2 * blocks * bins,
            transcendentals=0,
        ),
    )(place, near, far, receivers, *([begun] if resumed else []))


def after(value, *others):
    return lax.optimization_barrier((value,) + others)[0]


def per_device(spectra, src_block, quality):
    windows, channels, _, num_bins = spectra.shape
    tm = lax.axis_size("tm")
    chan = lax.axis_size("chan")
    me = lax.axis_index("chan")
    my_tm = lax.axis_index("tm")
    kept = channels // tm
    bit = lambda value, place: (value >> place) & 1
    swap = lambda value, place: lax.ppermute(
        value, "chan", [(i, i ^ (1 << place)) for i in range(chan)]
    )

    def part_of(value, which):
        width = value.shape[-1] // 2
        return lax.dynamic_slice_in_dim(value, which * width, width, value.ndim - 1)

    def rows_of(value, which):
        return lax.dynamic_slice_in_dim(value, which * kept, kept, value.ndim - 2)

    raw = lax.optimization_barrier(spectra.transpose(0, 2, 1, 3))
    mine = part_of(raw, bit(me, 0))
    given = swap(part_of(raw, 1 - bit(me, 0)), 0)
    usable = quality.astype(jnp.float32)[None, :]
    wide = raw.astype(jnp.float32)
    power = jnp.mean(wide * wide, axis=(1, 3)) * usable
    scale = usable / jnp.sqrt(power + 1e-06)
    given_scale = swap(scale, 0)
    receivers = (wide * scale[:, None, :, None]).astype(jnp.bfloat16)
    table = lag_table(num_bins, LAG, windows * tm)

    def select(place, own, come):
        here = [bit(src_block[step], place) == bit(me, place) for step in range(STEPS)]
        return jnp.stack([jnp.where(h, own[k], come[k]) for k, h in enumerate(here)])

    def scatter(part):
        def chosen(which, *others):
            own, sib = after(mine, *others), after(given, *others)
            out = []
            for step in range(STEPS):
                here = bit(src_block[step], 0) == bit(me, 0)
                factor = jnp.where(here, scale, given_scale)
                value = jnp.where(here, part_of(own, which), part_of(sib, which))
                value = value.astype(jnp.float32) * factor[:, None, :, None]
                value = rows_of(value.astype(jnp.bfloat16), part)
                if chan > 16:
                    groups = [list(range(i, chan, 16)) for i in range(16)]
                    value = jnp.where(src_block[step] // 2 // 8 == me // 16, value, 0)
                    value = lax.psum(value, "chan", axis_index_groups=groups)
                out.append(value)
            return jnp.stack(out)

        def first_stage(place):
            return swap(chosen(1 - bit(me, place)), place)

        def first_choice(place, come):
            return select(place, chosen(bit(me, place), come), come)

        return first_stage, first_choice

    def second_stage(have, place):
        side = bit(me, place)
        come = swap(part_of(have, 1 - side), place)
        return select(place, part_of(have, side), come)

    def third_stage(have):
        return select(3, have, swap(have, 3))[None]

    def gather(have, place):
        return jnp.concatenate([have, swap(have, place)], 0)

    def order(first, second):
        return bit(me, 0) * 4 + bit(me, first) * 2 + bit(me, second)

    def lags(cross):
        return jnp.dot(
            cross.reshape(kept * channels, 2 * num_bins),
            table,
            preferred_element_type=jnp.float32,
        )

    steps = range(STEPS)
    send_order, keep_order = order(1, 2), order(2, 1)
    begins = lambda which: jnp.stack([which, jnp.int32(0)])
    resumes = lambda which: jnp.stack([which, jnp.int32(2)])

    send_stage, send_choice = scatter(1 - my_tm)
    keep_stage, keep_choice = scatter(my_tm)
    send_come, keep_come = send_stage(1), keep_stage(2)
    send = second_stage(send_choice(1, after(send_come, keep_come)), 2)
    keep = second_stage(keep_choice(2, keep_come), 1)
    send = third_stage(after(send, keep))
    keep = third_stage(after(keep, send))
    send = gather(send, 2)
    more = swap(send, 1)
    send_sib = swap(send, 0)
    sent = [
        cross_spectra(begins(send_order), send, send_sib, receivers, step=step) for step in steps
    ]
    keep = jnp.concatenate([keep, after(swap(keep, 1), *sent)], 0)
    more = after(more, keep)
    more_sib = swap(more, 0)
    more_keep = swap(keep, 2)
    partners = [(i, i ^ 1) for i in range(tm)]
    come = []
    for step in steps:
        cross = cross_spectra(
            resumes(send_order), more, more_sib, receivers, sent[step], step=step
        )
        sent[step] = lags(cross).astype(jnp.bfloat16)
        come.append(lax.ppermute(sent[step], "tm", partners))
    more_sib = swap(more_keep, 0)
    keep_sib = after(swap(keep, 0), more_sib, *sent)
    held = [
        cross_spectra(begins(keep_order), keep, keep_sib, receivers, step=step) for step in steps
    ]
    outs = []
    for step in steps:
        cross = cross_spectra(
            resumes(keep_order), more_keep, more_sib, receivers, held[step], step=step
        )
        outs.append(lags(after(cross, come[step])))
    outs = lax.optimization_barrier(outs)
    outs = [(out + got.astype(jnp.float32)).reshape(kept, channels, LAG) for out, got in zip(outs, come)]
    return jnp.stack(outs, 1)


def solution(mesh):
    return jax.shard_map(
        per_device,
        mesh=mesh,
        in_specs=(P("tm", "chan", None, None), P(), P("chan")),
        out_specs=P("tm", None, "chan", None),
        check_vma=False,
    )
```

```python
from functools import partial
import math

import jax
import jax.numpy as jnp
import numpy as np
from jax import lax
from jax.experimental import pallas as pl
from jax.experimental.pallas import tpu as pltpu
from jax.sharding import PartitionSpec as P

LAG = 512
STEPS = 2
LANES = 128
PACK = 16
BLOCKS = 8


def lag_table(num_bins, num_lags, windows):
    freq_bins = np.arange(num_bins, dtype=np.int64)[:, None]
    shifts = np.arange(num_lags, dtype=np.int64)[None, :] - num_lags // 2
    phases = np.mod(freq_bins * shifts, 2 * num_bins).astype(np.float32) * np.float32(
        math.pi / num_bins
    )
    scaling = np.float32(1.0 / math.sqrt(2.0 * num_bins * windows))
    table = np.concatenate([np.cos(phases) * scaling, -np.sin(phases) * scaling], 0)
    return jnp.asarray(table.astype(jnp.bfloat16))


def cross_kernel(place, near_ref, far_ref, rcv_ref, *refs, step, resumed):
    cross_ref, src = refs[1:] if resumed else refs
    blocks, _, windows, _, sources, bins = near_ref.shape
    channels = rcv_ref.shape[2]
    num_bins = rcv_ref.shape[3]
    order, first_block = place[0], place[1]
    chunks = bins // LANES

    def widen(w, carry):
        for start, ref in ((0, near_ref), (blocks, far_ref)):
            for entry in range(blocks):
                re, im = [ref[entry, step, w, part].astype(jnp.float32) for part in range(2)]
                for kind, value in enumerate((re, re - im, re + im)):
                    for low in range(0, sources, 8):
                        src[start + entry, low // 8, 3 * w + kind] = value[low : low + 8]
        return carry

    lax.fori_loop(0, windows, widen, 0)

    def body(at, carry):
        chan = pl.multiple_of((at % (channels // PACK)) * PACK, PACK)
        chunk = at // (channels // PACK)
        entry = chunk // chunks
        lane = (chunk % chunks) * LANES
        block = (first_block + entry % blocks + BLOCKS // 2 * (entry // blocks)) ^ order
        here = pl.multiple_of(block * bins + lane, LANES)
        there = pl.multiple_of(num_bins + here, LANES)
        lanes = pl.ds(pl.multiple_of(lane, LANES), LANES)
        rows = pl.ds(chan, PACK)
        received = []
        for w in range(windows):
            re, im = [
                rcv_ref[w, part, rows, pl.ds(here, LANES)].astype(jnp.float32) for part in range(2)
            ]
            received.append((re + im, im, re))
        for s in range(sources):
            sums = None
            for w in range(windows):
                shares = [
                    src[entry, s // 8, 3 * w + kind, pl.ds(s % 8, 1), lanes] * received[w][kind]
                    for kind in range(3)
                ]
                sums = shares if sums is None else [a + b for a, b in zip(sums, shares)]
            cross_ref[s, rows, pl.ds(here, LANES)] = (sums[0] - sums[1]).astype(jnp.bfloat16)
            cross_ref[s, rows, pl.ds(there, LANES)] = (sums[0] - sums[2]).astype(jnp.bfloat16)
        return carry

    lax.fori_loop(0, 2 * blocks * chunks * (channels // PACK), body, 0)


@partial(jax.jit, static_argnames="step")
def cross_spectra(place, near, far, receivers, begun=None, *, step):
    blocks, _, windows, _, sources, bins = near.shape
    channels, num_bins = receivers.shape[2:]
    vmem = pl.BlockSpec(memory_space=pltpu.VMEM)
    resumed = begun is not None
    return pl.pallas_call(
        partial(cross_kernel, step=step, resumed=resumed),
        in_specs=[pl.BlockSpec(memory_space=pltpu.SMEM)] + [vmem] * (4 if resumed else 3),
        out_specs=vmem,
        scratch_shapes=[
            pltpu.VMEM((2 * blocks, sources // 8, 3 * windows, 8, bins), jnp.float32)
        ],
        out_shape=jax.ShapeDtypeStruct((sources, channels, 2 * num_bins), jnp.bfloat16),
        input_output_aliases={4: 0} if resumed else {},
        compiler_params=pltpu.CompilerParams(vmem_limit_bytes=8 * 1024 * 1024),
        cost_estimate=pl.CostEstimate(
            flops=sources * channels * 2 * blocks * bins * windows * 8,
            bytes_accessed=sources * channels * 2 * blocks * bins,
            transcendentals=0,
        ),
    )(place, near, far, receivers, *([begun] if resumed else []))


def after(value, *others):
    return lax.optimization_barrier((value,) + others)[0]


def per_device(spectra, src_block, quality):
    windows, channels, _, num_bins = spectra.shape
    tm = lax.axis_size("tm")
    chan = lax.axis_size("chan")
    me = lax.axis_index("chan")
    my_tm = lax.axis_index("tm")
    kept = channels // tm
    bit = lambda value, place: (value >> place) & 1
    swap = lambda value, place: lax.ppermute(
        value, "chan", [(i, i ^ (1 << place)) for i in range(chan)]
    )

    def part_of(value, which):
        width = value.shape[-1] // 2
        return lax.dynamic_slice_in_dim(value, which * width, width, value.ndim - 1)

    def rows_of(value, which):
        return lax.dynamic_slice_in_dim(value, which * kept, kept, value.ndim - 2)

    raw = lax.optimization_barrier(spectra.transpose(0, 2, 1, 3))
    mine = part_of(raw, bit(me, 0))
    given = swap(part_of(raw, 1 - bit(me, 0)), 0)
    usable = quality.astype(jnp.float32)[None, :]
    wide = raw.astype(jnp.float32)
    power = jnp.mean(wide * wide, axis=(1, 3)) * usable
    scale = usable / jnp.sqrt(power + 1e-06)
    given_scale = swap(scale, 0)
    receivers = (wide * scale[:, None, :, None]).astype(jnp.bfloat16)
    table = lag_table(num_bins, LAG, windows * tm)

    def select(place, own, come):
        here = [bit(src_block[step], place) == bit(me, place) for step in range(STEPS)]
        return jnp.stack([jnp.where(h, own[k], come[k]) for k, h in enumerate(here)])

    def scatter(part):
        def chosen(which, *others):
            own, sib = after(mine, *others), after(given, *others)
            out = []
            for step in range(STEPS):
                here = bit(src_block[step], 0) == bit(me, 0)
                factor = jnp.where(here, scale, given_scale)
                value = jnp.where(here, part_of(own, which), part_of(sib, which))
                value = value.astype(jnp.float32) * factor[:, None, :, None]
                value = rows_of(value.astype(jnp.bfloat16), part)
                if chan > 16:
                    groups = [list(range(i, chan, 16)) for i in range(16)]
                    value = jnp.where(src_block[step] // 2 // 8 == me // 16, value, 0)
                    value = lax.psum(value, "chan", axis_index_groups=groups)
                out.append(value)
            return jnp.stack(out)

        def first_stage(place):
            return swap(chosen(1 - bit(me, place)), place)

        def first_choice(place, come):
            return select(place, chosen(bit(me, place), come), come)

        return first_stage, first_choice

    def second_stage(have, place):
        side = bit(me, place)
        come = swap(part_of(have, 1 - side), place)
        return select(place, part_of(have, side), come)

    def third_stage(have):
        return select(3, have, swap(have, 3))[None]

    def gather(have, place):
        return jnp.concatenate([have, swap(have, place)], 0)

    def order(first, second):
        return bit(me, 0) * 4 + bit(me, first) * 2 + bit(me, second)

    def lags(cross):
        return jnp.dot(
            cross.reshape(kept * channels, 2 * num_bins),
            table,
            preferred_element_type=jnp.float32,
        )

    steps = range(STEPS)
    send_order, keep_order = order(1, 2), order(2, 1)
    begins = lambda which: jnp.stack([which, jnp.int32(0)])
    resumes = lambda which: jnp.stack([which, jnp.int32(2)])

    send_stage, send_choice = scatter(1 - my_tm)
    keep_stage, keep_choice = scatter(my_tm)
    send_come, keep_come = send_stage(1), keep_stage(2)
    send = second_stage(send_choice(1, after(send_come, keep_come)), 2)
    keep = second_stage(keep_choice(2, keep_come), 1)
    send = third_stage(after(send, keep))
    keep = third_stage(after(keep, send))
    send = gather(send, 2)
    more = swap(send, 1)
    send_sib = swap(send, 0)
    sent = [
        cross_spectra(begins(send_order), send, send_sib, receivers, step=step) for step in steps
    ]
    keep = jnp.concatenate([keep, after(swap(keep, 1), *sent)], 0)
    more = after(more, keep)
    more_sib = swap(more, 0)
    more_keep = swap(keep, 2)
    partners = [(i, i ^ 1) for i in range(tm)]
    come = []
    for step in steps:
        cross = cross_spectra(
            resumes(send_order), more, more_sib, receivers, sent[step], step=step
        )
        sent[step] = lags(cross).astype(jnp.bfloat16)
        come.append(lax.ppermute(sent[step], "tm", partners))
    keep = jnp.concatenate([keep, after(more_keep, sent[0])], 0)
    keep_sib = after(swap(keep, 0), *sent)
    outs = []
    for step in steps:
        cross = cross_spectra(begins(keep_order), keep, keep_sib, receivers, step=step)
        outs.append(lags(after(cross, come[step])))
    outs = lax.optimization_barrier(outs)
    outs = [(out + got.astype(jnp.float32)).reshape(kept, channels, LAG) for out, got in zip(outs, come)]
    return jnp.stack(outs, 1)


def solution(mesh):
    return jax.shard_map(
        per_device,
        mesh=mesh,
        in_specs=(P("tm", "chan", None, None), P(), P("chan")),
        out_specs=P("tm", None, "chan", None),
        check_vma=False,
    )
```

```python
from functools import partial
import math

import jax
import jax.numpy as jnp
import numpy as np
from jax import lax
from jax.experimental import pallas as pl
from jax.experimental.pallas import tpu as pltpu
from jax.sharding import PartitionSpec as P

LAG = 512
STEPS = 2
LANES = 128
PACK = 16
BLOCKS = 8


def lag_table(num_bins, num_lags, windows):
    freq_bins = np.arange(num_bins, dtype=np.int64)[:, None]
    shifts = np.arange(num_lags, dtype=np.int64)[None, :] - num_lags // 2
    phases = np.mod(freq_bins * shifts, 2 * num_bins).astype(np.float32) * np.float32(
        math.pi / num_bins
    )
    scaling = np.float32(1.0 / math.sqrt(2.0 * num_bins * windows))
    table = np.concatenate([np.cos(phases) * scaling, -np.sin(phases) * scaling], 0)
    return jnp.asarray(table.astype(jnp.bfloat16))


def cross_kernel(place, near_ref, far_ref, rcv_ref, cross_ref, src, *, step):
    blocks, windows, _, sources, bins = near_ref.shape
    channels = rcv_ref.shape[2]
    num_bins = rcv_ref.shape[3]
    order = place[0]
    groups = range(0, channels, PACK)
    chunks = bins // LANES

    def widen(w, carry):
        for start, ref in ((0, near_ref), (blocks, far_ref.at[step])):
            for entry in range(blocks):
                for part in range(2):
                    value = ref[entry, w, part].astype(jnp.float32)
                    for low in range(0, sources, 8):
                        src[start + entry, low // 8, 2 * w + part] = value[low : low + 8]
        return carry

    lax.fori_loop(0, windows, widen, 0)

    def body(at, carry):
        low = at % (sources // 8)
        chunk = at // (sources // 8)
        entry = chunk // chunks
        lane = (chunk % chunks) * LANES
        here = pl.multiple_of((entry ^ order) * bins + lane, LANES)
        there = pl.multiple_of(num_bins + here, LANES)
        lanes = pl.ds(pl.multiple_of(lane, LANES), LANES)
        received = [
            [
                [rcv_ref[w, part, pl.ds(chan, PACK), pl.ds(here, LANES)] for chan in groups]
                for part in range(2)
            ]
            for w in range(windows)
        ]
        for s in range(8):

            def summed(first, last):
                if last - first > 1:
                    middle = (first + last) // 2
                    left, right = summed(first, middle), summed(middle, last)
                    return [a + b for a, b in zip(left, right)]
                s_re, s_im = [
                    jnp.broadcast_to(
                        src[entry, low, 2 * first + part, pl.ds(s, 1), lanes], (PACK, LANES)
                    ).astype(jnp.bfloat16)
                    for part in range(2)
                ]
                values = []
                for c_re, c_im in zip(*received[first]):
                    values.append(s_re * c_re + s_im * c_im)
                    values.append(s_re * c_im - s_im * c_re)
                return values

            values = summed(0, windows)
            for g, chan in enumerate(groups):
                rows = pl.ds(chan, PACK)
                cross_ref[low * 8 + s, rows, pl.ds(here, LANES)] = values[2 * g]
                cross_ref[low * 8 + s, rows, pl.ds(there, LANES)] = values[2 * g + 1]
        return carry

    lax.fori_loop(0, 2 * blocks * chunks * (sources // 8), body, 0)


@partial(jax.jit, static_argnames="step")
def cross_spectra(order, near, far, receivers, *, step):
    blocks, windows, _, sources, bins = near.shape
    channels, num_bins = receivers.shape[2:]
    vmem = pl.BlockSpec(memory_space=pltpu.VMEM)
    return pl.pallas_call(
        partial(cross_kernel, step=step),
        in_specs=[pl.BlockSpec(memory_space=pltpu.SMEM), vmem, vmem, vmem],
        out_specs=vmem,
        scratch_shapes=[
            pltpu.VMEM((2 * blocks, sources // 8, 2 * windows, 8, bins), jnp.float32)
        ],
        out_shape=jax.ShapeDtypeStruct((sources, channels, 2 * num_bins), jnp.bfloat16),
        compiler_params=pltpu.CompilerParams(vmem_limit_bytes=8 * 1024 * 1024),
        cost_estimate=pl.CostEstimate(
            flops=sources * channels * 2 * blocks * bins * windows * 8,
            bytes_accessed=sources * channels * 2 * blocks * bins,
            transcendentals=0,
        ),
    )(order[None], near, far, receivers)


def after(value, *others):
    return lax.optimization_barrier((value,) + others)[0]


def per_device(spectra, src_block, quality):
    windows, channels, _, num_bins = spectra.shape
    tm = lax.axis_size("tm")
    chan = lax.axis_size("chan")
    me = lax.axis_index("chan")
    my_tm = lax.axis_index("tm")
    kept = channels // tm
    bit = lambda value, place: (value >> place) & 1
    swap = lambda value, place: lax.ppermute(
        value, "chan", [(i, i ^ (1 << place)) for i in range(chan)]
    )

    def part_of(value, which):
        width = value.shape[-1] // 2
        return lax.dynamic_slice_in_dim(value, which * width, width, value.ndim - 1)

    def rows_of(value, which):
        return lax.dynamic_slice_in_dim(value, which * kept, kept, value.ndim - 2)

    raw = lax.optimization_barrier(spectra.transpose(0, 2, 1, 3))
    mine = part_of(raw, bit(me, 0))
    given = swap(part_of(raw, 1 - bit(me, 0)), 0)
    usable = quality.astype(jnp.float32)[None, :]
    wide = raw.astype(jnp.float32)
    power = jnp.mean(wide * wide, axis=(1, 3)) * usable
    scale = usable / jnp.sqrt(power + 1e-06)
    given_scale = swap(scale, 0)
    receivers = (wide * scale[:, None, :, None]).astype(jnp.bfloat16)
    table = lag_table(num_bins, LAG, windows * tm)

    def chosen(step, part, which):
        here = bit(src_block[step], 0) == bit(me, 0)
        factor = jnp.where(here, scale, given_scale)
        value = jnp.where(here, part_of(mine, which), part_of(given, which))
        value = value.astype(jnp.float32) * factor[:, None, :, None]
        value = rows_of(value.astype(jnp.bfloat16), part)
        if chan > 16:
            groups = [list(range(i, chan, 16)) for i in range(16)]
            value = jnp.where(src_block[step] // 16 == me // 16, value, 0)
            value = lax.psum(value, "chan", axis_index_groups=groups)
        return value

    steps = range(STEPS)
    places = [(1, 2) if step % 2 == 0 else (2, 1) for step in steps]

    def broadcast(part, ahead=None, work=None):
        tie = lambda value, phase: after(value, *ahead[phase]) if ahead else value
        seen = []
        have = []
        for step in steps:
            first = places[step][0]
            have.append(swap(tie(chosen(step, part, 1 - bit(me, first)), 0), first))
        seen.append(tuple(have))
        for step in steps:
            first = places[step][0]
            here = bit(src_block[step], first) == bit(me, first)
            have[step] = jnp.where(here, chosen(step, part, bit(me, first)), have[step])
        come = []
        for step in steps:
            second = places[step][1]
            come.append(swap(tie(part_of(have[step], 1 - bit(me, second)), 1), second))
        seen.append(tuple(come))
        for step in steps:
            second = places[step][1]
            here = bit(src_block[step], second) == bit(me, second)
            have[step] = jnp.where(here, part_of(have[step], bit(me, second)), come[step])
        come = swap(tie(jnp.stack(have), 2), 3)
        seen.append((come,))
        for step in steps:
            here = bit(src_block[step], 3) == bit(me, 3)
            have[step] = jnp.where(here, have[step], come[step])[None]
        for phase in (3, 4):
            come = [
                swap(tie(have[step], phase), places[step][4 - phase]) for step in steps
            ]
            seen.append(tuple(come))
            if work:
                come = [after(value, work[phase - 3]) for value in come]
            have = [jnp.concatenate(pair, 0) for pair in zip(have, come)]
        return have, swap(jnp.stack(have), 0), seen

    def lags(cross):
        return jnp.dot(
            cross.reshape(kept * channels, 2 * num_bins),
            table,
            preferred_element_type=jnp.float32,
        )

    orders = [
        bit(me, 0) * 4 + bit(me, first) * 2 + bit(me, second) for first, second in places
    ]
    partners = [(i, i ^ 1) for i in range(tm)]
    near, far, seen = broadcast(1 - my_tm)
    work = []
    sent = []
    for step in steps:
        first = after(near[step], *sent)
        work.append(cross_spectra(orders[step], first, far, receivers, step=step))
        sent.append(lags(work[step]).astype(jnp.bfloat16))
    kept_near, kept_far, _ = broadcast(my_tm, seen, work)
    come = [lax.ppermute(value, "tm", partners) for value in sent]
    outs = []
    for step in steps:
        first = after(kept_near[step], *sent)
        cross = cross_spectra(orders[step], first, kept_far, receivers, step=step)
        outs.append(lags(after(cross, come[step])))
    outs = lax.optimization_barrier(outs)
    outs = [
        (out + got.astype(jnp.float32)).reshape(kept, channels, LAG)
        for out, got in zip(outs, come)
    ]
    return jnp.stack(outs, 1)


def solution(mesh):
    return jax.shard_map(
        per_device,
        mesh=mesh,
        in_specs=(P("tm", "chan", None, None), P(), P("chan")),
        out_specs=P("tm", None, "chan", None),
        check_vma=False,
    )
```

```python
from functools import partial
import math

import jax
import jax.numpy as jnp
import numpy as np
from jax import lax
from jax.experimental import pallas as pl
from jax.experimental.pallas import tpu as pltpu
from jax.sharding import PartitionSpec as P

LAG = 512
STEPS = 2
LANES = 128
PACK = 16
BLOCKS = 8


def lag_table(num_bins, num_lags, windows):
    freq_bins = np.arange(num_bins, dtype=np.int64)[:, None]
    shifts = np.arange(num_lags, dtype=np.int64)[None, :] - num_lags // 2
    phases = np.mod(freq_bins * shifts, 2 * num_bins).astype(np.float32) * np.float32(
        math.pi / num_bins
    )
    scaling = np.float32(1.0 / math.sqrt(2.0 * num_bins * windows))
    table = np.concatenate([np.cos(phases) * scaling, -np.sin(phases) * scaling], 0)
    return jnp.asarray(table.astype(jnp.bfloat16))


def cross_kernel(place, near_ref, far_ref, rcv_ref, *refs, step):
    cross_ref, done_ref, src = refs[-3:]
    blocks, windows, _, sources, bins = near_ref.shape
    channels = rcv_ref.shape[2]
    num_bins = rcv_ref.shape[3]
    order, first_block = place[0], place[1]
    groups = range(0, channels, PACK)
    chunks = bins // LANES

    def widen(w, carry):
        for start, ref in ((0, near_ref), (blocks, far_ref.at[step])):
            for entry in range(blocks):
                for part in range(2):
                    value = ref[entry, w, part].astype(jnp.float32)
                    for low in range(0, sources, 8):
                        src[start + entry, low // 8, 2 * w + part] = value[low : low + 8]
        return carry

    lax.fori_loop(0, windows, widen, 0)

    def body(at, carry):
        low = at % (sources // 8)
        chunk = at // (sources // 8)
        entry = chunk // chunks
        lane = (chunk % chunks) * LANES
        block = (first_block + entry % blocks + BLOCKS // 2 * (entry // blocks)) ^ order
        here = pl.multiple_of(block * bins + lane, LANES)
        there = pl.multiple_of(num_bins + here, LANES)
        lanes = pl.ds(pl.multiple_of(lane, LANES), LANES)
        received = [
            [
                [rcv_ref[w, part, pl.ds(chan, PACK), pl.ds(here, LANES)] for chan in groups]
                for part in range(2)
            ]
            for w in range(windows)
        ]
        for s in range(8):

            def summed(first, last):
                if last - first > 1:
                    middle = (first + last) // 2
                    left, right = summed(first, middle), summed(middle, last)
                    return [a + b for a, b in zip(left, right)]
                s_re, s_im = [
                    jnp.broadcast_to(
                        src[entry, low, 2 * first + part, pl.ds(s, 1), lanes], (PACK, LANES)
                    ).astype(jnp.bfloat16)
                    for part in range(2)
                ]
                values = []
                for c_re, c_im in zip(*received[first]):
                    values.append(s_re * c_re + s_im * c_im)
                    values.append(s_re * c_im - s_im * c_re)
                return values

            values = summed(0, windows)
            for g, chan in enumerate(groups):
                rows = pl.ds(chan, PACK)
                cross_ref[low * 8 + s, rows, pl.ds(here, LANES)] = values[2 * g]
                cross_ref[low * 8 + s, rows, pl.ds(there, LANES)] = values[2 * g + 1]
        return carry

    lax.fori_loop(0, 2 * blocks * chunks * (sources // 8), body, 0)
    done_ref[...] = jnp.zeros_like(done_ref)


@partial(jax.jit, static_argnames="step")
def cross_spectra(place, near, far, receivers, begun=None, *, step):
    blocks, windows, _, sources, bins = near.shape
    channels, num_bins = receivers.shape[2:]
    vmem = pl.BlockSpec(memory_space=pltpu.VMEM)
    given = [place, near, far, receivers] + ([] if begun is None else [begun])
    return pl.pallas_call(
        partial(cross_kernel, step=step),
        in_specs=[pl.BlockSpec(memory_space=pltpu.SMEM)] + [vmem] * (len(given) - 1),
        out_specs=[vmem, vmem],
        scratch_shapes=[
            pltpu.VMEM((2 * blocks, sources // 8, 2 * windows, 8, bins), jnp.float32)
        ],
        out_shape=[
            jax.ShapeDtypeStruct((sources, channels, 2 * num_bins), jnp.bfloat16),
            jax.ShapeDtypeStruct((8, LANES), jnp.float32),
        ],
        input_output_aliases={} if begun is None else {4: 0},
        compiler_params=pltpu.CompilerParams(vmem_limit_bytes=8 * 1024 * 1024),
        cost_estimate=pl.CostEstimate(
            flops=sources * channels * 2 * blocks * bins * windows * 8,
            bytes_accessed=sources * channels * 2 * blocks * bins,
            transcendentals=0,
        ),
    )(*given)


def after(value, *others):
    return lax.optimization_barrier((value,) + others)[0]


def per_device(spectra, src_block, quality):
    windows, channels, _, num_bins = spectra.shape
    tm = lax.axis_size("tm")
    chan = lax.axis_size("chan")
    me = lax.axis_index("chan")
    my_tm = lax.axis_index("tm")
    kept = channels // tm
    bit = lambda value, place: (value >> place) & 1
    swap = lambda value, place: lax.ppermute(
        value, "chan", [(i, i ^ (1 << place)) for i in range(chan)]
    )

    def part_of(value, which):
        width = value.shape[-1] // 2
        return lax.dynamic_slice_in_dim(value, which * width, width, value.ndim - 1)

    def rows_of(value, which):
        return lax.dynamic_slice_in_dim(value, which * kept, kept, value.ndim - 2)

    raw = lax.optimization_barrier(spectra.transpose(0, 2, 1, 3))
    mine = part_of(raw, bit(me, 0))
    given = swap(part_of(raw, 1 - bit(me, 0)), 0)
    usable = quality.astype(jnp.float32)[None, :]
    wide = raw.astype(jnp.float32)
    power = jnp.mean(wide * wide, axis=(1, 3)) * usable
    scale = usable / jnp.sqrt(power + 1e-06)
    given_scale = swap(scale, 0)
    receivers = (wide * scale[:, None, :, None]).astype(jnp.bfloat16)
    table = lag_table(num_bins, LAG, windows * tm)

    def chosen(step, part, which):
        here = bit(src_block[step], 0) == bit(me, 0)
        factor = jnp.where(here, scale, given_scale)
        value = jnp.where(here, part_of(mine, which), part_of(given, which))
        value = value.astype(jnp.float32) * factor[:, None, :, None]
        value = rows_of(value.astype(jnp.bfloat16), part)
        if chan > 16:
            groups = [list(range(i, chan, 16)) for i in range(16)]
            value = jnp.where(src_block[step] // 16 == me // 16, value, 0)
            value = lax.psum(value, "chan", axis_index_groups=groups)
        return value

    steps = range(STEPS)
    places = [(1, 2) if step % 2 == 0 else (2, 1) for step in steps]

    def broadcast(part):
        behind = yield
        come = []
        for step in steps:
            first = places[step][0]
            value = chosen(step, part, 1 - bit(me, first))
            come.append(swap(after(value, *behind), first))
        behind = yield come
        have = []
        for step in steps:
            first = places[step][0]
            here = bit(src_block[step], first) == bit(me, first)
            have.append(jnp.where(here, chosen(step, part, bit(me, first)), come[step]))
        come = []
        for step in steps:
            second = places[step][1]
            value = part_of(have[step], 1 - bit(me, second))
            come.append(swap(after(value, *behind), second))
        behind = yield come
        for step in steps:
            second = places[step][1]
            here = bit(src_block[step], second) == bit(me, second)
            have[step] = jnp.where(here, part_of(have[step], bit(me, second)), come[step])
        come = swap(after(jnp.stack(have), *behind), 3)
        behind = yield [come]
        for step in steps:
            here = bit(src_block[step], 3) == bit(me, 3)
            have[step] = jnp.where(here, have[step], come[step])[None]
        come = [swap(after(have[step], *behind), places[step][1]) for step in steps]
        behind = yield come
        near = [jnp.concatenate([have[k], after(come[k], *behind)], 0) for k in steps]
        yield near, [swap(near[step], places[step][0]) for step in steps]

    def lags(cross):
        return jnp.dot(
            cross.reshape(kept * channels, 2 * num_bins),
            table,
            preferred_element_type=jnp.float32,
        )

    orders = [
        bit(me, 0) * 4 + bit(me, first) * 2 + bit(me, second) for first, second in places
    ]
    partners = [(i, i ^ 1) for i in range(tm)]

    def spectra(step, first_block, own, sib, *begun):
        place = jnp.stack([orders[step], jnp.int32(first_block)])
        return cross_spectra(place, own, sib, receivers, *begun, step=step)

    send, keep = broadcast(1 - my_tm), broadcast(my_tm)
    next(send), next(keep)
    send.send(())
    keep.send(send.send(()))
    keep.send(send.send(()))
    ahead = keep.send(send.send(()))
    near, more = send.send(())
    sib = swap(jnp.stack(near), 0)
    begun = [spectra(step, 0, near[step], sib) for step in steps]
    more = [after(value, *ahead, *(done for _, done in begun)) for value in more]
    keep.send(more)
    far = swap(jnp.stack(more), 0)
    sent = []
    come = []
    for step in steps:
        own = after(more[step], *sent)
        cross, _ = spectra(step, 2, own, far, begun[step][0])
        sent.append(lags(cross).astype(jnp.bfloat16))
        come.append(lax.ppermute(after(sent[step], *come), "tm", partners))
    near, more = keep.send(sent[:1])
    sib = swap(jnp.stack(near), 0)
    begun = [spectra(step, 0, after(near[step], *sent), sib) for step in steps]
    more = [after(value, begun[0][1], come[0]) for value in more]
    far = swap(jnp.stack(more), 0)
    more = [after(value, begun[-1][1]) for value in more]
    outs = []
    for step in steps:
        cross, _ = spectra(step, 2, more[step], far, begun[step][0])
        outs.append(lags(after(cross, *come) if outs else cross))
    outs = lax.optimization_barrier(outs)
    outs = [
        (out + got.astype(jnp.float32)).reshape(kept, channels, LAG)
        for out, got in zip(outs, come)
    ]
    return jnp.stack(outs, 1)


def solution(mesh):
    return jax.shard_map(
        per_device,
        mesh=mesh,
        in_specs=(P("tm", "chan", None, None), P(), P("chan")),
        out_specs=P("tm", None, "chan", None),
        check_vma=False,
    )
```

```python
from functools import partial
import math

import jax
import jax.numpy as jnp
import numpy as np
from jax import lax
from jax.experimental import pallas as pl
from jax.experimental.pallas import tpu as pltpu
from jax.sharding import PartitionSpec as P

LAG = 512
STEPS = 2
LANES = 128
PACK = 16
BLOCKS = 8


def lag_table(num_bins, num_lags, windows):
    freq_bins = np.arange(num_bins, dtype=np.int64)[:, None]
    shifts = np.arange(num_lags, dtype=np.int64)[None, :] - num_lags // 2
    phases = np.mod(freq_bins * shifts, 2 * num_bins).astype(np.float32) * np.float32(
        math.pi / num_bins
    )
    scaling = np.float32(1.0 / math.sqrt(2.0 * num_bins * windows))
    table = np.concatenate([np.cos(phases) * scaling, -np.sin(phases) * scaling], 0)
    return jnp.asarray(table.astype(jnp.bfloat16))


def cross_kernel(place, near_ref, far_ref, rcv_ref, cross_ref, done_ref, src, *, steps):
    blocks, _, windows, _, sources, bins = near_ref.shape
    channels = rcv_ref.shape[2]
    num_bins = rcv_ref.shape[3]
    order = place[0]
    groups = range(0, channels, PACK)
    chunks = bins // LANES

    def widen(w, carry):
        for start, ref in ((0, near_ref), (blocks, far_ref)):
            for at, step in enumerate(steps):
                for entry in range(blocks):
                    for part in range(2):
                        value = ref[entry, step, w, part].astype(jnp.float32)
                        for low in range(0, sources, 8):
                            group = (at * sources + low) // 8
                            src[start + entry, group, 2 * w + part] = value[low : low + 8]
        return carry

    lax.fori_loop(0, windows, widen, 0)

    def body(at, carry):
        low = at % src.shape[1]
        chunk = at // src.shape[1]
        entry = chunk // chunks
        lane = (chunk % chunks) * LANES
        here = pl.multiple_of((entry ^ order) * bins + lane, LANES)
        there = pl.multiple_of(num_bins + here, LANES)
        lanes = pl.ds(pl.multiple_of(lane, LANES), LANES)
        received = [
            [
                [rcv_ref[w, part, pl.ds(chan, PACK), pl.ds(here, LANES)] for chan in groups]
                for part in range(2)
            ]
            for w in range(windows)
        ]
        for s in range(8):

            def summed(first, last):
                if last - first > 1:
                    middle = (first + last) // 2
                    left, right = summed(first, middle), summed(middle, last)
                    return [a + b for a, b in zip(left, right)]
                s_re, s_im = [
                    jnp.broadcast_to(
                        src[entry, low, 2 * first + part, pl.ds(s, 1), lanes], (PACK, LANES)
                    ).astype(jnp.bfloat16)
                    for part in range(2)
                ]
                values = []
                for c_re, c_im in zip(*received[first]):
                    values.append(s_re * c_re + s_im * c_im)
                    values.append(s_re * c_im - s_im * c_re)
                return values

            values = summed(0, windows)
            for g, chan in enumerate(groups):
                rows = pl.ds(chan, PACK)
                cross_ref[low * 8 + s, rows, pl.ds(here, LANES)] = values[2 * g]
                cross_ref[low * 8 + s, rows, pl.ds(there, LANES)] = values[2 * g + 1]
        return carry

    lax.fori_loop(0, 2 * blocks * chunks * src.shape[1], body, 0)
    done_ref[...] = jnp.zeros_like(done_ref)


@partial(jax.jit, static_argnames="steps")
def cross_spectra(order, near, far, receivers, *, steps):
    blocks, _, windows, _, sources, bins = near.shape
    channels, num_bins = receivers.shape[2:]
    rows = len(steps) * sources
    vmem = pl.BlockSpec(memory_space=pltpu.VMEM)
    return pl.pallas_call(
        partial(cross_kernel, steps=steps),
        in_specs=[pl.BlockSpec(memory_space=pltpu.SMEM), vmem, vmem, vmem],
        out_specs=[vmem, vmem],
        scratch_shapes=[pltpu.VMEM((2 * blocks, rows // 8, 2 * windows, 8, bins), jnp.float32)],
        out_shape=[
            jax.ShapeDtypeStruct((rows, channels, 2 * num_bins), jnp.bfloat16),
            jax.ShapeDtypeStruct((8, LANES), jnp.float32),
        ],
        compiler_params=pltpu.CompilerParams(vmem_limit_bytes=8 * 1024 * 1024),
        cost_estimate=pl.CostEstimate(
            flops=rows * channels * 2 * blocks * bins * windows * 8,
            bytes_accessed=rows * channels * 2 * blocks * bins,
            transcendentals=0,
        ),
    )(order[None], near, far, receivers)


def after(value, *others):
    return lax.optimization_barrier((value,) + others)[0]


def per_device(spectra, src_block, quality):
    windows, channels, _, num_bins = spectra.shape
    tm = lax.axis_size("tm")
    chan = lax.axis_size("chan")
    me = lax.axis_index("chan")
    my_tm = lax.axis_index("tm")
    kept = channels // tm
    bit = lambda value, place: (value >> place) & 1
    core, side, level, far_side = 1, 2, 4, 8
    swap = lambda value, mask: lax.ppermute(value, "chan", [(i, i ^ mask) for i in range(chan)])

    raw = lax.optimization_barrier(spectra.transpose(0, 2, 1, 3))
    usable = quality.astype(jnp.float32)[None, :]
    wide = raw.astype(jnp.float32)
    power = jnp.mean(wide * wide, axis=(1, 3)) * usable
    scale = usable / jnp.sqrt(power + 1e-06)
    receivers = lax.optimization_barrier(
        (wide * scale[:, None, :, None]).astype(jnp.bfloat16)
    )
    half = num_bins // 2
    mine = lax.dynamic_slice_in_dim(receivers, bit(me, 0) * half, half, 3)
    given = swap(lax.dynamic_slice_in_dim(receivers, (1 - bit(me, 0)) * half, half, 3), core)
    table = lag_table(num_bins, LAG, windows * tm)

    steps = range(STEPS)
    bins = num_bins // BLOCKS
    order = bit(me, 0) * 4 + bit(me, 1) * 2 + bit(me, 2)
    moved = {0: 0, level: 1, side: 2, side + level: 3}

    def choose(cases, other):
        out = []
        for step in steps:
            value = other[step]
            for condition, case in cases:
                value = jnp.where(condition(src_block[step]), case[step], value)
            out.append(value)
        return jnp.stack(out)

    def piece(part, mask):
        at = ((order ^ moved[mask]) % 4) * bins

        def cut(value):
            sizes = (windows, 2, kept, bins)
            return lax.dynamic_slice(value, (0, 0, part * kept, at), sizes)

        out = choose([(lambda owner: bit(owner, 0) == bit(me, 0), [cut(mine)] * STEPS)], [cut(given)] * STEPS)
        if chan > 16:
            groups = [list(range(i, chan, 16)) for i in range(16)]
            own = jnp.stack([src_block[step] // 16 == me // 16 for step in steps])
            out = jnp.where(own[:, None, None, None, None], out, 0)
            out = lax.psum(out, "chan", axis_index_groups=groups)
        return out

    def broadcast(part):
        masks = (side + level, side, level)
        behind = yield
        pieces = [after(piece(part, mask), *behind) for mask in masks]
        come = [swap(value, mask) for value, mask in zip(pieces, masks)]
        behind = yield pieces, come
        come = [after(value, *behind) for value in come]
        have = choose(
            [
                (lambda owner, mask=mask: ((owner ^ me) & (side + level)) == mask, value)
                for mask, value in zip(masks, come)
            ],
            piece(part, 0),
        )
        come = swap(have, far_side)
        behind = yield [have], [come]
        come = after(come, *behind)
        have = choose([(lambda owner: bit(owner, 3) == bit(me, 3), have)], come)
        come = [swap(have, mask) for mask in masks]
        behind = yield [have], come
        come = [after(value, *behind) for value in come]
        near = jnp.stack([have, come[2], come[1], come[0]])
        yield near, swap(near, core)

    def lags(cross):
        return jnp.dot(
            cross.reshape(-1, 2 * num_bins), table, preferred_element_type=jnp.float32
        )

    spectra_of = partial(cross_spectra, order, receivers=receivers)
    partners = [(i, i ^ 1) for i in range(tm)]
    send, keep = broadcast(1 - my_tm), broadcast(my_tm)
    next(send), next(keep)
    send.send(())
    ready, _ = send.send(())
    _, ahead = keep.send(ready)
    ready, _ = send.send(ahead)
    _, ahead = keep.send(ready)
    near, far = send.send(ahead)
    sent = []
    come = []
    done = []
    for step in steps:
        cross, token = spectra_of(after(near, *sent), far, steps=(step,))
        done.append(token)
        sent.append(lags(cross).astype(jnp.bfloat16))
        come.append(lax.ppermute(after(sent[step], *come), "tm", partners))
    keep.send(done[:1])
    near, far = keep.send(done)
    cross, token = spectra_of(after(near, *sent), far, steps=tuple(steps))
    come = [after(value, token) for value in come]
    outs = lax.optimization_barrier(lags(after(cross, *come)))
    come = jnp.stack(come).astype(jnp.float32).reshape(outs.shape)
    outs = (outs + come).reshape(STEPS, kept, channels, LAG)
    return outs.transpose(1, 0, 2, 3)


def solution(mesh):
    return jax.shard_map(
        per_device,
        mesh=mesh,
        in_specs=(P("tm", "chan", None, None), P(), P("chan")),
        out_specs=P("tm", None, "chan", None),
        check_vma=False,
    )
```

```python
from functools import partial
import math

import jax
import jax.numpy as jnp
import numpy as np
from jax import lax
from jax.experimental import pallas as pl
from jax.experimental.pallas import tpu as pltpu
from jax.sharding import PartitionSpec as P

LAG = 512
STEPS = 2
LANES = 128
PACK = 16
BLOCKS = 8


def lag_table(num_bins, num_lags, windows):
    freq_bins = np.arange(num_bins, dtype=np.int64)[:, None]
    shifts = np.arange(num_lags, dtype=np.int64)[None, :] - num_lags // 2
    phases = np.mod(freq_bins * shifts, 2 * num_bins).astype(np.float32) * np.float32(
        math.pi / num_bins
    )
    scaling = np.float32(1.0 / math.sqrt(2.0 * num_bins * windows))
    table = np.concatenate([np.cos(phases) * scaling, -np.sin(phases) * scaling], 0)
    return jnp.asarray(table.astype(jnp.bfloat16))


def cross_kernel(place, near_ref, far_ref, rcv_ref, cross_ref, src, *, steps):
    _, blocks, windows, _, sources, bins = near_ref.shape
    channels = rcv_ref.shape[2]
    num_bins = rcv_ref.shape[3]
    groups = range(0, channels, PACK)
    chunks = bins // LANES

    def widen(w, carry):
        for start, ref in ((0, near_ref), (blocks, far_ref)):
            for at, step in enumerate(steps):
                for entry in range(blocks):
                    for part in range(2):
                        value = ref[step, entry, w, part].astype(jnp.float32)
                        for low in range(0, sources, 8):
                            group = (at * sources + low) // 8
                            src[start + entry, group, 2 * w + part] = value[low : low + 8]
        return carry

    lax.fori_loop(0, windows, widen, 0)

    def body(at, carry):
        low = at % src.shape[1]
        chunk = at // src.shape[1]
        entry = chunk // chunks
        lane = (chunk % chunks) * LANES
        order = place[steps[0] + low // (sources // 8)]
        here = pl.multiple_of((entry ^ order) * bins + lane, LANES)
        there = pl.multiple_of(num_bins + here, LANES)
        lanes = pl.ds(pl.multiple_of(lane, LANES), LANES)
        received = [
            [
                [rcv_ref[w, part, pl.ds(chan, PACK), pl.ds(here, LANES)] for chan in groups]
                for part in range(2)
            ]
            for w in range(windows)
        ]
        for s in range(8):

            def summed(first, last):
                if last - first > 1:
                    middle = (first + last) // 2
                    left, right = summed(first, middle), summed(middle, last)
                    return [a + b for a, b in zip(left, right)]
                s_re, s_im = [
                    jnp.broadcast_to(
                        src[entry, low, 2 * first + part, pl.ds(s, 1), lanes], (PACK, LANES)
                    ).astype(jnp.bfloat16)
                    for part in range(2)
                ]
                values = []
                for c_re, c_im in zip(*received[first]):
                    values.append(s_re * c_re + s_im * c_im)
                    values.append(s_re * c_im - s_im * c_re)
                return values

            values = summed(0, windows)
            for g, chan in enumerate(groups):
                rows = pl.ds(chan, PACK)
                cross_ref[low * 8 + s, rows, pl.ds(here, LANES)] = values[2 * g]
                cross_ref[low * 8 + s, rows, pl.ds(there, LANES)] = values[2 * g + 1]
        return carry

    lax.fori_loop(0, 2 * blocks * chunks * src.shape[1], body, 0)


@partial(jax.jit, static_argnames="steps")
def cross_spectra(orders, near, far, receivers, *, steps):
    _, blocks, windows, _, sources, bins = near.shape
    channels, num_bins = receivers.shape[2:]
    rows = len(steps) * sources
    vmem = pl.BlockSpec(memory_space=pltpu.VMEM)
    return pl.pallas_call(
        partial(cross_kernel, steps=steps),
        in_specs=[pl.BlockSpec(memory_space=pltpu.SMEM), vmem, vmem, vmem],
        out_specs=vmem,
        scratch_shapes=[pltpu.VMEM((2 * blocks, rows // 8, 2 * windows, 8, bins), jnp.float32)],
        out_shape=jax.ShapeDtypeStruct((rows, channels, 2 * num_bins), jnp.bfloat16),
        compiler_params=pltpu.CompilerParams(vmem_limit_bytes=8 * 1024 * 1024),
        cost_estimate=pl.CostEstimate(
            flops=rows * channels * 2 * blocks * bins * windows * 8,
            bytes_accessed=rows * channels * 2 * blocks * bins,
            transcendentals=0,
        ),
    )(orders, near, far, receivers)


def after(value, *others):
    return lax.optimization_barrier((value,) + others)[0]


def per_device(spectra, src_block, quality):
    windows, channels, _, num_bins = spectra.shape
    tm = lax.axis_size("tm")
    chan = lax.axis_size("chan")
    me = lax.axis_index("chan")
    my_tm = lax.axis_index("tm")
    kept = channels // tm
    bit = lambda value, place: (value >> place) & 1
    swap = lambda value, place: lax.ppermute(
        value, "chan", [(i, i ^ (1 << place)) for i in range(chan)]
    )

    def part_of(value, which):
        width = value.shape[-1] // 2
        return lax.dynamic_slice_in_dim(value, which * width, width, value.ndim - 1)

    def rows_of(value, which):
        return lax.dynamic_slice_in_dim(value, which * kept, kept, value.ndim - 2)

    raw = lax.optimization_barrier(spectra.transpose(0, 2, 1, 3))
    usable = lax.optimization_barrier(quality.astype(jnp.float32))[None, :]
    wide = raw.astype(jnp.float32)
    power = jnp.mean(wide * wide, axis=(1, 3)) * usable
    scale = usable / jnp.sqrt(power + 1e-06)
    receivers = lax.optimization_barrier(
        (wide * scale[:, None, :, None]).astype(jnp.bfloat16)
    )
    mine = part_of(receivers, bit(me, 0))
    given = swap(part_of(receivers, 1 - bit(me, 0)), 0)
    table = lag_table(num_bins, LAG, windows * tm)

    def chosen(step, part, which):
        here = bit(src_block[step], 0) == bit(me, 0)
        cut = lambda value: rows_of(part_of(value, which), part)
        value = jnp.where(here, cut(mine), cut(given))
        if chan > 16:
            groups = [list(range(i, chan, 16)) for i in range(16)]
            value = jnp.where(src_block[step] // 16 == me // 16, value, 0)
            value = lax.psum(value, "chan", axis_index_groups=groups)
        return value

    steps = range(STEPS)
    places = [(1, 2) if step % 2 == 0 else (2, 1) for step in steps]

    def broadcast(part):
        behind = yield
        come = []
        for step in steps:
            first = places[step][0]
            value = chosen(step, part, 1 - bit(me, first))
            come.append(swap(after(value, *behind), first))
        behind = yield come
        have = []
        for step in steps:
            first = places[step][0]
            here = bit(src_block[step], first) == bit(me, first)
            have.append(jnp.where(here, chosen(step, part, bit(me, first)), come[step]))
        come = []
        for step in steps:
            second = places[step][1]
            value = part_of(have[step], 1 - bit(me, second))
            come.append(swap(after(value, *behind), second))
        behind = yield come
        for step in steps:
            second = places[step][1]
            here = bit(src_block[step], second) == bit(me, second)
            have[step] = jnp.where(here, part_of(have[step], bit(me, second)), come[step])
        come = swap(after(jnp.stack(have), *behind), 3)
        behind = yield [come]
        come = after(come, *behind)
        for step in steps:
            here = bit(src_block[step], 3) == bit(me, 3)
            have[step] = jnp.where(here, have[step], come[step])[None]
        for phase in (1, 0):
            come = [swap(have[step], places[step][phase]) for step in steps]
            behind = yield come
            have = [jnp.concatenate([have[k], after(come[k], *behind)], 0) for k in steps]
        near = jnp.stack(have)
        yield near, swap(near, 0)

    def lags(cross):
        return jnp.dot(
            cross.reshape(-1, 2 * num_bins), table, preferred_element_type=jnp.float32
        )

    orders = jnp.stack(
        [bit(me, 0) * 4 + bit(me, first) * 2 + bit(me, second) for first, second in places]
    )
    spectra_of = partial(cross_spectra, orders, receivers=receivers)
    partners = [(i, i ^ 1) for i in range(tm)]
    send, keep = broadcast(1 - my_tm), broadcast(my_tm)
    next(send), next(keep)
    send.send(())
    keep.send(send.send(()))
    keep.send(send.send(()))
    keep.send(send.send(()))
    last = send.send(())
    near, far = send.send(())
    done = []
    sent = []
    come = []
    for step in steps:
        done.append(spectra_of(after(near, *sent, *last), far, steps=(step,)))
        sent.append(lags(done[step]).astype(jnp.bfloat16))
        come.append(lax.ppermute(sent[step], "tm", partners))
        if not step:
            last = keep.send((*last, *done))
            keep.send(())
    near, far = keep.send(done[1:])
    cross = spectra_of(after(near, *sent, come[0]), far, steps=tuple(steps))
    come = [after(value, cross) for value in come]
    outs = lax.optimization_barrier(lags(after(cross, *come)))
    come = jnp.stack(come).astype(jnp.float32).reshape(outs.shape)
    outs = (outs + come).reshape(STEPS, kept, channels, LAG)
    return outs.transpose(1, 0, 2, 3)


def solution(mesh):
    return jax.shard_map(
        per_device,
        mesh=mesh,
        in_specs=(P("tm", "chan", None, None), P(), P("chan")),
        out_specs=P("tm", None, "chan", None),
        check_vma=False,
    )
```

```python
from functools import partial
import math

import jax
import jax.numpy as jnp
import numpy as np
from jax import lax
from jax.experimental import pallas as pl
from jax.experimental.pallas import tpu as pltpu
from jax.sharding import PartitionSpec as P

LAG = 512
STEPS = 2
LANES = 128
PACK = 16
BLOCKS = 8


def lag_table(num_bins, num_lags, windows):
    freq_bins = np.arange(num_bins, dtype=np.int64)[:, None]
    shifts = np.arange(num_lags, dtype=np.int64)[None, :] - num_lags // 2
    phases = np.mod(freq_bins * shifts, 2 * num_bins).astype(np.float32) * np.float32(
        math.pi / num_bins
    )
    scaling = np.float32(1.0 / math.sqrt(2.0 * num_bins * windows))
    table = np.concatenate([np.cos(phases) * scaling, -np.sin(phases) * scaling], 0)
    return jnp.asarray(table.astype(jnp.bfloat16))


def cross_kernel(place, near_ref, far_ref, rcv_ref, cross_ref, src, *, steps):
    _, blocks, windows, _, sources, bins = near_ref.shape
    channels = rcv_ref.shape[2]
    num_bins = rcv_ref.shape[3]
    groups = range(0, channels, PACK)
    chunks = bins // LANES

    def widen(w, carry):
        for start, ref in ((0, near_ref), (blocks, far_ref)):
            for at, step in enumerate(steps):
                for entry in range(blocks):
                    for part in range(2):
                        value = ref[step, entry, w, part].astype(jnp.float32)
                        for low in range(0, sources, 8):
                            group = (at * sources + low) // 8
                            src[start + entry, group, 2 * w + part] = value[low : low + 8]
        return carry

    lax.fori_loop(0, windows, widen, 0)

    def one_step(at, carry):
        order = place[steps[0] + at]

        def body(chunk, inner):
            entry = chunk // chunks
            lane = (chunk % chunks) * LANES
            here = pl.multiple_of((entry ^ order) * bins + lane, LANES)
            there = pl.multiple_of(num_bins + here, LANES)
            lanes = pl.ds(pl.multiple_of(lane, LANES), LANES)
            received = [
                [
                    [rcv_ref[w, part, pl.ds(chan, PACK), pl.ds(here, LANES)] for chan in groups]
                    for part in range(2)
                ]
                for w in range(windows)
            ]
            for s in range(sources):
                group = at * (sources // 8) + s // 8

                def summed(first, last):
                    if last - first > 1:
                        middle = (first + last) // 2
                        left, right = summed(first, middle), summed(middle, last)
                        return [a + b for a, b in zip(left, right)]
                    s_re, s_im = [
                        jnp.broadcast_to(
                            src[entry, group, 2 * first + part, pl.ds(s % 8, 1), lanes],
                            (PACK, LANES),
                        ).astype(jnp.bfloat16)
                        for part in range(2)
                    ]
                    values = []
                    for c_re, c_im in zip(*received[first]):
                        values.append(s_re * c_re + s_im * c_im)
                        values.append(s_re * c_im - s_im * c_re)
                    return values

                values = summed(0, windows)
                row = at * sources + s
                for g, chan in enumerate(groups):
                    rows = pl.ds(chan, PACK)
                    cross_ref[row, rows, pl.ds(here, LANES)] = values[2 * g]
                    cross_ref[row, rows, pl.ds(there, LANES)] = values[2 * g + 1]
            return inner

        return lax.fori_loop(0, 2 * blocks * chunks, body, carry)

    lax.fori_loop(0, len(steps), one_step, 0)


@partial(jax.jit, static_argnames="steps")
def cross_spectra(orders, near, far, receivers, *, steps):
    _, blocks, windows, _, sources, bins = near.shape
    channels, num_bins = receivers.shape[2:]
    rows = len(steps) * sources
    vmem = pl.BlockSpec(memory_space=pltpu.VMEM)
    return pl.pallas_call(
        partial(cross_kernel, steps=steps),
        in_specs=[pl.BlockSpec(memory_space=pltpu.SMEM), vmem, vmem, vmem],
        out_specs=vmem,
        scratch_shapes=[pltpu.VMEM((2 * blocks, rows // 8, 2 * windows, 8, bins), jnp.float32)],
        out_shape=jax.ShapeDtypeStruct((rows, channels, 2 * num_bins), jnp.bfloat16),
        compiler_params=pltpu.CompilerParams(vmem_limit_bytes=8 * 1024 * 1024),
        cost_estimate=pl.CostEstimate(
            flops=rows * channels * 2 * blocks * bins * windows * 8,
            bytes_accessed=rows * channels * 2 * blocks * bins,
            transcendentals=0,
        ),
    )(orders, near, far, receivers)


def after(value, *others):
    return lax.optimization_barrier((value,) + others)[0]


def per_device(spectra, src_block, quality):
    windows, channels, _, num_bins = spectra.shape
    tm = lax.axis_size("tm")
    chan = lax.axis_size("chan")
    me = lax.axis_index("chan")
    my_tm = lax.axis_index("tm")
    kept = channels // tm
    bit = lambda value, place: (value >> place) & 1
    swap = lambda value, place: lax.ppermute(
        value, "chan", [(i, i ^ (1 << place)) for i in range(chan)]
    )

    def part_of(value, which):
        width = value.shape[-1] // 2
        return lax.dynamic_slice_in_dim(value, which * width, width, value.ndim - 1)

    def rows_of(value, which):
        return lax.dynamic_slice_in_dim(value, which * kept, kept, value.ndim - 2)

    raw = lax.optimization_barrier(spectra.transpose(0, 2, 1, 3))
    usable = lax.optimization_barrier(quality.astype(jnp.float32))[None, :]
    wide = raw.astype(jnp.float32)
    power = jnp.mean(wide * wide, axis=(1, 3)) * usable
    scale = usable / jnp.sqrt(power + 1e-06)
    receivers = lax.optimization_barrier(
        (wide * scale[:, None, :, None]).astype(jnp.bfloat16)
    )
    mine = part_of(receivers, bit(me, 0))
    given = swap(part_of(receivers, 1 - bit(me, 0)), 0)
    table = lag_table(num_bins, LAG, windows * tm)

    def chosen(step, part, which):
        here = bit(src_block[step], 0) == bit(me, 0)
        cut = lambda value: rows_of(part_of(value, which), part)
        value = jnp.where(here, cut(mine), cut(given))
        if chan > 16:
            groups = [list(range(i, chan, 16)) for i in range(16)]
            value = jnp.where(src_block[step] // 16 == me // 16, value, 0)
            value = lax.psum(value, "chan", axis_index_groups=groups)
        return value

    steps = range(STEPS)
    places = [(1, 2) if step % 2 == 0 else (2, 1) for step in steps]

    def broadcast(part):
        behind = yield
        come = []
        for step in steps:
            first = places[step][0]
            value = chosen(step, part, 1 - bit(me, first))
            come.append(swap(after(value, *behind), first))
        behind = yield come
        have = []
        for step in steps:
            first = places[step][0]
            here = bit(src_block[step], first) == bit(me, first)
            have.append(jnp.where(here, chosen(step, part, bit(me, first)), come[step]))
        come = []
        for step in steps:
            second = places[step][1]
            value = part_of(have[step], 1 - bit(me, second))
            come.append(swap(after(value, *behind), second))
        behind = yield come
        for step in steps:
            second = places[step][1]
            here = bit(src_block[step], second) == bit(me, second)
            have[step] = jnp.where(here, part_of(have[step], bit(me, second)), come[step])
        come = swap(after(jnp.stack(have), *behind), 3)
        behind = yield [come]
        come = after(come, *behind)
        for step in steps:
            here = bit(src_block[step], 3) == bit(me, 3)
            have[step] = jnp.where(here, have[step], come[step])[None]
        for phase in (1, 0):
            come = [swap(have[step], places[step][phase]) for step in steps]
            behind = yield come
            have = [jnp.concatenate([have[k], after(come[k], *behind)], 0) for k in steps]
        near = jnp.stack(have)
        yield near, swap(near, 0)

    def lags(cross):
        return jnp.dot(
            cross.reshape(-1, 2 * num_bins), table, preferred_element_type=jnp.float32
        )

    orders = jnp.stack(
        [bit(me, 0) * 4 + bit(me, first) * 2 + bit(me, second) for first, second in places]
    )
    spectra_of = partial(cross_spectra, orders, receivers=receivers)
    partners = [(i, i ^ 1) for i in range(tm)]
    send, keep = broadcast(1 - my_tm), broadcast(my_tm)
    next(send), next(keep)
    send.send(())
    kept_come = [keep.send(send.send(()))]
    kept_come.append(keep.send(send.send(())))
    keep.send(send.send(kept_come[0]))
    send.send(kept_come[1])
    near, far = send.send(())
    done = []
    sent = []
    come = []
    last = ()
    for step in steps:
        done.append(spectra_of(after(near, *sent, *last), far, steps=(step,)))
        sent.append(lags(done[step]).astype(jnp.bfloat16))
        come.append(lax.ppermute(sent[step], "tm", partners))
        if not step:
            last = keep.send(done)
            keep.send(sent)
    near, far = keep.send(done[1:])
    cross = spectra_of(after(near, *sent, come[0]), far, steps=tuple(steps))
    come = [after(value, cross) for value in come]
    outs = lax.optimization_barrier(lags(after(cross, *come)))
    come = jnp.stack(come).astype(jnp.float32).reshape(outs.shape)
    outs = (outs + come).reshape(STEPS, kept, channels, LAG)
    return outs.transpose(1, 0, 2, 3)


def solution(mesh):
    return jax.shard_map(
        per_device,
        mesh=mesh,
        in_specs=(P("tm", "chan", None, None), P(), P("chan")),
        out_specs=P("tm", None, "chan", None),
        check_vma=False,
    )
```

```python
from functools import partial
import math

import jax
import jax.numpy as jnp
import numpy as np
from jax import lax
from jax.experimental import pallas as pl
from jax.experimental.pallas import tpu as pltpu
from jax.sharding import PartitionSpec as P

LAG = 512
STEPS = 2
LANES = 128
PACK = 16
BLOCKS = 8


def lag_table(num_bins, num_lags, windows):
    freq_bins = np.arange(num_bins, dtype=np.int64)[:, None]
    shifts = np.arange(num_lags, dtype=np.int64)[None, :] - num_lags // 2
    phases = np.mod(freq_bins * shifts, 2 * num_bins).astype(np.float32) * np.float32(
        math.pi / num_bins
    )
    scaling = np.float32(1.0 / math.sqrt(2.0 * num_bins * windows))
    table = np.concatenate([np.cos(phases) * scaling, -np.sin(phases) * scaling], 0)
    return jnp.asarray(table.astype(jnp.bfloat16))


def cross_kernel(place, near_ref, far_ref, rcv_ref, cross_ref, src, *, steps):
    blocks, _, windows, _, sources, bins = near_ref.shape
    channels = rcv_ref.shape[2]
    num_bins = rcv_ref.shape[3]
    groups = range(0, channels, PACK)
    chunks = bins // LANES

    for start, ref in ((0, near_ref), (blocks, far_ref)):
        for at, step in enumerate(steps):

            def widen(index, carry, start=start, ref=ref, at=at, step=step):
                entry, w = index // windows, index % windows
                for part in range(2):
                    value = ref[entry, step, w, part].astype(jnp.float32)
                    for low in range(0, sources, 8):
                        group = (at * sources + low) // 8
                        src[start + entry, group, 2 * w + part] = value[low : low + 8]
                return carry

            lax.fori_loop(0, blocks * windows, widen, 0)

    def one_step(at, carry):
        order = place[0]

        def body(turn, inner):
            low = turn % (sources // 8)
            chunk = turn // (sources // 8)
            entry = chunk // chunks
            lane = (chunk % chunks) * LANES
            here = pl.multiple_of((entry ^ order) * bins + lane, LANES)
            there = pl.multiple_of(num_bins + here, LANES)
            lanes = pl.ds(pl.multiple_of(lane, LANES), LANES)
            received = [
                [
                    [rcv_ref[w, part, pl.ds(chan, PACK), pl.ds(here, LANES)] for chan in groups]
                    for part in range(2)
                ]
                for w in range(windows)
            ]
            group = at * (sources // 8) + low
            for s in range(8):

                def summed(first, last):
                    if last - first > 1:
                        middle = (first + last) // 2
                        left, right = summed(first, middle), summed(middle, last)
                        return [a + b for a, b in zip(left, right)]
                    s_re, s_im = [
                        jnp.broadcast_to(
                            src[entry, group, 2 * first + part, pl.ds(s, 1), lanes],
                            (PACK, LANES),
                        ).astype(jnp.bfloat16)
                        for part in range(2)
                    ]
                    values = []
                    for c_re, c_im in zip(*received[first]):
                        values.append(s_re * c_re + s_im * c_im)
                        values.append(s_re * c_im - s_im * c_re)
                    return values

                values = summed(0, windows)
                row = group * 8 + s
                for g, chan in enumerate(groups):
                    rows = pl.ds(chan, PACK)
                    cross_ref[row, rows, pl.ds(here, LANES)] = values[2 * g]
                    cross_ref[row, rows, pl.ds(there, LANES)] = values[2 * g + 1]
            return inner

        return lax.fori_loop(0, 2 * blocks * chunks * (sources // 8), body, carry)

    lax.fori_loop(0, len(steps), one_step, 0)


@partial(jax.jit, static_argnames="steps")
def cross_spectra(order, near, far, receivers, *, steps):
    blocks, _, windows, _, sources, bins = near.shape
    channels, num_bins = receivers.shape[2:]
    rows = len(steps) * sources
    vmem = pl.BlockSpec(memory_space=pltpu.VMEM)
    return pl.pallas_call(
        partial(cross_kernel, steps=steps),
        in_specs=[pl.BlockSpec(memory_space=pltpu.SMEM), vmem, vmem, vmem],
        out_specs=vmem,
        scratch_shapes=[pltpu.VMEM((2 * blocks, rows // 8, 2 * windows, 8, bins), jnp.float32)],
        out_shape=jax.ShapeDtypeStruct((rows, channels, 2 * num_bins), jnp.bfloat16),
        compiler_params=pltpu.CompilerParams(vmem_limit_bytes=8 * 1024 * 1024),
        cost_estimate=pl.CostEstimate(
            flops=rows * channels * 2 * blocks * bins * windows * 8,
            bytes_accessed=rows * channels * 2 * blocks * bins,
            transcendentals=0,
        ),
    )(order[None], near, far, receivers)


def after(value, *others):
    return lax.optimization_barrier((value,) + others)[0]


def per_device(spectra, src_block, quality):
    windows, channels, _, num_bins = spectra.shape
    tm = lax.axis_size("tm")
    chan = lax.axis_size("chan")
    me = lax.axis_index("chan")
    my_tm = lax.axis_index("tm")
    kept = channels // tm
    bit = lambda value, place: (value >> place) & 1
    swap = lambda value, place: lax.ppermute(
        value, "chan", [(i, i ^ (1 << place)) for i in range(chan)]
    )

    def part_of(value, which):
        width = value.shape[-1] // 2
        return lax.dynamic_slice_in_dim(value, which * width, width, value.ndim - 1)

    def rows_of(value, which):
        return lax.dynamic_slice_in_dim(value, which * kept, kept, value.ndim - 2)

    raw = lax.optimization_barrier(spectra.transpose(0, 2, 1, 3))
    usable = lax.optimization_barrier(quality.astype(jnp.float32))[None, :]
    wide = raw.astype(jnp.float32)
    power = jnp.mean(wide * wide, axis=(1, 3)) * usable
    scale = usable / jnp.sqrt(power + 1e-06)
    receivers = lax.optimization_barrier(
        (wide * scale[:, None, :, None]).astype(jnp.bfloat16)
    )
    mine = part_of(receivers, bit(me, 0))
    given = swap(part_of(receivers, 1 - bit(me, 0)), 0)
    table = lag_table(num_bins, LAG, windows * tm)

    steps = range(STEPS)

    def chosen(held, which, part, behind):
        cut = lambda value: rows_of(part_of(after(value, *behind), which), part)
        out = []
        for step in held:
            here = bit(src_block[step], 0) == bit(me, 0)
            value = jnp.where(here, cut(mine), cut(given))
            if chan > 16:
                groups = [list(range(i, chan, 16)) for i in range(16)]
                value = jnp.where(src_block[step] // 16 == me // 16, value, 0)
                value = lax.psum(value, "chan", axis_index_groups=groups)
            out.append(value)
        return jnp.stack(out)

    def select(held, place, own, come):
        here = [bit(src_block[step], place) == bit(me, place) for step in held]
        return jnp.stack([jnp.where(h, own[k], come[k]) for k, h in enumerate(here)])

    def broadcast(part, streams):
        behind = yield
        come = [
            swap(chosen(held, 1 - bit(me, first), part, behind), first)
            for held, (first, _) in streams
        ]
        behind = (*(yield come), *come)
        have = [
            select(held, first, chosen(held, bit(me, first), part, behind), after(got, *behind))
            for (held, (first, _)), got in zip(streams, come)
        ]
        come = [
            swap(part_of(value, 1 - bit(me, second)), second)
            for (_, (_, second)), value in zip(streams, have)
        ]
        behind = (*(yield come), *come)
        have = [
            select(held, second, part_of(value, bit(me, second)), after(got, *behind))
            for (held, (_, second)), value, got in zip(streams, have, come)
        ]
        have = jnp.concatenate(have, 0)
        come = swap(have, 3)
        behind = yield [come]
        have = select(steps, 3, have, after(come, *behind))
        cuts = np.cumsum([len(held) for held, _ in streams])[:-1]
        have = [value[None] for value in jnp.split(have, cuts, 0)]
        for phase in (1, 0):
            come = [swap(value, places[phase]) for value, (_, places) in zip(have, streams)]
            behind = (*(yield come), *come)
            have = [
                jnp.concatenate([value, after(got, *behind)], 0) for value, got in zip(have, come)
            ]
        yield have, [swap(value, 0) for value in have]

    def order(stream):
        first, second = stream[1]
        return bit(me, 0) * 4 + bit(me, first) * 2 + bit(me, second)

    def lags(cross):
        return jnp.dot(
            cross.reshape(-1, 2 * num_bins), table, preferred_element_type=jnp.float32
        )

    partners = [(i, i ^ 1) for i in range(tm)]
    sent_streams = [((0,), (1, 2)), ((1,), (2, 1))]
    kept_streams = [((0, 1), (1, 2))]
    send, keep = broadcast(1 - my_tm, sent_streams), broadcast(my_tm, kept_streams)
    next(send), next(keep)
    send.send(())
    first = keep.send(send.send(()))
    send.send(())
    send.send(())
    send.send(first)
    second = keep.send(())
    near, far = send.send(second)
    keep.send(())
    done = []
    sent = []
    come = []
    last = ()
    for step in steps:
        cross = cross_spectra(
            order(sent_streams[step]),
            after(near[step], *sent, *last),
            far[step],
            receivers,
            steps=(0,),
        )
        done.append(cross)
        sent.append(lags(cross).astype(jnp.bfloat16))
        come.append(lax.ppermute(sent[step], "tm", partners))
        if not step:
            last = keep.send(done)
            keep.send(sent)
    near, far = keep.send(done[1:])
    cross = cross_spectra(
        order(kept_streams[0]),
        after(near[0], *sent, come[0]),
        far[0],
        receivers,
        steps=tuple(steps),
    )
    come = [after(value, cross) for value in come]
    outs = lax.optimization_barrier(lags(after(cross, *come)))
    come = jnp.stack(come).astype(jnp.float32).reshape(outs.shape)
    outs = (outs + come).reshape(STEPS, kept, channels, LAG)
    return outs.transpose(1, 0, 2, 3)


def solution(mesh):
    return jax.shard_map(
        per_device,
        mesh=mesh,
        in_specs=(P("tm", "chan", None, None), P(), P("chan")),
        out_specs=P("tm", None, "chan", None),
        check_vma=False,
    )
```

```python
from functools import partial
import math

import jax
import jax.numpy as jnp
import numpy as np
from jax import lax
from jax.experimental import pallas as pl
from jax.experimental.pallas import tpu as pltpu
from jax.sharding import PartitionSpec as P

LAG = 512
STEPS = 2
LANES = 128
PACK = 16
BLOCKS = 8


def lag_table(num_bins, num_lags, windows):
    freq_bins = np.arange(num_bins, dtype=np.int64)[:, None]
    shifts = np.arange(num_lags, dtype=np.int64)[None, :] - num_lags // 2
    phases = np.mod(freq_bins * shifts, 2 * num_bins).astype(np.float32) * np.float32(
        math.pi / num_bins
    )
    scaling = np.float32(1.0 / math.sqrt(2.0 * num_bins * windows))
    table = np.concatenate([np.cos(phases) * scaling, -np.sin(phases) * scaling], 0)
    return jnp.asarray(table.astype(jnp.bfloat16))


def cross_kernel(place, near_ref, far_ref, rcv_ref, cross_ref, src, *, step):
    blocks, windows, _, sources, bins = near_ref.shape
    channels = rcv_ref.shape[2]
    num_bins = rcv_ref.shape[3]
    order = place[0]
    groups = range(0, channels, PACK)
    chunks = bins // LANES

    def widen(w, carry):
        for start, ref in ((0, near_ref), (blocks, far_ref.at[step])):
            for entry in range(blocks):
                for part in range(2):
                    value = ref[entry, w, part].astype(jnp.float32)
                    for low in range(0, sources, 8):
                        src[start + entry, low // 8, 2 * w + part] = value[low : low + 8]
        return carry

    lax.fori_loop(0, windows, widen, 0)

    def body(chunk, carry):
        entry = chunk // chunks
        lane = (chunk % chunks) * LANES
        here = pl.multiple_of((entry ^ order) * bins + lane, LANES)
        there = pl.multiple_of(num_bins + here, LANES)
        lanes = pl.ds(pl.multiple_of(lane, LANES), LANES)
        received = [
            [
                [rcv_ref[w, part, pl.ds(chan, PACK), pl.ds(here, LANES)] for chan in groups]
                for part in range(2)
            ]
            for w in range(windows)
        ]
        for s in range(sources):

            def summed(first, last):
                if last - first > 1:
                    middle = (first + last) // 2
                    left, right = summed(first, middle), summed(middle, last)
                    return [a + b for a, b in zip(left, right)]
                s_re, s_im = [
                    jnp.broadcast_to(
                        src[entry, s // 8, 2 * first + part, pl.ds(s % 8, 1), lanes], (PACK, LANES)
                    ).astype(jnp.bfloat16)
                    for part in range(2)
                ]
                values = []
                for c_re, c_im in zip(*received[first]):
                    values.append(s_re * c_re + s_im * c_im)
                    values.append(s_re * c_im - s_im * c_re)
                return values

            values = summed(0, windows)
            for g, chan in enumerate(groups):
                rows = pl.ds(chan, PACK)
                cross_ref[s, rows, pl.ds(here, LANES)] = values[2 * g]
                cross_ref[s, rows, pl.ds(there, LANES)] = values[2 * g + 1]
        return carry

    lax.fori_loop(0, 2 * blocks * chunks, body, 0)


@partial(jax.jit, static_argnames="step")
def cross_spectra(order, near, far, receivers, *, step):
    blocks, windows, _, sources, bins = near.shape
    channels, num_bins = receivers.shape[2:]
    vmem = pl.BlockSpec(memory_space=pltpu.VMEM)
    return pl.pallas_call(
        partial(cross_kernel, step=step),
        in_specs=[pl.BlockSpec(memory_space=pltpu.SMEM), vmem, vmem, vmem],
        out_specs=vmem,
        scratch_shapes=[
            pltpu.VMEM((2 * blocks, sources // 8, 2 * windows, 8, bins), jnp.float32)
        ],
        out_shape=jax.ShapeDtypeStruct((sources, channels, 2 * num_bins), jnp.bfloat16),
        compiler_params=pltpu.CompilerParams(vmem_limit_bytes=8 * 1024 * 1024),
        cost_estimate=pl.CostEstimate(
            flops=sources * channels * 2 * blocks * bins * windows * 8,
            bytes_accessed=sources * channels * 2 * blocks * bins,
            transcendentals=0,
        ),
    )(order[None], near, far, receivers)


def after(value, *others):
    return lax.optimization_barrier((value,) + others)[0]


def per_device(spectra, src_block, quality):
    windows, channels, _, num_bins = spectra.shape
    tm = lax.axis_size("tm")
    chan = lax.axis_size("chan")
    me = lax.axis_index("chan")
    my_tm = lax.axis_index("tm")
    kept = channels // tm
    bit = lambda value, place: (value >> place) & 1
    swap = lambda value, place: lax.ppermute(
        value, "chan", [(i, i ^ (1 << place)) for i in range(chan)]
    )

    def part_of(value, which):
        width = value.shape[-1] // 2
        return lax.dynamic_slice_in_dim(value, which * width, width, value.ndim - 1)

    def rows_of(value, which):
        return lax.dynamic_slice_in_dim(value, which * kept, kept, value.ndim - 2)

    raw = lax.optimization_barrier(spectra.transpose(0, 2, 1, 3))
    mine = part_of(raw, bit(me, 0))
    given = swap(part_of(raw, 1 - bit(me, 0)), 0)
    usable = quality.astype(jnp.float32)[None, :]
    wide = raw.astype(jnp.float32)
    power = jnp.mean(wide * wide, axis=(1, 3)) * usable
    scale = usable / jnp.sqrt(power + 1e-06)
    given_scale = swap(scale, 0)
    receivers = (wide * scale[:, None, :, None]).astype(jnp.bfloat16)
    table = lag_table(num_bins, LAG, windows * tm)

    def chosen(step, part, which):
        here = bit(src_block[step], 0) == bit(me, 0)
        factor = jnp.where(here, scale, given_scale)
        value = jnp.where(here, part_of(mine, which), part_of(given, which))
        value = value.astype(jnp.float32) * factor[:, None, :, None]
        value = rows_of(value.astype(jnp.bfloat16), part)
        if chan > 16:
            groups = [list(range(i, chan, 16)) for i in range(16)]
            value = jnp.where(src_block[step] // 16 == me // 16, value, 0)
            value = lax.psum(value, "chan", axis_index_groups=groups)
        return value

    steps = range(STEPS)
    places = [(1, 2) if step % 2 == 0 else (2, 1) for step in steps]

    def broadcast(part, ahead=None, work=None):
        tie = lambda value, phase: after(value, *ahead[phase]) if ahead else value
        seen = []
        have = []
        for step in steps:
            first = places[step][0]
            have.append(swap(tie(chosen(step, part, 1 - bit(me, first)), 0), first))
        seen.append(tuple(have))
        for step in steps:
            first = places[step][0]
            here = bit(src_block[step], first) == bit(me, first)
            have[step] = jnp.where(here, chosen(step, part, bit(me, first)), have[step])
        come = []
        for step in steps:
            second = places[step][1]
            come.append(swap(tie(part_of(have[step], 1 - bit(me, second)), 1), second))
        seen.append(tuple(come))
        for step in steps:
            second = places[step][1]
            here = bit(src_block[step], second) == bit(me, second)
            have[step] = jnp.where(here, part_of(have[step], bit(me, second)), come[step])
        come = swap(tie(jnp.stack(have), 2), 3)
        seen.append((come,))
        for step in steps:
            here = bit(src_block[step], 3) == bit(me, 3)
            have[step] = jnp.where(here, have[step], come[step])[None]
        for phase in (3, 4):
            come = [
                swap(tie(have[step], phase), places[step][4 - phase]) for step in steps
            ]
            seen.append(tuple(come))
            if work:
                come = [after(value, work[phase - 3]) for value in come]
            have = [jnp.concatenate(pair, 0) for pair in zip(have, come)]
        return have, swap(jnp.stack(have), 0), seen

    def lags(cross):
        return jnp.dot(
            cross.reshape(kept * channels, 2 * num_bins),
            table,
            preferred_element_type=jnp.float32,
        )

    orders = [
        bit(me, 0) * 4 + bit(me, first) * 2 + bit(me, second) for first, second in places
    ]
    partners = [(i, i ^ 1) for i in range(tm)]
    near, far, seen = broadcast(1 - my_tm)
    work = []
    sent = []
    for step in steps:
        first = after(near[step], *sent)
        work.append(cross_spectra(orders[step], first, far, receivers, step=step))
        sent.append(lags(work[step]).astype(jnp.bfloat16))
    kept_near, kept_far, _ = broadcast(my_tm, seen, work)
    come = [lax.ppermute(value, "tm", partners) for value in sent]
    cross = []
    for step in steps:
        first = after(kept_near[step], *sent, *cross, *come[:step])
        cross.append(cross_spectra(orders[step], first, kept_far, receivers, step=step))
    come = [after(value, cross[-1]) for value in come]
    outs = [lags(after(value, *come)) for value in cross]
    outs = lax.optimization_barrier(outs)
    outs = [
        (out + got.astype(jnp.float32)).reshape(kept, channels, LAG)
        for out, got in zip(outs, come)
    ]
    return jnp.stack(outs, 1)


def solution(mesh):
    return jax.shard_map(
        per_device,
        mesh=mesh,
        in_specs=(P("tm", "chan", None, None), P(), P("chan")),
        out_specs=P("tm", None, "chan", None),
        check_vma=False,
    )
```

```python
from functools import partial
import math

import jax
import jax.numpy as jnp
import numpy as np
from jax import lax
from jax.experimental import pallas as pl
from jax.experimental.pallas import tpu as pltpu
from jax.sharding import PartitionSpec as P

LAG = 512
STEPS = 2
LANES = 128
PACK = 16
BLOCKS = 8


def lag_table(num_bins, num_lags, windows):
    freq_bins = np.arange(num_bins, dtype=np.int64)[:, None]
    shifts = np.arange(num_lags, dtype=np.int64)[None, :] - num_lags // 2
    phases = np.mod(freq_bins * shifts, 2 * num_bins).astype(np.float32) * np.float32(
        math.pi / num_bins
    )
    scaling = np.float32(1.0 / math.sqrt(2.0 * num_bins * windows))
    table = np.concatenate([np.cos(phases) * scaling, -np.sin(phases) * scaling], 0)
    return jnp.asarray(table.astype(jnp.bfloat16))


def cross_kernel(place, near_ref, far_ref, rcv_ref, cross_ref, src):
    blocks, windows, _, sources, bins = near_ref.shape
    channels = rcv_ref.shape[2]
    num_bins = rcv_ref.shape[3]
    order = place[0]
    groups = range(0, channels, PACK)

    def widen(w, carry):
        for start, ref in ((0, near_ref), (blocks, far_ref)):
            for entry in range(blocks):
                for part in range(2):
                    value = ref[entry, w, part].astype(jnp.float32)
                    for low in range(0, sources, 8):
                        src[start + entry, low // 8, 2 * w + part] = value[low : low + 8]
        return carry

    lax.fori_loop(0, windows, widen, 0)

    def lane_group(entry, lane):
        here = pl.multiple_of((entry ^ order) * bins + lane, LANES)
        there = pl.multiple_of(num_bins + here, LANES)
        lanes = pl.ds(lane, LANES)
        received = [
            [
                [rcv_ref[w, part, pl.ds(chan, PACK), pl.ds(here, LANES)] for chan in groups]
                for part in range(2)
            ]
            for w in range(windows)
        ]
        for s in range(sources):

            def summed(first, last):
                if last - first > 1:
                    middle = (first + last) // 2
                    left, right = summed(first, middle), summed(middle, last)
                    return [a + b for a, b in zip(left, right)]
                s_re, s_im = [
                    jnp.broadcast_to(
                        src[entry, s // 8, 2 * first + part, pl.ds(s % 8, 1), lanes], (PACK, LANES)
                    ).astype(jnp.bfloat16)
                    for part in range(2)
                ]
                values = []
                for c_re, c_im in zip(*received[first]):
                    values.append(s_re * c_re + s_im * c_im)
                    values.append(s_re * c_im - s_im * c_re)
                return values

            values = summed(0, windows)
            for g, chan in enumerate(groups):
                rows = pl.ds(chan, PACK)
                cross_ref[s, rows, pl.ds(here, LANES)] = values[2 * g]
                cross_ref[s, rows, pl.ds(there, LANES)] = values[2 * g + 1]

    def body(entry, carry):
        for lane in range(0, bins, LANES):
            lane_group(entry, lane)
        return carry

    lax.fori_loop(0, 2 * blocks, body, 0)


@jax.jit
def cross_spectra(order, near, far, receivers):
    blocks, windows, _, sources, bins = near.shape
    channels, num_bins = receivers.shape[2:]
    vmem = pl.BlockSpec(memory_space=pltpu.VMEM)
    return pl.pallas_call(
        cross_kernel,
        in_specs=[pl.BlockSpec(memory_space=pltpu.SMEM), vmem, vmem, vmem],
        out_specs=vmem,
        scratch_shapes=[
            pltpu.VMEM((2 * blocks, sources // 8, 2 * windows, 8, bins), jnp.float32)
        ],
        out_shape=jax.ShapeDtypeStruct((sources, channels, 2 * num_bins), jnp.bfloat16),
        compiler_params=pltpu.CompilerParams(vmem_limit_bytes=8 * 1024 * 1024),
        cost_estimate=pl.CostEstimate(
            flops=sources * channels * 2 * blocks * bins * windows * 8,
            bytes_accessed=sources * channels * 2 * blocks * bins,
            transcendentals=0,
        ),
    )(order[None], near, far, receivers)


def after(value, *others):
    return lax.optimization_barrier((value,) + others)[0]


def per_device(spectra, src_block, quality):
    windows, channels, _, num_bins = spectra.shape
    tm = lax.axis_size("tm")
    chan = lax.axis_size("chan")
    me = lax.axis_index("chan")
    my_tm = lax.axis_index("tm")
    kept = channels // tm
    bit = lambda value, place: (value >> place) & 1
    swap = lambda value, place: lax.ppermute(
        value, "chan", [(i, i ^ (1 << place)) for i in range(chan)]
    )

    def part_of(value, which):
        width = value.shape[-1] // 2
        return lax.dynamic_slice_in_dim(value, which * width, width, value.ndim - 1)

    def rows_of(value, which):
        return lax.dynamic_slice_in_dim(value, which * kept, kept, value.ndim - 2)

    raw = lax.optimization_barrier(spectra.transpose(0, 2, 1, 3))
    mine = part_of(raw, bit(me, 0))
    given = swap(part_of(raw, 1 - bit(me, 0)), 0)
    usable = quality.astype(jnp.float32)[None, :]
    wide = raw.astype(jnp.float32)
    power = jnp.mean(wide * wide, axis=(1, 3)) * usable
    scale = usable / jnp.sqrt(power + 1e-06)
    given_scale = swap(scale, 0)
    receivers = (wide * scale[:, None, :, None]).astype(jnp.bfloat16)
    table = lag_table(num_bins, LAG, windows * tm)

    def chosen(step, part, which):
        here = bit(src_block[step], 0) == bit(me, 0)
        factor = jnp.where(here, scale, given_scale)
        value = jnp.where(here, part_of(mine, which), part_of(given, which))
        value = value.astype(jnp.float32) * factor[:, None, :, None]
        value = rows_of(value.astype(jnp.bfloat16), part)
        if chan > 16:
            groups = [list(range(i, chan, 16)) for i in range(16)]
            value = jnp.where(src_block[step] // 16 == me // 16, value, 0)
            value = lax.psum(value, "chan", axis_index_groups=groups)
        return value

    steps = range(STEPS)
    places = [(1, 2) if step % 2 == 0 else (2, 1) for step in steps]

    def broadcast(part, ahead=None, work=()):
        tie = lambda value, phase: after(value, *ahead[max(phase, 1)]) if ahead else value
        seen = []
        have = []
        for step in steps:
            first = places[step][0]
            have.append(swap(tie(chosen(step, part, 1 - bit(me, first)), 0), first))
        seen.append(tuple(have))
        for step in steps:
            first = places[step][0]
            here = bit(src_block[step], first) == bit(me, first)
            have[step] = jnp.where(here, chosen(step, part, bit(me, first)), have[step])
        come = []
        for step in steps:
            second = places[step][1]
            come.append(swap(tie(part_of(have[step], 1 - bit(me, second)), 1), second))
        seen.append(tuple(come))
        for step in steps:
            second = places[step][1]
            here = bit(src_block[step], second) == bit(me, second)
            have[step] = jnp.where(here, part_of(have[step], bit(me, second)), come[step])
        come = swap(tie(after(jnp.stack(have), receivers), 2), 3)
        seen.append((come,))
        come = after(come, *work[:1])
        for step in steps:
            here = bit(src_block[step], 3) == bit(me, 3)
            have[step] = jnp.where(here, have[step], come[step])[None]
        come = [swap(tie(have[step], 3), places[step][1]) for step in steps]
        seen.append(tuple(come))
        come = [after(value, *come, *work[1:]) for value in come]
        have = [jnp.concatenate(pair, 0) for pair in zip(have, come)]
        come = [swap(tie(have[step], 4), places[step][0]) for step in steps]
        seen.append(tuple(come))
        return have, come, seen

    def whole(have, come, *behind):
        near = jnp.concatenate([have, after(come, *behind)], 0)
        return near, swap(near, 0)

    def lags(cross):
        return jnp.dot(
            cross.reshape(kept * channels, 2 * num_bins),
            table,
            preferred_element_type=jnp.float32,
        )

    orders = [
        bit(me, 0) * 4 + bit(me, first) * 2 + bit(me, second) for first, second in places
    ]
    partners = [(i, i ^ 1) for i in range(tm)]
    have, more, seen = broadcast(1 - my_tm)
    work = []
    sent = []
    for step in steps:
        near, far = whole(have[step], more[step], *work)
        work.append(cross_spectra(orders[step], after(near, *sent), far, receivers))
        sent.append(lags(work[step]).astype(jnp.bfloat16))
    have, more, _ = broadcast(my_tm, seen, (work[0], sent[0]))
    come = [lax.ppermute(value, "tm", partners) for value in sent]
    cross = []
    for step in steps:
        near, far = whole(have[step], more[step], work[1])
        near = after(near, *sent, *cross, *come[:step])
        cross.append(cross_spectra(orders[step], near, far, receivers))
    come = [after(value, cross[-1]) for value in come]
    outs = [lags(after(value, *come)) for value in cross]
    outs = lax.optimization_barrier(outs)
    outs = [
        (out + got.astype(jnp.float32)).reshape(kept, channels, LAG)
        for out, got in zip(outs, come)
    ]
    return jnp.stack(outs, 1)


def solution(mesh):
    return jax.shard_map(
        per_device,
        mesh=mesh,
        in_specs=(P("tm", "chan", None, None), P(), P("chan")),
        out_specs=P("tm", None, "chan", None),
        check_vma=False,
    )
```

```python
from functools import partial
import math

import jax
import jax.numpy as jnp
import numpy as np
from jax import lax
from jax.experimental import pallas as pl
from jax.experimental.pallas import tpu as pltpu
from jax.sharding import PartitionSpec as P

LAG = 512
STEPS = 2
LANES = 128
PACK = 16
BLOCKS = 8


def lag_table(num_bins, num_lags, windows):
    freq_bins = np.arange(num_bins, dtype=np.int64)[:, None]
    shifts = np.arange(num_lags, dtype=np.int64)[None, :] - num_lags // 2
    phases = np.mod(freq_bins * shifts, 2 * num_bins).astype(np.float32) * np.float32(
        math.pi / num_bins
    )
    scaling = np.float32(1.0 / math.sqrt(2.0 * num_bins * windows))
    table = np.concatenate([np.cos(phases) * scaling, -np.sin(phases) * scaling], 0)
    return jnp.asarray(table.astype(jnp.bfloat16))


def cross_kernel(place, near_ref, far_ref, rcv_ref, cross_ref, src):
    blocks, windows, _, sources, bins = near_ref.shape
    channels = rcv_ref.shape[2]
    num_bins = rcv_ref.shape[3]
    order = place[0]
    groups = range(0, channels, PACK)

    def widen(w, carry):
        for start, ref in ((0, near_ref), (blocks, far_ref)):
            for entry in range(blocks):
                for part in range(2):
                    value = ref[entry, w, part].astype(jnp.float32)
                    for low in range(0, sources, 8):
                        src[start + entry, low // 8, 2 * w + part] = value[low : low + 8]
        return carry

    lax.fori_loop(0, windows, widen, 0)

    def lane_group(entry, lane):
        here = pl.multiple_of((entry ^ order) * bins + lane, LANES)
        there = pl.multiple_of(num_bins + here, LANES)
        lanes = pl.ds(lane, LANES)
        received = [
            [
                [rcv_ref[w, part, pl.ds(chan, PACK), pl.ds(here, LANES)] for chan in groups]
                for part in range(2)
            ]
            for w in range(windows)
        ]
        for s in range(sources):

            def summed(first, last):
                if last - first > 1:
                    middle = (first + last) // 2
                    left, right = summed(first, middle), summed(middle, last)
                    return [a + b for a, b in zip(left, right)]
                s_re, s_im = [
                    jnp.broadcast_to(
                        src[entry, s // 8, 2 * first + part, pl.ds(s % 8, 1), lanes], (PACK, LANES)
                    ).astype(jnp.bfloat16)
                    for part in range(2)
                ]
                values = []
                for c_re, c_im in zip(*received[first]):
                    values.append(s_re * c_re + s_im * c_im)
                    values.append(s_re * c_im - s_im * c_re)
                return values

            values = summed(0, windows)
            for g, chan in enumerate(groups):
                rows = pl.ds(chan, PACK)
                cross_ref[s, rows, pl.ds(here, LANES)] = values[2 * g]
                cross_ref[s, rows, pl.ds(there, LANES)] = values[2 * g + 1]

    def body(entry, carry):
        for lane in range(0, bins, LANES):
            lane_group(entry, lane)
        return carry

    lax.fori_loop(0, 2 * blocks, body, 0)


@jax.jit
def cross_spectra(order, near, far, receivers):
    blocks, windows, _, sources, bins = near.shape
    channels, num_bins = receivers.shape[2:]
    vmem = pl.BlockSpec(memory_space=pltpu.VMEM)
    return pl.pallas_call(
        cross_kernel,
        in_specs=[pl.BlockSpec(memory_space=pltpu.SMEM), vmem, vmem, vmem],
        out_specs=vmem,
        scratch_shapes=[
            pltpu.VMEM((2 * blocks, sources // 8, 2 * windows, 8, bins), jnp.float32)
        ],
        out_shape=jax.ShapeDtypeStruct((sources, channels, 2 * num_bins), jnp.bfloat16),
        compiler_params=pltpu.CompilerParams(vmem_limit_bytes=8 * 1024 * 1024),
        cost_estimate=pl.CostEstimate(
            flops=sources * channels * 2 * blocks * bins * windows * 8,
            bytes_accessed=sources * channels * 2 * blocks * bins,
            transcendentals=0,
        ),
    )(order[None], near, far, receivers)


def after(value, *others):
    return lax.optimization_barrier((value,) + others)[0]


def per_device(spectra, src_block, quality):
    windows, channels, _, num_bins = spectra.shape
    tm = lax.axis_size("tm")
    chan = lax.axis_size("chan")
    me = lax.axis_index("chan")
    my_tm = lax.axis_index("tm")
    kept = channels // tm
    bit = lambda value, place: (value >> place) & 1
    swap = lambda value, place: lax.ppermute(
        value, "chan", [(i, i ^ (1 << place)) for i in range(chan)]
    )

    def part_of(value, which):
        width = value.shape[-1] // 2
        return lax.dynamic_slice_in_dim(value, which * width, width, value.ndim - 1)

    def rows_of(value, which):
        return lax.dynamic_slice_in_dim(value, which * kept, kept, value.ndim - 2)

    raw = lax.optimization_barrier(spectra.transpose(0, 2, 1, 3))
    mine = part_of(raw, bit(me, 0))
    given = swap(part_of(raw, 1 - bit(me, 0)), 0)
    usable = quality.astype(jnp.float32)[None, :]
    wide = raw.astype(jnp.float32)
    power = jnp.mean(wide * wide, axis=(1, 3)) * usable
    scale = usable / jnp.sqrt(power + 1e-06)
    given_scale = swap(scale, 0)
    receivers = (wide * scale[:, None, :, None]).astype(jnp.bfloat16)
    table = lag_table(num_bins, LAG, windows * tm)

    def chosen(step, part, which):
        here = bit(src_block[step], 0) == bit(me, 0)
        factor = jnp.where(here, scale, given_scale)
        value = jnp.where(here, part_of(mine, which), part_of(given, which))
        value = value.astype(jnp.float32) * factor[:, None, :, None]
        value = rows_of(value.astype(jnp.bfloat16), part)
        if chan > 16:
            groups = [list(range(i, chan, 16)) for i in range(16)]
            value = jnp.where(src_block[step] // 16 == me // 16, value, 0)
            value = lax.psum(value, "chan", axis_index_groups=groups)
        return value

    steps = range(STEPS)
    places = [(1, 2) if step % 2 == 0 else (2, 1) for step in steps]

    def broadcast(part, ahead=None, work=()):
        tie = lambda value, phase: after(value, *ahead[max(phase, 1)]) if ahead else value
        seen = []
        have = []
        for step in steps:
            first = places[step][0]
            have.append(swap(tie(chosen(step, part, 1 - bit(me, first)), 0), first))
        seen.append(tuple(have))
        for step in steps:
            first = places[step][0]
            here = bit(src_block[step], first) == bit(me, first)
            have[step] = jnp.where(here, chosen(step, part, bit(me, first)), have[step])
        come = []
        for step in steps:
            second = places[step][1]
            come.append(swap(tie(part_of(have[step], 1 - bit(me, second)), 1), second))
        seen.append(tuple(come))
        for step in steps:
            second = places[step][1]
            here = bit(src_block[step], second) == bit(me, second)
            have[step] = jnp.where(here, part_of(have[step], bit(me, second)), come[step])
        come = swap(tie(jnp.stack(have), 2), 3)
        seen.append((come,))
        come = after(come, *work[:1])
        for step in steps:
            here = bit(src_block[step], 3) == bit(me, 3)
            have[step] = jnp.where(here, have[step], come[step])[None]
        come = [swap(tie(have[step], 3), places[step][1]) for step in steps]
        seen.append(tuple(come))
        come = [after(value, *come, *work[1:]) for value in come]
        have = [jnp.concatenate(pair, 0) for pair in zip(have, come)]
        come = [swap(tie(have[step], 4), places[step][0]) for step in steps]
        seen.append(tuple(come))
        return have, come, seen

    def whole(have, come, *behind):
        near = jnp.concatenate([have, after(come, *behind)], 0)
        return near, swap(near, 0)

    def lags(cross):
        return jnp.dot(
            cross.reshape(kept * channels, 2 * num_bins),
            table,
            preferred_element_type=jnp.float32,
        )

    orders = [
        bit(me, 0) * 4 + bit(me, first) * 2 + bit(me, second) for first, second in places
    ]
    partners = [(i, i ^ 1) for i in range(tm)]
    have, more, seen = broadcast(1 - my_tm)
    work = []
    sent = []
    for step in steps:
        near, far = whole(have[step], more[step], *work)
        work.append(cross_spectra(orders[step], after(near, *sent), far, receivers))
        sent.append(lags(work[step]).astype(jnp.bfloat16))
    have, more, _ = broadcast(my_tm, seen, (work[0], sent[0]))
    come = [lax.ppermute(value, "tm", partners) for value in sent]
    cross = []
    for step in steps:
        near, far = whole(have[step], more[step], work[1])
        near = after(near, *sent, *cross, *come[:step])
        cross.append(cross_spectra(orders[step], near, far, receivers))
    come = [after(value, cross[-1]) for value in come]
    outs = [lags(after(value, *come)) for value in cross]
    outs = lax.optimization_barrier(outs)
    outs = [
        (out + got.astype(jnp.float32)).reshape(kept, channels, LAG)
        for out, got in zip(outs, come)
    ]
    return jnp.stack(outs, 1)


def solution(mesh):
    return jax.shard_map(
        per_device,
        mesh=mesh,
        in_specs=(P("tm", "chan", None, None), P(), P("chan")),
        out_specs=P("tm", None, "chan", None),
        check_vma=False,
    )
```

```python
from functools import partial
import math

import jax
import jax.numpy as jnp
import numpy as np
from jax import lax
from jax.experimental import pallas as pl
from jax.experimental.pallas import tpu as pltpu
from jax.sharding import PartitionSpec as P

LAG = 512
STEPS = 2
LANES = 128
PACK = 16
BLOCKS = 8


def lag_table(num_bins, num_lags, windows):
    freq_bins = np.arange(num_bins, dtype=np.int64)[:, None]
    shifts = np.arange(num_lags, dtype=np.int64)[None, :] - num_lags // 2
    phases = np.mod(freq_bins * shifts, 2 * num_bins).astype(np.float32) * np.float32(
        math.pi / num_bins
    )
    scaling = np.float32(1.0 / math.sqrt(2.0 * num_bins * windows))
    table = np.concatenate([np.cos(phases) * scaling, -np.sin(phases) * scaling], 0)
    return jnp.asarray(table.astype(jnp.bfloat16))


def cross_kernel(place, *refs):
    *pieces, rcv_ref, cross_ref, src = refs
    blocks, windows, _, sources, bins = pieces[0].shape
    channels = rcv_ref.shape[2]
    num_bins = rcv_ref.shape[3]
    order = place[0]
    groups = range(0, channels, PACK)

    def widen(w, carry):
        for at, ref in enumerate(pieces):
            for entry in range(blocks):
                for part in range(2):
                    value = ref[entry, w, part].astype(jnp.float32)
                    for low in range(0, sources, 8):
                        src[at * blocks + entry, low // 8, 2 * w + part] = value[low : low + 8]
        return carry

    lax.fori_loop(0, windows, widen, 0)

    def lane_group(entry, lane):
        here = pl.multiple_of((entry ^ order) * bins + lane, LANES)
        there = pl.multiple_of(num_bins + here, LANES)
        lanes = pl.ds(lane, LANES)
        received = [
            [
                [rcv_ref[w, part, pl.ds(chan, PACK), pl.ds(here, LANES)] for chan in groups]
                for part in range(2)
            ]
            for w in range(windows)
        ]
        for s in range(sources):

            def summed(first, last):
                if last - first > 1:
                    middle = (first + last) // 2
                    left, right = summed(first, middle), summed(middle, last)
                    return [a + b for a, b in zip(left, right)]
                s_re, s_im = [
                    jnp.broadcast_to(
                        src[entry, s // 8, 2 * first + part, pl.ds(s % 8, 1), lanes], (PACK, LANES)
                    ).astype(jnp.bfloat16)
                    for part in range(2)
                ]
                values = []
                for c_re, c_im in zip(*received[first]):
                    values.append(s_re * c_re + s_im * c_im)
                    values.append(s_re * c_im - s_im * c_re)
                return values

            values = summed(0, windows)
            for g, chan in enumerate(groups):
                rows = pl.ds(chan, PACK)
                cross_ref[s, rows, pl.ds(here, LANES)] = values[2 * g]
                cross_ref[s, rows, pl.ds(there, LANES)] = values[2 * g + 1]

    def body(entry, carry):
        for lane in range(0, bins, LANES):
            lane_group(entry, lane)
        return carry

    lax.fori_loop(0, len(pieces) * blocks, body, 0)


@jax.jit
def cross_spectra(order, pieces, receivers):
    blocks, windows, _, sources, bins = pieces[0].shape
    channels, num_bins = receivers.shape[2:]
    vmem = pl.BlockSpec(memory_space=pltpu.VMEM)
    return pl.pallas_call(
        cross_kernel,
        in_specs=[pl.BlockSpec(memory_space=pltpu.SMEM)] + [vmem] * (len(pieces) + 1),
        out_specs=vmem,
        scratch_shapes=[
            pltpu.VMEM((len(pieces) * blocks, sources // 8, 2 * windows, 8, bins), jnp.float32)
        ],
        out_shape=jax.ShapeDtypeStruct((sources, channels, 2 * num_bins), jnp.bfloat16),
        compiler_params=pltpu.CompilerParams(vmem_limit_bytes=8 * 1024 * 1024),
        cost_estimate=pl.CostEstimate(
            flops=sources * channels * num_bins * windows * 8,
            bytes_accessed=sources * channels * num_bins,
            transcendentals=0,
        ),
    )(order[None], *pieces, receivers)


def after(value, *others):
    return lax.optimization_barrier((value,) + others)[0]


def per_device(spectra, src_block, quality):
    windows, channels, _, num_bins = spectra.shape
    tm = lax.axis_size("tm")
    chan = lax.axis_size("chan")
    me = lax.axis_index("chan")
    my_tm = lax.axis_index("tm")
    kept = channels // tm
    bit = lambda value, place: (value >> place) & 1
    swap = lambda value, place: lax.ppermute(
        value, "chan", [(i, i ^ (1 << place)) for i in range(chan)]
    )

    def part_of(value, which):
        width = value.shape[-1] // 2
        return lax.dynamic_slice_in_dim(value, which * width, width, value.ndim - 1)

    def rows_of(value, which):
        return lax.dynamic_slice_in_dim(value, which * kept, kept, value.ndim - 2)

    raw = lax.optimization_barrier(spectra.transpose(0, 2, 1, 3))
    mine = part_of(raw, bit(me, 0))
    given = swap(part_of(raw, 1 - bit(me, 0)), 0)
    usable = quality.astype(jnp.float32)[None, :]
    wide = raw.astype(jnp.float32)
    power = jnp.mean(wide * wide, axis=(1, 3)) * usable
    scale = usable / jnp.sqrt(power + 1e-06)
    given_scale = swap(scale, 0)
    receivers = (wide * scale[:, None, :, None]).astype(jnp.bfloat16)
    table = lag_table(num_bins, LAG, windows * tm)

    def chosen(step, part, which):
        here = bit(src_block[step], 0) == bit(me, 0)
        factor = jnp.where(here, scale, given_scale)
        value = jnp.where(here, part_of(mine, which), part_of(given, which))
        value = value.astype(jnp.float32) * factor[:, None, :, None]
        value = rows_of(value.astype(jnp.bfloat16), part)
        if chan > 16:
            groups = [list(range(i, chan, 16)) for i in range(16)]
            value = jnp.where(src_block[step] // 16 == me // 16, value, 0)
            value = lax.psum(value, "chan", axis_index_groups=groups)
        return value

    steps = range(STEPS)
    places = [(1, 2) if step % 2 == 0 else (2, 1) for step in steps]

    def broadcast(part, ahead=None):
        tie = lambda value, phase: after(value, *ahead[max(phase, 1)]) if ahead else value
        seen = []
        have = []
        for step in steps:
            first = places[step][0]
            have.append(tie(chosen(step, part, 1 - bit(me, first)), 0))
        have = [
            swap(value, places[step][0])
            for step, value in zip(steps, lax.optimization_barrier(tuple(have)))
        ]
        seen.append(tuple(have))
        for step in steps:
            first = places[step][0]
            here = bit(src_block[step], first) == bit(me, first)
            have[step] = jnp.where(here, chosen(step, part, bit(me, first)), have[step])
        come = []
        for step in steps:
            second = places[step][1]
            come.append(swap(tie(part_of(have[step], 1 - bit(me, second)), 1), second))
        seen.append(tuple(come))
        for step in steps:
            second = places[step][1]
            here = bit(src_block[step], second) == bit(me, second)
            have[step] = jnp.where(here, part_of(have[step], bit(me, second)), come[step])
        stacked = tie(jnp.stack(have), 2)
        come = swap(stacked, 3)
        seen.append((come,))
        work = yield stacked
        come = after(come, *work[0])
        for step in steps:
            here = bit(src_block[step], 3) == bit(me, 3)
            have[step] = jnp.where(here, have[step], come[step])[None]
        come = [swap(tie(have[step], 3), places[step][1]) for step in steps]
        seen.append(tuple(come))
        come = [after(value, *come, *work[1]) for value in come]
        have = [jnp.concatenate(pair, 0) for pair in zip(have, come)]
        come = [swap(tie(have[step], 4), places[step][0]) for step in steps]
        seen.append(tuple(come))
        yield have, come, seen

    def whole(have, come, behind, joined=False):
        come = after(come, *behind)
        pieces = [jnp.concatenate([have, come], 0)] if joined else [have, come]
        return pieces + [swap(piece, 0) for piece in pieces]

    def lags(cross):
        return jnp.dot(
            cross.reshape(kept * channels, 2 * num_bins),
            table,
            preferred_element_type=jnp.float32,
        )

    orders = [
        bit(me, 0) * 4 + bit(me, first) * 2 + bit(me, second) for first, second in places
    ]
    partners = [(i, i ^ 1) for i in range(tm)]
    send = broadcast(1 - my_tm)
    next(send)
    have, more, seen = send.send(((), ()))
    keep = broadcast(my_tm, seen)
    work = []
    sent = []
    operand = next(keep)
    behind = []
    for step in steps:
        first, *rest = whole(have[step], more[step], behind, not step)
        work.append(cross_spectra(orders[step], (after(first, *sent), *rest), receivers))
        sent.append(lags(work[step]).astype(jnp.bfloat16))
        behind = work[:1]
    have, more, _ = keep.send((work[:1], sent[:1]))
    come = [lax.ppermute(value, "tm", partners) for value in sent]
    cross = []
    for step in steps:
        first, *rest = whole(have[step], more[step], work[1:])
        first = after(first, *sent, *cross, *come[:step])
        cross.append(cross_spectra(orders[step], (first, *rest), receivers))
    come = [after(value, cross[-1]) for value in come]
    outs = [lags(after(value, *come)) for value in cross]
    outs = lax.optimization_barrier(outs)
    outs = [
        (out + got.astype(jnp.float32)).reshape(kept, channels, LAG)
        for out, got in zip(outs, come)
    ]
    return jnp.stack(outs, 1)


def solution(mesh):
    return jax.shard_map(
        per_device,
        mesh=mesh,
        in_specs=(P("tm", "chan", None, None), P(), P("chan")),
        out_specs=P("tm", None, "chan", None),
        check_vma=False,
    )
```

```python
from functools import partial
import math

import jax
import jax.numpy as jnp
import numpy as np
from jax import lax
from jax.experimental import pallas as pl
from jax.experimental.pallas import tpu as pltpu
from jax.sharding import PartitionSpec as P

LAG = 512
STEPS = 2
LANES = 128
PACK = 16
BLOCKS = 8


def lag_table(num_bins, num_lags, windows):
    freq_bins = np.arange(num_bins, dtype=np.int64)[:, None]
    shifts = np.arange(num_lags, dtype=np.int64)[None, :] - num_lags // 2
    phases = np.mod(freq_bins * shifts, 2 * num_bins).astype(np.float32) * np.float32(
        math.pi / num_bins
    )
    scaling = np.float32(1.0 / math.sqrt(2.0 * num_bins * windows))
    table = np.concatenate([np.cos(phases) * scaling, -np.sin(phases) * scaling], 0)
    return jnp.asarray(table.astype(jnp.bfloat16))


def cross_kernel(place, *refs):
    *pieces, rcv_ref, cross_ref, src = refs
    blocks, windows, _, sources, bins = pieces[0].shape
    channels = rcv_ref.shape[2]
    num_bins = rcv_ref.shape[3]
    order = place[0]
    groups = range(0, channels, PACK)

    def widen(w, carry):
        for at, ref in enumerate(pieces):
            for entry in range(blocks):
                for part in range(2):
                    value = ref[entry, w, part].astype(jnp.float32)
                    for low in range(0, sources, 8):
                        src[at * blocks + entry, low // 8, 2 * w + part] = value[low : low + 8]
        return carry

    lax.fori_loop(0, windows, widen, 0)

    def lane_group(entry, lane):
        here = pl.multiple_of((entry ^ order) * bins + lane, LANES)
        there = pl.multiple_of(num_bins + here, LANES)
        lanes = pl.ds(lane, LANES)
        received = [
            [
                [rcv_ref[w, part, pl.ds(chan, PACK), pl.ds(here, LANES)] for chan in groups]
                for part in range(2)
            ]
            for w in range(windows)
        ]
        for s in range(sources):

            def summed(first, last):
                if last - first > 1:
                    middle = (first + last) // 2
                    left, right = summed(first, middle), summed(middle, last)
                    return [a + b for a, b in zip(left, right)]
                s_re, s_im = [
                    jnp.broadcast_to(
                        src[entry, s // 8, 2 * first + part, pl.ds(s % 8, 1), lanes], (PACK, LANES)
                    ).astype(jnp.bfloat16)
                    for part in range(2)
                ]
                values = []
                for c_re, c_im in zip(*received[first]):
                    values.append(s_re * c_re + s_im * c_im)
                    values.append(s_re * c_im - s_im * c_re)
                return values

            values = summed(0, windows)
            for g, chan in enumerate(groups):
                rows = pl.ds(chan, PACK)
                cross_ref[s, rows, pl.ds(here, LANES)] = values[2 * g]
                cross_ref[s, rows, pl.ds(there, LANES)] = values[2 * g + 1]

    def body(entry, carry):
        for lane in range(0, bins, LANES):
            lane_group(entry, lane)
        return carry

    lax.fori_loop(0, len(pieces) * blocks, body, 0)


@jax.jit
def cross_spectra(order, pieces, receivers):
    blocks, windows, _, sources, bins = pieces[0].shape
    channels, num_bins = receivers.shape[2:]
    vmem = pl.BlockSpec(memory_space=pltpu.VMEM)
    return pl.pallas_call(
        cross_kernel,
        in_specs=[pl.BlockSpec(memory_space=pltpu.SMEM)] + [vmem] * (len(pieces) + 1),
        out_specs=vmem,
        scratch_shapes=[
            pltpu.VMEM((len(pieces) * blocks, sources // 8, 2 * windows, 8, bins), jnp.float32)
        ],
        out_shape=jax.ShapeDtypeStruct((sources, channels, 2 * num_bins), jnp.bfloat16),
        compiler_params=pltpu.CompilerParams(vmem_limit_bytes=8 * 1024 * 1024),
        cost_estimate=pl.CostEstimate(
            flops=sources * channels * num_bins * windows * 8,
            bytes_accessed=sources * channels * num_bins,
            transcendentals=0,
        ),
    )(order[None], *pieces, receivers)


def after(value, *others):
    return lax.optimization_barrier((value,) + others)[0]


def per_device(spectra, src_block, quality):
    windows, channels, _, num_bins = spectra.shape
    tm = lax.axis_size("tm")
    chan = lax.axis_size("chan")
    me = lax.axis_index("chan")
    my_tm = lax.axis_index("tm")
    kept = channels // tm
    bit = lambda value, place: (value >> place) & 1
    swap = lambda value, place: lax.ppermute(
        value, "chan", [(i, i ^ (1 << place)) for i in range(chan)]
    )

    def cut(value, axis, start, size):
        at = [0] * value.ndim
        at[axis] = start
        sizes = list(value.shape)
        sizes[axis] = size
        return lax.dynamic_slice(value, at, sizes, allow_negative_indices=False)

    raw = lax.optimization_barrier(spectra.transpose(0, 2, 1, 3))
    half = num_bins // 2
    mine = cut(raw, 3, bit(me, 0) * half, half)
    given = swap(cut(raw, 3, (1 - bit(me, 0)) * half, half), 0)
    usable = quality.astype(jnp.float32)[None, :]
    wide = raw.astype(jnp.float32)
    power = jnp.mean(wide * wide, axis=(1, 3)) * usable
    scale = usable / jnp.sqrt(power + 1e-06)
    given_scale = swap(scale, 0)
    receivers = (wide * scale[:, None, :, None]).astype(jnp.bfloat16)
    table = lag_table(num_bins, LAG, windows * tm)

    steps = range(STEPS)
    same = [
        [bit(src_block[step], place) == bit(me, place) for place in range(4)] for step in steps
    ]
    starts = [
        [[(bit(me, place) ^ other) * (half >> deep) for deep in (1, 2)] for other in (0, 1)]
        for place in (1, 2)
    ]
    first_rows = [(1 - my_tm) * kept, my_tm * kept]
    given_scale, same, starts, first_rows = lax.optimization_barrier(
        (given_scale, same, starts, first_rows)
    )

    def part_of(value, place, other):
        size = value.shape[-1] // 2
        deep = 0 if size == half // 2 else 1
        return cut(value, value.ndim - 1, starts[place - 1][other][deep], size)

    def chosen(step, part, place, other):
        here = same[step][0]
        factor = jnp.where(here, scale, given_scale)
        value = jnp.where(here, part_of(mine, place, other), part_of(given, place, other))
        value = value.astype(jnp.float32) * factor[:, None, :, None]
        value = cut(value.astype(jnp.bfloat16), 2, first_rows[part], kept)
        if chan > 16:
            groups = [list(range(i, chan, 16)) for i in range(16)]
            value = jnp.where(src_block[step] // 16 == me // 16, value, 0)
            value = lax.psum(value, "chan", axis_index_groups=groups)
        return value

    places = [(1, 2) if step % 2 == 0 else (2, 1) for step in steps]

    def broadcast(part, ahead=None):
        tie = lambda value, phase: after(value, *ahead[max(phase, 1)]) if ahead else value
        seen = []
        have = []
        for step in steps:
            first = places[step][0]
            have.append(tie(chosen(step, part, first, 1), 0))
        have = [
            swap(value, places[step][0])
            for step, value in zip(steps, lax.optimization_barrier(tuple(have)))
        ]
        seen.append(tuple(have))
        for step in steps:
            first = places[step][0]
            have[step] = jnp.where(same[step][first], chosen(step, part, first, 0), have[step])
        come = []
        for step in steps:
            second = places[step][1]
            come.append(swap(tie(part_of(have[step], second, 1), 1), second))
        seen.append(tuple(come))
        for step in steps:
            second = places[step][1]
            own = part_of(have[step], second, 0)
            have[step] = jnp.where(same[step][second], own, come[step])
        stacked = tie(jnp.stack(have), 2)
        come = swap(stacked, 3)
        seen.append((come,))
        work = yield stacked
        come = after(come, *work[0])
        for step in steps:
            have[step] = jnp.where(same[step][3], have[step], come[step])[None]
        come = [swap(tie(have[step], 3), places[step][1]) for step in steps]
        seen.append(tuple(come))
        come = [after(value, *come, *work[1]) for value in come]
        have = [jnp.concatenate(pair, 0) for pair in zip(have, come)]
        come = [swap(tie(have[step], 4), places[step][0]) for step in steps]
        seen.append(tuple(come))
        yield have, come, seen

    def whole(have, come, behind, joined=False):
        come = after(come, *behind)
        pieces = [jnp.concatenate([have, come], 0)] if joined else [have, come]
        return pieces + [swap(piece, 0) for piece in pieces]

    def lags(cross):
        return jnp.dot(
            cross.reshape(kept * channels, 2 * num_bins),
            table,
            preferred_element_type=jnp.float32,
        )

    orders = [
        bit(me, 0) * 4 + bit(me, first) * 2 + bit(me, second) for first, second in places
    ]
    partners = [(i, i ^ 1) for i in range(tm)]
    send = broadcast(0)
    next(send)
    have, more, seen = send.send(((), ()))
    keep = broadcast(1, seen)
    work = []
    sent = []
    operand = next(keep)
    behind = []
    for step in steps:
        first, *rest = whole(have[step], more[step], behind, not step)
        work.append(cross_spectra(orders[step], (after(first, *sent), *rest), receivers))
        sent.append(lags(work[step]).astype(jnp.bfloat16))
        behind = work[:1]
    have, more, _ = keep.send((work[:1], sent[:1]))
    come = [lax.ppermute(value, "tm", partners) for value in sent]
    cross = []
    for step in steps:
        first, *rest = whole(have[step], more[step], work[1:])
        first = after(first, *sent, *cross, *come[:step])
        cross.append(cross_spectra(orders[step], (first, *rest), receivers))
    come = [after(value, cross[-1]) for value in come]
    outs = [lags(after(value, *come)) for value in cross]
    outs = lax.optimization_barrier(outs)
    outs = [
        (out + got.astype(jnp.float32)).reshape(kept, channels, LAG)
        for out, got in zip(outs, come)
    ]
    return jnp.stack(outs, 1)


def solution(mesh):
    return jax.shard_map(
        per_device,
        mesh=mesh,
        in_specs=(P("tm", "chan", None, None), P(), P("chan")),
        out_specs=P("tm", None, "chan", None),
        check_vma=False,
    )
```

```python
from functools import partial
import math

import jax
import jax.numpy as jnp
import numpy as np
from jax import lax
from jax.experimental import pallas as pl
from jax.experimental.pallas import tpu as pltpu
from jax.sharding import PartitionSpec as P

LAG = 512
STEPS = 2
LANES = 128
PACK = 16
BLOCKS = 8


def lag_table(num_bins, num_lags, windows):
    freq_bins = np.arange(num_bins, dtype=np.int64)[:, None]
    shifts = np.arange(num_lags, dtype=np.int64)[None, :] - num_lags // 2
    phases = np.mod(freq_bins * shifts, 2 * num_bins).astype(np.float32) * np.float32(
        math.pi / num_bins
    )
    scaling = np.float32(1.0 / math.sqrt(2.0 * num_bins * windows))
    table = np.concatenate([np.cos(phases) * scaling, -np.sin(phases) * scaling], 0)
    return jnp.asarray(table.astype(jnp.bfloat16))


def cross_kernel(place, *refs):
    *pieces, rcv_ref, cross_ref, src = refs
    blocks, windows, _, sources, bins = pieces[0].shape
    channels = rcv_ref.shape[2]
    num_bins = rcv_ref.shape[3]
    order = place[0]
    groups = range(0, channels, PACK)

    def widen(w, carry):
        for at, ref in enumerate(pieces):
            for entry in range(blocks):
                for part in range(2):
                    value = ref[entry, w, part].astype(jnp.float32)
                    for low in range(0, sources, 8):
                        src[at * blocks + entry, low // 8, 2 * w + part] = value[low : low + 8]
        return carry

    lax.fori_loop(0, windows, widen, 0)

    def lane_group(entry, lane):
        here = pl.multiple_of((entry ^ order) * bins + lane, LANES)
        there = pl.multiple_of(num_bins + here, LANES)
        lanes = pl.ds(lane, LANES)
        received = [
            [
                [rcv_ref[w, part, pl.ds(chan, PACK), pl.ds(here, LANES)] for chan in groups]
                for part in range(2)
            ]
            for w in range(windows)
        ]
        for s in range(sources):

            def summed(first, last):
                if last - first > 1:
                    middle = (first + last) // 2
                    left, right = summed(first, middle), summed(middle, last)
                    return [a + b for a, b in zip(left, right)]
                s_re, s_im = [
                    jnp.broadcast_to(
                        src[entry, s // 8, 2 * first + part, pl.ds(s % 8, 1), lanes], (PACK, LANES)
                    ).astype(jnp.bfloat16)
                    for part in range(2)
                ]
                values = []
                for c_re, c_im in zip(*received[first]):
                    values.append(s_re * c_re + s_im * c_im)
                    values.append(s_re * c_im - s_im * c_re)
                return values

            values = summed(0, windows)
            for g, chan in enumerate(groups):
                rows = pl.ds(chan, PACK)
                cross_ref[s, rows, pl.ds(here, LANES)] = values[2 * g]
                cross_ref[s, rows, pl.ds(there, LANES)] = values[2 * g + 1]

    def body(entry, carry):
        for lane in range(0, bins, LANES):
            lane_group(entry, lane)
        return carry

    lax.fori_loop(0, len(pieces) * blocks, body, 0)


@jax.jit
def cross_spectra(order, pieces, receivers):
    blocks, windows, _, sources, bins = pieces[0].shape
    channels, num_bins = receivers.shape[2:]
    vmem = pl.BlockSpec(memory_space=pltpu.VMEM)
    return pl.pallas_call(
        cross_kernel,
        in_specs=[pl.BlockSpec(memory_space=pltpu.SMEM)] + [vmem] * (len(pieces) + 1),
        out_specs=vmem,
        scratch_shapes=[
            pltpu.VMEM((len(pieces) * blocks, sources // 8, 2 * windows, 8, bins), jnp.float32)
        ],
        out_shape=jax.ShapeDtypeStruct((sources, channels, 2 * num_bins), jnp.bfloat16),
        compiler_params=pltpu.CompilerParams(vmem_limit_bytes=8 * 1024 * 1024),
        cost_estimate=pl.CostEstimate(
            flops=sources * channels * num_bins * windows * 8,
            bytes_accessed=sources * channels * num_bins,
            transcendentals=0,
        ),
    )(order[None], *pieces, receivers)


def after(value, *others):
    return lax.optimization_barrier((value,) + others)[0]


def per_device(spectra, src_block, quality):
    windows, channels, _, num_bins = spectra.shape
    tm = lax.axis_size("tm")
    chan = lax.axis_size("chan")
    me = lax.axis_index("chan")
    my_tm = lax.axis_index("tm")
    kept = channels // tm
    bit = lambda value, place: (value >> place) & 1
    swap = lambda value, place: lax.ppermute(
        value, "chan", [(i, i ^ (1 << place)) for i in range(chan)]
    )

    def cut(value, axis, start, size):
        at = [0] * value.ndim
        at[axis] = start
        sizes = list(value.shape)
        sizes[axis] = size
        return lax.dynamic_slice(value, at, sizes, allow_negative_indices=False)

    raw = lax.optimization_barrier(spectra.transpose(0, 2, 1, 3))
    half = num_bins // 2
    own_half = (me & 1) * half
    mine = cut(raw, 3, own_half, half)
    given = swap(cut(raw, 3, half - own_half, half), 0)
    usable = quality.astype(jnp.float32)[None, :]
    wide = raw.astype(jnp.float32)
    power = jnp.mean(wide * wide, axis=(1, 3)) * usable
    scale = usable / jnp.sqrt(power + 1e-06)
    given_scale = swap(scale, 0)
    receivers = (wide * scale[:, None, :, None]).astype(jnp.bfloat16)
    table = lag_table(num_bins, LAG, windows * tm)

    steps = range(STEPS)
    apart = [src_block[step] ^ me for step in steps]

    def starts_of(size):
        out = []
        for place in (1, 2):
            own = (me & (1 << place)) * (size >> place)
            out.append([own, size - own])
        return out

    def same_side(place):
        return [(apart[step] & (1 << place)) == 0 for step in steps]

    first_rows = [(1 - my_tm) * kept, my_tm * kept]
    given_scale, *early = lax.optimization_barrier(
        (given_scale, same_side(0), starts_of(half // 2), first_rows)
    )
    same, starts, first_rows = {0: early[0]}, {half // 2: early[1]}, early[2]

    def later_scalars(value):
        late = ([same_side(place) for place in (1, 2, 3)], starts_of(half // 4))
        value, (sides, starts[half // 4]) = lax.optimization_barrier((value, late))
        same.update(zip((1, 2, 3), sides))
        return value

    def part_of(value, place, other):
        size = value.shape[-1] // 2
        return cut(value, value.ndim - 1, starts[size][place - 1][other], size)

    def chosen(step, part, place, other):
        here = same[0][step]
        factor = jnp.where(here, scale, given_scale)
        value = jnp.where(here, part_of(mine, place, other), part_of(given, place, other))
        value = value.astype(jnp.float32) * factor[:, None, :, None]
        value = cut(value.astype(jnp.bfloat16), 2, first_rows[part], kept)
        if chan > 16:
            groups = [list(range(i, chan, 16)) for i in range(16)]
            value = jnp.where(src_block[step] // 16 == me // 16, value, 0)
            value = lax.psum(value, "chan", axis_index_groups=groups)
        return value

    places = [(1, 2) if step % 2 == 0 else (2, 1) for step in steps]

    def broadcast(part, ahead=None):
        tie = lambda value, phase: after(value, *ahead[max(phase, 1)]) if ahead else value
        seen = []
        have = []
        for step in steps:
            first = places[step][0]
            have.append(tie(chosen(step, part, first, 1), 0))
        have = [
            swap(value, places[step][0])
            for step, value in zip(steps, lax.optimization_barrier(tuple(have)))
        ]
        if not ahead:
            have = later_scalars(have)
        seen.append(tuple(have))
        for step in steps:
            first = places[step][0]
            have[step] = jnp.where(same[first][step], chosen(step, part, first, 0), have[step])
        come = []
        for step in steps:
            second = places[step][1]
            come.append(swap(tie(part_of(have[step], second, 1), 1), second))
        seen.append(tuple(come))
        for step in steps:
            second = places[step][1]
            own = part_of(have[step], second, 0)
            have[step] = jnp.where(same[second][step], own, come[step])
        stacked = tie(jnp.stack(have), 2)
        come = swap(stacked, 3)
        seen.append((come,))
        work = yield stacked
        come = after(come, *work[0])
        for step in steps:
            have[step] = jnp.where(same[3][step], have[step], come[step])[None]
        come = [swap(tie(have[step], 3), places[step][1]) for step in steps]
        seen.append(tuple(come))
        come = [after(value, *come, *work[1]) for value in come]
        have = [jnp.concatenate(pair, 0) for pair in zip(have, come)]
        come = [swap(tie(have[step], 4), places[step][0]) for step in steps]
        seen.append(tuple(come))
        yield have, come, seen

    def whole(have, come, behind, joined=False):
        come = after(come, *behind)
        pieces = [jnp.concatenate([have, come], 0)] if joined else [have, come]
        return pieces + [swap(piece, 0) for piece in pieces]

    def lags(cross):
        return jnp.dot(
            cross.reshape(kept * channels, 2 * num_bins),
            table,
            preferred_element_type=jnp.float32,
        )

    orders = [
        bit(me, 0) * 4 + bit(me, first) * 2 + bit(me, second) for first, second in places
    ]
    partners = [(i, i ^ 1) for i in range(tm)]
    send = broadcast(0)
    next(send)
    have, more, seen = send.send(((), ()))
    keep = broadcast(1, seen)
    work = []
    sent = []
    operand = next(keep)
    behind = []
    for step in steps:
        first, *rest = whole(have[step], more[step], behind, not step)
        work.append(cross_spectra(orders[step], (after(first, *sent), *rest), receivers))
        sent.append(lags(work[step]).astype(jnp.bfloat16))
        behind = work[:1]
    have, more, _ = keep.send((work[:1], sent[:1]))
    come = [lax.ppermute(value, "tm", partners) for value in sent]
    cross = []
    for step in steps:
        first, *rest = whole(have[step], more[step], work[1:])
        first = after(first, *sent, *cross, *come[:step])
        cross.append(cross_spectra(orders[step], (first, *rest), receivers))
    come = [after(value, cross[-1]) for value in come]
    outs = [lags(after(value, *come)) for value in cross]
    outs = lax.optimization_barrier(outs)
    outs = [
        (out + got.astype(jnp.float32)).reshape(kept, channels, LAG)
        for out, got in zip(outs, come)
    ]
    return jnp.stack(outs, 1)


def solution(mesh):
    return jax.shard_map(
        per_device,
        mesh=mesh,
        in_specs=(P("tm", "chan", None, None), P(), P("chan")),
        out_specs=P("tm", None, "chan", None),
        check_vma=False,
    )
```

```python
from functools import partial
import math

import jax
import jax.numpy as jnp
import numpy as np
from jax import lax
from jax.experimental import pallas as pl
from jax.experimental.pallas import tpu as pltpu
from jax.sharding import PartitionSpec as P

LAG = 512
STEPS = 2
LANES = 128
PACK = 16
BLOCKS = 8


def lag_table(num_bins, num_lags, windows):
    freq_bins = np.arange(num_bins, dtype=np.int64)[:, None]
    shifts = np.arange(num_lags, dtype=np.int64)[None, :] - num_lags // 2
    phases = np.mod(freq_bins * shifts, 2 * num_bins).astype(np.float32) * np.float32(
        math.pi / num_bins
    )
    scaling = np.float32(1.0 / math.sqrt(2.0 * num_bins * windows))
    table = np.concatenate([np.cos(phases) * scaling, -np.sin(phases) * scaling], 0)
    return jnp.asarray(table.astype(jnp.bfloat16))


def cross_kernel(place, *refs):
    *pieces, rcv_ref, cross_ref, src = refs
    blocks, windows, _, sources, bins = pieces[0].shape
    channels = rcv_ref.shape[2]
    num_bins = rcv_ref.shape[3]
    order = place[0]
    groups = range(0, channels, PACK)

    def widen(w, carry):
        for at, ref in enumerate(pieces):
            for entry in range(blocks):
                for part in range(2):
                    value = ref[entry, w, part].astype(jnp.float32)
                    for low in range(0, sources, 8):
                        src[at * blocks + entry, low // 8, 2 * w + part] = value[low : low + 8]
        return carry

    lax.fori_loop(0, windows, widen, 0)

    def lane_group(entry, lane):
        here = pl.multiple_of((entry ^ order) * bins + lane, LANES)
        there = pl.multiple_of(num_bins + here, LANES)
        lanes = pl.ds(lane, LANES)
        received = [
            [
                [rcv_ref[w, part, pl.ds(chan, PACK), pl.ds(here, LANES)] for chan in groups]
                for part in range(2)
            ]
            for w in range(windows)
        ]
        for s in range(sources):

            def summed(first, last):
                if last - first > 1:
                    middle = (first + last) // 2
                    left, right = summed(first, middle), summed(middle, last)
                    return [a + b for a, b in zip(left, right)]
                s_re, s_im = [
                    jnp.broadcast_to(
                        src[entry, s // 8, 2 * first + part, pl.ds(s % 8, 1), lanes], (PACK, LANES)
                    ).astype(jnp.bfloat16)
                    for part in range(2)
                ]
                values = []
                for c_re, c_im in zip(*received[first]):
                    values.append(s_re * c_re + s_im * c_im)
                    values.append(s_re * c_im - s_im * c_re)
                return values

            values = summed(0, windows)
            for g, chan in enumerate(groups):
                rows = pl.ds(chan, PACK)
                cross_ref[s, rows, pl.ds(here, LANES)] = values[2 * g]
                cross_ref[s, rows, pl.ds(there, LANES)] = values[2 * g + 1]

    def body(entry, carry):
        for lane in range(0, bins, LANES):
            lane_group(entry, lane)
        return carry

    lax.fori_loop(0, len(pieces) * blocks, body, 0)


@jax.jit
def cross_spectra(order, pieces, receivers):
    blocks, windows, _, sources, bins = pieces[0].shape
    channels, num_bins = receivers.shape[2:]
    vmem = pl.BlockSpec(memory_space=pltpu.VMEM)
    return pl.pallas_call(
        cross_kernel,
        in_specs=[pl.BlockSpec(memory_space=pltpu.SMEM)] + [vmem] * (len(pieces) + 1),
        out_specs=vmem,
        scratch_shapes=[
            pltpu.VMEM((len(pieces) * blocks, sources // 8, 2 * windows, 8, bins), jnp.float32)
        ],
        out_shape=jax.ShapeDtypeStruct((sources, channels, 2 * num_bins), jnp.bfloat16),
        compiler_params=pltpu.CompilerParams(vmem_limit_bytes=8 * 1024 * 1024),
        cost_estimate=pl.CostEstimate(
            flops=sources * channels * num_bins * windows * 8,
            bytes_accessed=sources * channels * num_bins,
            transcendentals=0,
        ),
    )(order[None], *pieces, receivers)


def after(value, *others):
    return lax.optimization_barrier((value,) + others)[0]


def per_device(spectra, src_block, quality):
    windows, channels, _, num_bins = spectra.shape
    tm = lax.axis_size("tm")
    chan = lax.axis_size("chan")
    me = lax.axis_index("chan")
    my_tm = lax.axis_index("tm")
    kept = channels // tm
    bit = lambda value, place: (value >> place) & 1
    swap = lambda value, place: lax.ppermute(
        value, "chan", [(i, i ^ (1 << place)) for i in range(chan)]
    )

    def cut(value, axis, start, size):
        at = [0] * value.ndim
        at[axis] = start
        sizes = list(value.shape)
        sizes[axis] = size
        return lax.dynamic_slice(value, at, sizes, allow_negative_indices=False)

    raw = lax.optimization_barrier(spectra.transpose(0, 2, 1, 3))
    half = num_bins // 2
    own_half = me & 1
    mine = cut(raw, 3, own_half * half, half)
    given = swap(cut(raw, 3, (own_half ^ 1) * half, half), 0)
    usable = quality.astype(jnp.float32)[None, :]
    wide = raw.astype(jnp.float32)
    power = jnp.mean(wide * wide, axis=(1, 3)) * usable
    scale = usable / jnp.sqrt(power + 1e-06)
    given_scale = swap(scale, 0)
    receivers = (wide * scale[:, None, :, None]).astype(jnp.bfloat16)
    table = lag_table(num_bins, LAG, windows * tm)

    steps = range(STEPS)
    apart = [src_block[step] ^ me for step in steps]

    def starts_of(size):
        out = []
        for place in (1, 2):
            own = me & (1 << place)
            out.append([own * (size >> place), (own ^ (1 << place)) * (size >> place)])
        return out

    def same_side(place):
        return [(apart[step] & (1 << place)) == 0 for step in steps]

    first_rows = [(1 - my_tm) * kept, my_tm * kept]
    given_scale, *early = lax.optimization_barrier(
        (given_scale, same_side(0), starts_of(half // 2), first_rows)
    )
    same, starts, first_rows = {0: early[0]}, {half // 2: early[1]}, early[2]

    def later_scalars(value):
        late = ([same_side(place) for place in (1, 2, 3)], starts_of(half // 4))
        value, (sides, starts[half // 4]) = lax.optimization_barrier((value, late))
        same.update(zip((1, 2, 3), sides))
        return value

    def part_of(value, place, other):
        size = value.shape[-1] // 2
        return cut(value, value.ndim - 1, starts[size][place - 1][other], size)

    def chosen(step, part, place, other):
        here = same[0][step]
        factor = jnp.where(here, scale, given_scale)
        value = jnp.where(here, part_of(mine, place, other), part_of(given, place, other))
        value = value.astype(jnp.float32) * factor[:, None, :, None]
        value = cut(value.astype(jnp.bfloat16), 2, first_rows[part], kept)
        if chan > 16:
            groups = [list(range(i, chan, 16)) for i in range(16)]
            value = jnp.where(src_block[step] // 16 == me // 16, value, 0)
            value = lax.psum(value, "chan", axis_index_groups=groups)
        return value

    places = [(1, 2) if step % 2 == 0 else (2, 1) for step in steps]

    def broadcast(part, ahead=None):
        tie = lambda value, phase: after(value, *ahead[max(phase, 1)]) if ahead else value
        seen = []
        have = []
        for step in steps:
            first = places[step][0]
            have.append(tie(chosen(step, part, first, 1), 0))
        have = [
            swap(value, places[step][0])
            for step, value in zip(steps, lax.optimization_barrier(tuple(have)))
        ]
        if not ahead:
            have = later_scalars(have)
        seen.append(tuple(have))
        for step in steps:
            first = places[step][0]
            have[step] = jnp.where(same[first][step], chosen(step, part, first, 0), have[step])
        come = []
        for step in steps:
            second = places[step][1]
            come.append(swap(tie(part_of(have[step], second, 1), 1), second))
        seen.append(tuple(come))
        for step in steps:
            second = places[step][1]
            own = part_of(have[step], second, 0)
            have[step] = jnp.where(same[second][step], own, come[step])
        stacked = tie(jnp.stack(have), 2)
        come = swap(stacked, 3)
        seen.append((come,))
        work = yield stacked
        come = after(come, *work[0])
        for step in steps:
            have[step] = jnp.where(same[3][step], have[step], come[step])[None]
        come = [swap(tie(have[step], 3), places[step][1]) for step in steps]
        seen.append(tuple(come))
        come = [after(value, *come, *work[1]) for value in come]
        have = [jnp.concatenate(pair, 0) for pair in zip(have, come)]
        come = [swap(tie(have[step], 4), places[step][0]) for step in steps]
        seen.append(tuple(come))
        yield have, come, seen

    def whole(have, come, behind, joined=False):
        come = after(come, *behind)
        pieces = [jnp.concatenate([have, come], 0)] if joined else [have, come]
        return pieces + [swap(piece, 0) for piece in pieces]

    def lags(cross):
        return jnp.dot(
            cross.reshape(kept * channels, 2 * num_bins),
            table,
            preferred_element_type=jnp.float32,
        )

    orders = [
        bit(me, 0) * 4 + bit(me, first) * 2 + bit(me, second) for first, second in places
    ]
    partners = [(i, i ^ 1) for i in range(tm)]
    send = broadcast(0)
    next(send)
    have, more, seen = send.send(((), ()))
    keep = broadcast(1, seen)
    work = []
    sent = []
    operand = next(keep)
    behind = []
    for step in steps:
        first, *rest = whole(have[step], more[step], behind, not step)
        work.append(cross_spectra(orders[step], (after(first, *sent), *rest), receivers))
        sent.append(lags(work[step]).astype(jnp.bfloat16))
        behind = work[:1]
    have, more, _ = keep.send((work[:1], sent[:1]))
    come = [lax.ppermute(value, "tm", partners) for value in sent]
    cross = []
    for step in steps:
        first, *rest = whole(have[step], more[step], work[1:])
        first = after(first, *sent, *cross, *come[:step])
        cross.append(cross_spectra(orders[step], (first, *rest), receivers))
    come = [after(value, cross[-1]) for value in come]
    outs = [lags(after(value, *come)) for value in cross]
    outs = lax.optimization_barrier(outs)
    outs = [
        (out + got.astype(jnp.float32)).reshape(kept, channels, LAG)
        for out, got in zip(outs, come)
    ]
    return jnp.stack(outs, 1)


def solution(mesh):
    return jax.shard_map(
        per_device,
        mesh=mesh,
        in_specs=(P("tm", "chan", None, None), P(), P("chan")),
        out_specs=P("tm", None, "chan", None),
        check_vma=False,
    )
```

```python
from functools import partial
import math

import jax
import jax.numpy as jnp
import numpy as np
from jax import lax
from jax.experimental import pallas as pl
from jax.experimental.pallas import tpu as pltpu
from jax.sharding import PartitionSpec as P

LAG = 512
STEPS = 2
LANES = 128
PACK = 16
BLOCKS = 8


def lag_table(num_bins, num_lags, windows):
    freq_bins = np.arange(num_bins, dtype=np.int64)[:, None]
    shifts = np.arange(num_lags, dtype=np.int64)[None, :] - num_lags // 2
    phases = np.mod(freq_bins * shifts, 2 * num_bins).astype(np.float32) * np.float32(
        math.pi / num_bins
    )
    scaling = np.float32(1.0 / math.sqrt(2.0 * num_bins * windows))
    table = np.concatenate([np.cos(phases) * scaling, -np.sin(phases) * scaling], 0)
    return jnp.asarray(table.astype(jnp.bfloat16))


def cross_kernel(place, *refs):
    *pieces, rcv_ref, cross_ref, src = refs
    blocks, windows, _, sources, bins = pieces[0].shape
    channels = rcv_ref.shape[2]
    num_bins = rcv_ref.shape[3]
    order = place[0]
    groups = range(0, channels, PACK)

    def widen(w, carry):
        for at, ref in enumerate(pieces):
            for entry in range(blocks):
                for part in range(2):
                    value = ref[entry, w, part].astype(jnp.float32)
                    for low in range(0, sources, 8):
                        src[at * blocks + entry, low // 8, 2 * w + part] = value[low : low + 8]
        return carry

    lax.fori_loop(0, windows, widen, 0)

    def lane_group(entry, lane):
        here = pl.multiple_of((entry ^ order) * bins + lane, LANES)
        there = pl.multiple_of(num_bins + here, LANES)
        lanes = pl.ds(lane, LANES)
        received = [
            [
                [rcv_ref[w, part, pl.ds(chan, PACK), pl.ds(here, LANES)] for chan in groups]
                for part in range(2)
            ]
            for w in range(windows)
        ]
        for s in range(sources):

            def summed(first, last):
                if last - first > 1:
                    middle = (first + last) // 2
                    left, right = summed(first, middle), summed(middle, last)
                    return [a + b for a, b in zip(left, right)]
                s_re, s_im = [
                    jnp.broadcast_to(
                        src[entry, s // 8, 2 * first + part, pl.ds(s % 8, 1), lanes], (PACK, LANES)
                    ).astype(jnp.bfloat16)
                    for part in range(2)
                ]
                values = []
                for c_re, c_im in zip(*received[first]):
                    values.append(s_re * c_re + s_im * c_im)
                    values.append(s_re * c_im - s_im * c_re)
                return values

            values = summed(0, windows)
            for g, chan in enumerate(groups):
                rows = pl.ds(chan, PACK)
                cross_ref[s, rows, pl.ds(here, LANES)] = values[2 * g]
                cross_ref[s, rows, pl.ds(there, LANES)] = values[2 * g + 1]

    def body(entry, carry):
        for lane in range(0, bins, LANES):
            lane_group(entry, lane)
        return carry

    lax.fori_loop(0, len(pieces) * blocks, body, 0)


@jax.jit
def cross_spectra(order, pieces, receivers):
    blocks, windows, _, sources, bins = pieces[0].shape
    channels, num_bins = receivers.shape[2:]
    vmem = pl.BlockSpec(memory_space=pltpu.VMEM)
    return pl.pallas_call(
        cross_kernel,
        in_specs=[pl.BlockSpec(memory_space=pltpu.SMEM)] + [vmem] * (len(pieces) + 1),
        out_specs=vmem,
        scratch_shapes=[
            pltpu.VMEM((len(pieces) * blocks, sources // 8, 2 * windows, 8, bins), jnp.float32)
        ],
        out_shape=jax.ShapeDtypeStruct((sources, channels, 2 * num_bins), jnp.bfloat16),
        compiler_params=pltpu.CompilerParams(vmem_limit_bytes=8 * 1024 * 1024),
        cost_estimate=pl.CostEstimate(
            flops=sources * channels * num_bins * windows * 8,
            bytes_accessed=sources * channels * num_bins,
            transcendentals=0,
        ),
    )(order[None], *pieces, receivers)


def after(value, *others):
    return lax.optimization_barrier((value,) + others)[0]


def per_device(spectra, src_block, quality):
    windows, channels, _, num_bins = spectra.shape
    tm = lax.axis_size("tm")
    chan = lax.axis_size("chan")
    me = lax.axis_index("chan")
    my_tm = lax.axis_index("tm")
    kept = channels // tm
    bit = lambda value, place: (value >> place) & 1
    swap = lambda value, place: lax.ppermute(
        value, "chan", [(i, i ^ (1 << place)) for i in range(chan)]
    )

    def cut(value, axis, start, size):
        at = [0] * value.ndim
        at[axis] = start
        sizes = list(value.shape)
        sizes[axis] = size
        return lax.dynamic_slice(value, at, sizes, allow_negative_indices=False)

    raw = lax.optimization_barrier(spectra.transpose(0, 2, 1, 3))
    half = num_bins // 2
    own_half = me & 1
    mine = cut(raw, 3, own_half * half, half)
    given = swap(cut(raw, 3, (own_half ^ 1) * half, half), 0)
    usable = quality.astype(jnp.float32)[None, :]
    wide = raw.astype(jnp.float32)
    power = jnp.mean(wide * wide, axis=(1, 3)) * usable
    scale = usable / jnp.sqrt(power + 1e-06)
    given_scale = swap(scale, 0)
    receivers = (wide * scale[:, None, :, None]).astype(jnp.bfloat16)
    table = lag_table(num_bins, LAG, windows * tm)

    steps = range(STEPS)
    apart = [src_block[step] ^ me for step in steps]

    def starts_of(size):
        out = []
        for place in (1, 2):
            own = bit(me, place)
            out.append([own * size, (1 - own) * size])
        return out

    def same_side(place):
        return [(apart[step] & (1 << place)) == 0 for step in steps]

    first_rows = [(1 - my_tm) * kept, my_tm * kept]
    same, starts = {0: same_side(0)}, {half // 2: starts_of(half // 2)}

    def later_scalars(value):
        late = ([same_side(place) for place in (1, 2, 3)], starts_of(half // 4))
        value, (sides, starts[half // 4]) = lax.optimization_barrier((value, late))
        same.update(zip((1, 2, 3), sides))
        return value

    def part_of(value, place, other):
        size = value.shape[-1] // 2
        return cut(value, value.ndim - 1, starts[size][place - 1][other], size)

    def chosen(step, part, place, other):
        here = same[0][step]
        factor = jnp.where(here, scale, given_scale)
        value = jnp.where(here, part_of(mine, place, other), part_of(given, place, other))
        value = value.astype(jnp.float32) * factor[:, None, :, None]
        value = cut(value.astype(jnp.bfloat16), 2, first_rows[part], kept)
        if chan > 16:
            groups = [list(range(i, chan, 16)) for i in range(16)]
            value = jnp.where(src_block[step] // 16 == me // 16, value, 0)
            value = lax.psum(value, "chan", axis_index_groups=groups)
        return value

    places = [(1, 2) if step % 2 == 0 else (2, 1) for step in steps]

    def broadcast(part, ahead=None):
        tie = lambda value, phase: after(value, *ahead[max(phase, 1)]) if ahead else value
        seen = []
        have = []
        for step in steps:
            first = places[step][0]
            have.append(tie(chosen(step, part, first, 1), 0))
        have = [
            swap(value, places[step][0])
            for step, value in zip(steps, lax.optimization_barrier(tuple(have)))
        ]
        if not ahead:
            have = later_scalars(have)
        seen.append(tuple(have))
        for step in steps:
            first = places[step][0]
            have[step] = jnp.where(same[first][step], chosen(step, part, first, 0), have[step])
        come = []
        for step in steps:
            second = places[step][1]
            come.append(swap(tie(part_of(have[step], second, 1), 1), second))
        seen.append(tuple(come))
        for step in steps:
            second = places[step][1]
            own = part_of(have[step], second, 0)
            have[step] = jnp.where(same[second][step], own, come[step])
        stacked = tie(jnp.stack(have), 2)
        come = swap(stacked, 3)
        seen.append((come,))
        work = yield stacked
        come = after(come, *work[0])
        for step in steps:
            have[step] = jnp.where(same[3][step], have[step], come[step])[None]
        come = [swap(tie(have[step], 3), places[step][1]) for step in steps]
        seen.append(tuple(come))
        come = [after(value, *come, *work[1]) for value in come]
        have = [jnp.concatenate(pair, 0) for pair in zip(have, come)]
        come = [swap(tie(have[step], 4), places[step][0]) for step in steps]
        seen.append(tuple(come))
        yield have, come, seen

    def whole(have, come, behind, joined=False):
        come = after(come, *behind)
        pieces = [jnp.concatenate([have, come], 0)] if joined else [have, come]
        return pieces + [swap(piece, 0) for piece in pieces]

    def lags(cross):
        return jnp.dot(
            cross.reshape(kept * channels, 2 * num_bins),
            table,
            preferred_element_type=jnp.float32,
        )

    orders = [
        bit(me, 0) * 4 + bit(me, first) * 2 + bit(me, second) for first, second in places
    ]
    partners = [(i, i ^ 1) for i in range(tm)]
    send = broadcast(0)
    next(send)
    have, more, seen = send.send(((), ()))
    keep = broadcast(1, seen)
    work = []
    sent = []
    operand = next(keep)
    behind = []
    for step in steps:
        first, *rest = whole(have[step], more[step], behind, not step)
        work.append(cross_spectra(orders[step], (after(first, *sent), *rest), receivers))
        sent.append(lags(work[step]).astype(jnp.bfloat16))
        behind = work[:1]
    have, more, _ = keep.send((work[:1], sent[:1]))
    come = [lax.ppermute(value, "tm", partners) for value in sent]
    cross = []
    for step in steps:
        first, *rest = whole(have[step], more[step], work[1:])
        first = after(first, *sent, *cross, *come[:step])
        cross.append(cross_spectra(orders[step], (first, *rest), receivers))
    come = [after(value, cross[-1]) for value in come]
    outs = [lags(after(value, *come)) for value in cross]
    outs = lax.optimization_barrier(outs)
    outs = [
        (out + got.astype(jnp.float32)).reshape(kept, channels, LAG)
        for out, got in zip(outs, come)
    ]
    return jnp.stack(outs, 1)


def solution(mesh):
    return jax.shard_map(
        per_device,
        mesh=mesh,
        in_specs=(P("tm", "chan", None, None), P(), P("chan")),
        out_specs=P("tm", None, "chan", None),
        check_vma=False,
    )
```

```python
from functools import partial
import math

import jax
import jax.numpy as jnp
import numpy as np
from jax import lax
from jax.experimental import pallas as pl
from jax.experimental.pallas import tpu as pltpu
from jax.sharding import PartitionSpec as P

LAG = 512
STEPS = 2
LANES = 128
PACK = 16
BLOCKS = 8


def lag_table(num_bins, num_lags, windows):
    freq_bins = np.arange(num_bins, dtype=np.int64)[:, None]
    shifts = np.arange(num_lags, dtype=np.int64)[None, :] - num_lags // 2
    phases = np.mod(freq_bins * shifts, 2 * num_bins).astype(np.float32) * np.float32(
        math.pi / num_bins
    )
    scaling = np.float32(1.0 / math.sqrt(2.0 * num_bins * windows))
    table = np.concatenate([np.cos(phases) * scaling, -np.sin(phases) * scaling], 0)
    return jnp.asarray(table.astype(jnp.bfloat16))


def cross_kernel(place, *refs):
    *pieces, rcv_ref, cross_ref, src = refs
    blocks, windows, _, sources, bins = pieces[0].shape
    channels = rcv_ref.shape[2]
    num_bins = rcv_ref.shape[3]
    order = place[0]
    groups = range(0, channels, PACK)

    def widen(w, carry):
        for at, ref in enumerate(pieces):
            for entry in range(blocks):
                for part in range(2):
                    value = ref[entry, w, part].astype(jnp.float32)
                    for low in range(0, sources, 8):
                        src[at * blocks + entry, low // 8, 2 * w + part] = value[low : low + 8]
        return carry

    lax.fori_loop(0, windows, widen, 0)

    def lane_group(entry, lane):
        here = pl.multiple_of((entry ^ order) * bins + lane, LANES)
        there = pl.multiple_of(num_bins + here, LANES)
        lanes = pl.ds(lane, LANES)
        received = [
            [
                [rcv_ref[w, part, pl.ds(chan, PACK), pl.ds(here, LANES)] for chan in groups]
                for part in range(2)
            ]
            for w in range(windows)
        ]
        for s in range(sources):

            def summed(first, last):
                if last - first > 1:
                    middle = (first + last) // 2
                    left, right = summed(first, middle), summed(middle, last)
                    return [a + b for a, b in zip(left, right)]
                s_re, s_im = [
                    jnp.broadcast_to(
                        src[entry, s // 8, 2 * first + part, pl.ds(s % 8, 1), lanes], (PACK, LANES)
                    ).astype(jnp.bfloat16)
                    for part in range(2)
                ]
                values = []
                for c_re, c_im in zip(*received[first]):
                    values.append(s_re * c_re + s_im * c_im)
                    values.append(s_re * c_im - s_im * c_re)
                return values

            values = summed(0, windows)
            for g, chan in enumerate(groups):
                rows = pl.ds(chan, PACK)
                cross_ref[s, rows, pl.ds(here, LANES)] = values[2 * g]
                cross_ref[s, rows, pl.ds(there, LANES)] = values[2 * g + 1]

    def body(entry, carry):
        for lane in range(0, bins, LANES):
            lane_group(entry, lane)
        return carry

    lax.fori_loop(0, len(pieces) * blocks, body, 0)


@jax.jit
def cross_spectra(order, pieces, receivers):
    blocks, windows, _, sources, bins = pieces[0].shape
    channels, num_bins = receivers.shape[2:]
    vmem = pl.BlockSpec(memory_space=pltpu.VMEM)
    return pl.pallas_call(
        cross_kernel,
        in_specs=[pl.BlockSpec(memory_space=pltpu.SMEM)] + [vmem] * (len(pieces) + 1),
        out_specs=vmem,
        scratch_shapes=[
            pltpu.VMEM((len(pieces) * blocks, sources // 8, 2 * windows, 8, bins), jnp.float32)
        ],
        out_shape=jax.ShapeDtypeStruct((sources, channels, 2 * num_bins), jnp.bfloat16),
        compiler_params=pltpu.CompilerParams(vmem_limit_bytes=8 * 1024 * 1024),
        cost_estimate=pl.CostEstimate(
            flops=sources * channels * num_bins * windows * 8,
            bytes_accessed=sources * channels * num_bins,
            transcendentals=0,
        ),
    )(order[None], *pieces, receivers)


def after(value, *others):
    return lax.optimization_barrier((value,) + others)[0]


def per_device(spectra, src_block, quality):
    windows, channels, _, num_bins = spectra.shape
    tm = lax.axis_size("tm")
    chan = lax.axis_size("chan")
    me = lax.axis_index("chan")
    my_tm = lax.axis_index("tm")
    kept = channels // tm
    bit = lambda value, place: (value >> place) & 1
    swap = lambda value, place: lax.ppermute(
        value, "chan", [(i, i ^ (1 << place)) for i in range(chan)]
    )

    def cut(value, axis, start, size):
        at = [0] * value.ndim
        at[axis] = start
        sizes = list(value.shape)
        sizes[axis] = size
        return lax.dynamic_slice(value, at, sizes, allow_negative_indices=False)

    raw = lax.optimization_barrier(spectra.transpose(0, 2, 1, 3))
    half = num_bins // 2
    own_half = me & 1
    mine = cut(raw, 3, own_half * half, half)
    given = swap(cut(raw, 3, (own_half ^ 1) * half, half), 0)
    usable = quality.astype(jnp.float32)[None, :]
    wide = raw.astype(jnp.float32)
    power = jnp.mean(wide * wide, axis=(1, 3)) * usable
    scale = usable / jnp.sqrt(power + 1e-06)
    given_scale = swap(scale, 0)
    receivers = (wide * scale[:, None, :, None]).astype(jnp.bfloat16)
    table = lag_table(num_bins, LAG, windows * tm)

    steps = range(STEPS)
    apart = [src_block[step] ^ me for step in steps]

    def starts_of(size):
        out = []
        for place in (1, 2):
            own = bit(me, place)
            out.append([own * size, (1 - own) * size])
        return out

    def same_side(place):
        return [(apart[step] & (1 << place)) == 0 for step in steps]

    first_rows = [(1 - my_tm) * kept, my_tm * kept]
    same, starts = {0: same_side(0)}, {half // 2: starts_of(half // 2)}

    def later_scalars(value):
        late = ([same_side(place) for place in (1, 2, 3)], starts_of(half // 4))
        value, (sides, starts[half // 4]) = lax.optimization_barrier((value, late))
        same.update(zip((1, 2, 3), sides))
        return value

    def part_of(value, place, other):
        size = value.shape[-1] // 2
        return cut(value, value.ndim - 1, starts[size][place - 1][other], size)

    def chosen(step, part, place, other, *behind):
        here = same[0][step]
        factor = jnp.where(here, scale, given_scale)
        factor = cut(factor, 1, first_rows[part], kept)
        pieces = []
        for value in (mine, given):
            value = after(value, *behind) if behind else value
            pieces.append(cut(part_of(value, place, other), 2, first_rows[part], kept))
        value = jnp.where(here, *pieces).astype(jnp.float32) * factor[:, None, :, None]
        value = value.astype(jnp.bfloat16)
        if chan > 16:
            groups = [list(range(i, chan, 16)) for i in range(16)]
            value = jnp.where(src_block[step] // 16 == me // 16, value, 0)
            value = lax.psum(value, "chan", axis_index_groups=groups)
        return value

    places = [(1, 2) if step % 2 == 0 else (2, 1) for step in steps]

    def broadcast(part, ahead=None):
        tie = lambda value, phase: after(value, *ahead[max(phase, 1)]) if ahead else value
        seen = []
        have = []
        for step in steps:
            first = places[step][0]
            have.append(chosen(step, part, first, 1, *(ahead[1] if ahead else ())))
        have = [
            swap(value, places[step][0])
            for step, value in zip(steps, lax.optimization_barrier(tuple(have)))
        ]
        if not ahead:
            have = later_scalars(have)
        seen.append(tuple(have))
        for step in steps:
            first = places[step][0]
            have[step] = jnp.where(
                same[first][step],
                chosen(step, part, first, 0, *(ahead[1] if ahead else ())),
                have[step],
            )
        come = []
        for step in steps:
            second = places[step][1]
            come.append(swap(tie(part_of(have[step], second, 1), 1), second))
        seen.append(tuple(come))
        for step in steps:
            second = places[step][1]
            own = part_of(have[step], second, 0)
            have[step] = jnp.where(same[second][step], own, come[step])
        stacked = tie(jnp.stack(have), 2)
        come = swap(stacked, 3)
        seen.append((come,))
        work = yield stacked
        come = after(come, *work[0])
        for step in steps:
            have[step] = jnp.where(same[3][step], have[step], come[step])[None]
        come = [swap(tie(have[step], 3), places[step][1]) for step in steps]
        seen.append(tuple(come))
        come = [after(value, *come, *work[1]) for value in come]
        have = [jnp.concatenate(pair, 0) for pair in zip(have, come)]
        come = [swap(tie(have[step], 4), places[step][0]) for step in steps]
        seen.append(tuple(come))
        yield have, come, seen

    def whole(have, come, behind, joined=False):
        come = after(come, *behind)
        pieces = [jnp.concatenate([have, come], 0)] if joined else [have, come]
        return pieces + [swap(piece, 0) for piece in pieces]

    def lags(cross):
        return jnp.dot(
            cross.reshape(kept * channels, 2 * num_bins),
            table,
            preferred_element_type=jnp.float32,
        )

    orders = [
        bit(me, 0) * 4 + bit(me, first) * 2 + bit(me, second) for first, second in places
    ]
    partners = [(i, i ^ 1) for i in range(tm)]
    send = broadcast(0)
    next(send)
    have, more, seen = send.send(((), ()))
    keep = broadcast(1, seen)
    work = []
    sent = []
    operand = next(keep)
    behind = []
    for step in steps:
        first, *rest = whole(have[step], more[step], behind, not step)
        work.append(cross_spectra(orders[step], (after(first, *sent), *rest), receivers))
        sent.append(lags(work[step]).astype(jnp.bfloat16))
        behind = work[:1]
    have, more, _ = keep.send((work[:1], sent[:1]))
    come = [lax.ppermute(value, "tm", partners) for value in sent]
    cross = []
    for step in steps:
        first, *rest = whole(have[step], more[step], work[1:])
        first = after(first, *sent, *cross, *come[:step])
        cross.append(cross_spectra(orders[step], (first, *rest), receivers))
    come = [after(value, cross[-1]) for value in come]
    outs = [lags(after(value, *come)) for value in cross]
    outs = lax.optimization_barrier(outs)
    outs = [
        (out + got.astype(jnp.float32)).reshape(kept, channels, LAG)
        for out, got in zip(outs, come)
    ]
    return jnp.stack(outs, 1)


def solution(mesh):
    return jax.shard_map(
        per_device,
        mesh=mesh,
        in_specs=(P("tm", "chan", None, None), P(), P("chan")),
        out_specs=P("tm", None, "chan", None),
        check_vma=False,
    )
```

```python
from functools import partial
import math

import jax
import jax.numpy as jnp
import numpy as np
from jax import lax
from jax.experimental import pallas as pl
from jax.experimental.pallas import tpu as pltpu
from jax.sharding import PartitionSpec as P

LAG = 512
STEPS = 2
LANES = 128
PACK = 16
BLOCKS = 8


def lag_table(num_bins, num_lags, windows):
    freq_bins = np.arange(num_bins, dtype=np.int64)[:, None]
    shifts = np.arange(num_lags, dtype=np.int64)[None, :] - num_lags // 2
    phases = np.mod(freq_bins * shifts, 2 * num_bins).astype(np.float32) * np.float32(
        math.pi / num_bins
    )
    scaling = np.float32(1.0 / math.sqrt(2.0 * num_bins * windows))
    table = np.concatenate([np.cos(phases) * scaling, -np.sin(phases) * scaling], 0)
    return jnp.asarray(table.astype(jnp.bfloat16))


def cross_kernel(place, *refs):
    *pieces, rcv_ref, cross_ref, src = refs
    blocks, windows, _, sources, bins = pieces[0].shape
    channels = rcv_ref.shape[2]
    num_bins = rcv_ref.shape[3]
    order = place[0]
    groups = range(0, channels, PACK)

    def widen(w, carry):
        for at, ref in enumerate(pieces):
            for entry in range(blocks):
                for part in range(2):
                    value = ref[entry, w, part].astype(jnp.float32)
                    for low in range(0, sources, 8):
                        src[at * blocks + entry, low // 8, 2 * w + part] = value[low : low + 8]
        return carry

    lax.fori_loop(0, windows, widen, 0)

    def lane_group(entry, lane):
        here = pl.multiple_of((entry ^ order) * bins + lane, LANES)
        there = pl.multiple_of(num_bins + here, LANES)
        lanes = pl.ds(lane, LANES)
        received = [
            [
                [rcv_ref[w, part, pl.ds(chan, PACK), pl.ds(here, LANES)] for chan in groups]
                for part in range(2)
            ]
            for w in range(windows)
        ]
        for s in range(sources):

            def summed(first, last):
                if last - first > 1:
                    middle = (first + last) // 2
                    left, right = summed(first, middle), summed(middle, last)
                    return [a + b for a, b in zip(left, right)]
                s_re, s_im = [
                    jnp.broadcast_to(
                        src[entry, s // 8, 2 * first + part, pl.ds(s % 8, 1), lanes], (PACK, LANES)
                    ).astype(jnp.bfloat16)
                    for part in range(2)
                ]
                values = []
                for c_re, c_im in zip(*received[first]):
                    values.append(s_re * c_re + s_im * c_im)
                    values.append(s_re * c_im - s_im * c_re)
                return values

            values = summed(0, windows)
            for g, chan in enumerate(groups):
                rows = pl.ds(chan, PACK)
                cross_ref[s, rows, pl.ds(here, LANES)] = values[2 * g]
                cross_ref[s, rows, pl.ds(there, LANES)] = values[2 * g + 1]

    def body(entry, carry):
        for lane in range(0, bins, LANES):
            lane_group(entry, lane)
        return carry

    lax.fori_loop(0, len(pieces) * blocks, body, 0)


@jax.jit
def cross_spectra(order, pieces, receivers):
    blocks, windows, _, sources, bins = pieces[0].shape
    channels, num_bins = receivers.shape[2:]
    vmem = pl.BlockSpec(memory_space=pltpu.VMEM)
    return pl.pallas_call(
        cross_kernel,
        in_specs=[pl.BlockSpec(memory_space=pltpu.SMEM)] + [vmem] * (len(pieces) + 1),
        out_specs=vmem,
        scratch_shapes=[
            pltpu.VMEM((len(pieces) * blocks, sources // 8, 2 * windows, 8, bins), jnp.float32)
        ],
        out_shape=jax.ShapeDtypeStruct((sources, channels, 2 * num_bins), jnp.bfloat16),
        compiler_params=pltpu.CompilerParams(vmem_limit_bytes=4 * 1024 * 1024),
        cost_estimate=pl.CostEstimate(
            flops=sources * channels * num_bins * windows * 8,
            bytes_accessed=sources * channels * num_bins,
            transcendentals=0,
        ),
    )(order[None], *pieces, receivers)


def after(value, *others):
    return lax.optimization_barrier((value,) + others)[0]


def per_device(spectra, src_block, quality):
    windows, channels, _, num_bins = spectra.shape
    tm = lax.axis_size("tm")
    chan = lax.axis_size("chan")
    me = lax.axis_index("chan")
    my_tm = lax.axis_index("tm")
    kept = channels // tm
    bit = lambda value, place: (value >> place) & 1
    swap = lambda value, place: lax.ppermute(
        value, "chan", [(i, i ^ (1 << place)) for i in range(chan)]
    )

    def cut(value, axis, start, size):
        at = [0] * value.ndim
        at[axis] = start
        sizes = list(value.shape)
        sizes[axis] = size
        return lax.dynamic_slice(value, at, sizes, allow_negative_indices=False)

    raw = lax.optimization_barrier(spectra.transpose(0, 2, 1, 3))
    half = num_bins // 2
    own_half = me & 1
    mine = cut(raw, 3, own_half * half, half)
    given = swap(cut(raw, 3, (own_half ^ 1) * half, half), 0)
    usable = quality.astype(jnp.float32)[None, :]
    wide = raw.astype(jnp.float32)
    power = jnp.mean(wide * wide, axis=(1, 3)) * usable
    scale = usable / jnp.sqrt(power + 1e-06)
    given_scale = swap(scale, 0)
    receivers = (wide * scale[:, None, :, None]).astype(jnp.bfloat16)
    table = lag_table(num_bins, LAG, windows * tm)

    steps = range(STEPS)
    apart = [src_block[step] ^ me for step in steps]

    def starts_of(size):
        out = []
        for place in (1, 2):
            own = bit(me, place)
            out.append([own * size, (1 - own) * size])
        return out

    def same_side(place):
        return [(apart[step] & (1 << place)) == 0 for step in steps]

    first_rows = [(1 - my_tm) * kept, my_tm * kept]
    same, starts = {0: same_side(0)}, {half // 2: starts_of(half // 2)}

    def later_scalars(value):
        late = ([same_side(place) for place in (1, 2, 3)], starts_of(half // 4))
        value, (sides, starts[half // 4]) = lax.optimization_barrier((value, late))
        same.update(zip((1, 2, 3), sides))
        return value

    def part_of(value, place, other):
        size = value.shape[-1] // 2
        return cut(value, value.ndim - 1, starts[size][place - 1][other], size)

    def chosen(step, part, place, other):
        here = same[0][step]
        factor = jnp.where(here, scale, given_scale)
        value = jnp.where(here, part_of(mine, place, other), part_of(given, place, other))
        value = value.astype(jnp.float32) * factor[:, None, :, None]
        value = cut(value.astype(jnp.bfloat16), 2, first_rows[part], kept)
        if chan > 16:
            groups = [list(range(i, chan, 16)) for i in range(16)]
            value = jnp.where(src_block[step] // 16 == me // 16, value, 0)
            value = lax.psum(value, "chan", axis_index_groups=groups)
        return value

    places = [(1, 2) if step % 2 == 0 else (2, 1) for step in steps]

    def broadcast(part, ahead=None):
        tie = lambda value, phase: after(value, *ahead[max(phase, 1)]) if ahead else value
        seen = []
        have = []
        for step in steps:
            first = places[step][0]
            have.append(tie(chosen(step, part, first, 1), 0))
        have = [
            swap(value, places[step][0])
            for step, value in zip(steps, lax.optimization_barrier(tuple(have)))
        ]
        if not ahead:
            have = later_scalars(have)
        seen.append(tuple(have))
        for step in steps:
            first = places[step][0]
            have[step] = jnp.where(same[first][step], chosen(step, part, first, 0), have[step])
        come = []
        for step in steps:
            second = places[step][1]
            come.append(swap(tie(part_of(have[step], second, 1), 1), second))
        seen.append(tuple(come))
        for step in steps:
            second = places[step][1]
            own = part_of(have[step], second, 0)
            have[step] = jnp.where(same[second][step], own, come[step])
        stacked = tie(jnp.stack(have), 2)
        come = swap(stacked, 3)
        seen.append((come,))
        work = yield stacked
        come = after(come, *work[0])
        for step in steps:
            have[step] = jnp.where(same[3][step], have[step], come[step])[None]
        come = [swap(tie(have[step], 3), places[step][1]) for step in steps]
        seen.append(tuple(come))
        come = [after(value, *come, *work[1]) for value in come]
        have = [jnp.concatenate(pair, 0) for pair in zip(have, come)]
        come = [swap(tie(have[step], 4), places[step][0]) for step in steps]
        seen.append(tuple(come))
        yield have, come, seen

    def whole(have, come, behind, joined=False):
        come = after(come, *behind)
        pieces = [jnp.concatenate([have, come], 0)] if joined else [have, come]
        return pieces + [swap(piece, 0) for piece in pieces]

    def lags(cross):
        return jnp.dot(
            cross.reshape(kept * channels, 2 * num_bins),
            table,
            preferred_element_type=jnp.float32,
        )

    orders = [
        bit(me, 0) * 4 + bit(me, first) * 2 + bit(me, second) for first, second in places
    ]
    partners = [(i, i ^ 1) for i in range(tm)]
    send = broadcast(0)
    next(send)
    have, more, seen = send.send(((), ()))
    keep = broadcast(1, seen)
    work = []
    sent = []
    operand = next(keep)
    behind = []
    for step in steps:
        first, *rest = whole(have[step], more[step], behind, not step)
        work.append(cross_spectra(orders[step], (after(first, *sent), *rest), receivers))
        sent.append(lags(work[step]).astype(jnp.bfloat16))
        behind = work[:1]
    have, more, _ = keep.send((work[:1], sent[:1]))
    come = [lax.ppermute(value, "tm", partners) for value in sent]
    cross = []
    for step in steps:
        first, *rest = whole(have[step], more[step], work[1:])
        first = after(first, *sent, *cross, *come[:step])
        cross.append(cross_spectra(orders[step], (first, *rest), receivers))
    come = [after(value, cross[-1]) for value in come]
    outs = [lags(after(value, *come)) for value in cross]
    outs = [
        (out + got.astype(jnp.float32)).reshape(kept, channels, LAG)
        for out, got in zip(outs, come)
    ]
    return jnp.stack(outs, 1)


def solution(mesh):
    return jax.shard_map(
        per_device,
        mesh=mesh,
        in_specs=(P("tm", "chan", None, None), P(), P("chan")),
        out_specs=P("tm", None, "chan", None),
        check_vma=False,
    )
```

```python
from functools import partial
import math

import jax
import jax.numpy as jnp
import numpy as np
from jax import lax
from jax.experimental import pallas as pl
from jax.experimental.pallas import tpu as pltpu
from jax.sharding import PartitionSpec as P

LAG = 512
STEPS = 2
LANES = 128
PACK = 16
BLOCKS = 8


def lag_table(num_bins, num_lags, windows):
    freq_bins = np.arange(num_bins, dtype=np.int64)[:, None]
    shifts = np.arange(num_lags, dtype=np.int64)[None, :] - num_lags // 2
    phases = np.mod(freq_bins * shifts, 2 * num_bins).astype(np.float32) * np.float32(
        math.pi / num_bins
    )
    scaling = np.float32(1.0 / math.sqrt(2.0 * num_bins * windows))
    table = np.concatenate([np.cos(phases) * scaling, -np.sin(phases) * scaling], 0)
    return jnp.asarray(table.astype(jnp.bfloat16))


def cross_kernel(place, *refs):
    *pieces, rcv_ref, cross_ref, src = refs
    blocks, windows, _, sources, bins = pieces[0].shape
    channels = rcv_ref.shape[2]
    num_bins = rcv_ref.shape[3]
    order = place[0]
    groups = range(0, channels, PACK)

    def widen(w, carry):
        for at, ref in enumerate(pieces):
            for entry in range(blocks):
                for part in range(2):
                    value = ref[entry, w, part].astype(jnp.float32)
                    for low in range(0, sources, 8):
                        src[at * blocks + entry, low // 8, 2 * w + part] = value[low : low + 8]
        return carry

    lax.fori_loop(0, windows, widen, 0)

    def lane_group(entry, lane):
        here = pl.multiple_of((entry ^ order) * bins + lane, LANES)
        there = pl.multiple_of(num_bins + here, LANES)
        lanes = pl.ds(lane, LANES)
        received = [
            [
                [rcv_ref[w, part, pl.ds(chan, PACK), pl.ds(here, LANES)] for chan in groups]
                for part in range(2)
            ]
            for w in range(windows)
        ]
        for s in range(sources):

            def summed(first, last):
                if last - first > 1:
                    middle = (first + last) // 2
                    left, right = summed(first, middle), summed(middle, last)
                    return [a + b for a, b in zip(left, right)]
                s_re, s_im = [
                    jnp.broadcast_to(
                        src[entry, s // 8, 2 * first + part, pl.ds(s % 8, 1), lanes], (PACK, LANES)
                    ).astype(jnp.bfloat16)
                    for part in range(2)
                ]
                values = []
                for c_re, c_im in zip(*received[first]):
                    values.append(s_re * c_re + s_im * c_im)
                    values.append(s_re * c_im - s_im * c_re)
                return values

            values = summed(0, windows)
            for g, chan in enumerate(groups):
                rows = pl.ds(chan, PACK)
                cross_ref[s, rows, pl.ds(here, LANES)] = values[2 * g]
                cross_ref[s, rows, pl.ds(there, LANES)] = values[2 * g + 1]

    def body(entry, carry):
        for lane in range(0, bins, LANES):
            lane_group(entry, lane)
        return carry

    lax.fori_loop(0, len(pieces) * blocks, body, 0)


@jax.jit
def cross_spectra(order, pieces, receivers):
    blocks, windows, _, sources, bins = pieces[0].shape
    channels, num_bins = receivers.shape[2:]
    vmem = pl.BlockSpec(memory_space=pltpu.VMEM)
    return pl.pallas_call(
        cross_kernel,
        in_specs=[pl.BlockSpec(memory_space=pltpu.SMEM)] + [vmem] * (len(pieces) + 1),
        out_specs=vmem,
        scratch_shapes=[
            pltpu.VMEM((len(pieces) * blocks, sources // 8, 2 * windows, 8, bins), jnp.float32)
        ],
        out_shape=jax.ShapeDtypeStruct((sources, channels, 2 * num_bins), jnp.bfloat16),
        compiler_params=pltpu.CompilerParams(vmem_limit_bytes=4 * 1024 * 1024),
        cost_estimate=pl.CostEstimate(
            flops=sources * channels * num_bins * windows * 8,
            bytes_accessed=sources * channels * num_bins,
            transcendentals=0,
        ),
    )(order[None], *pieces, receivers)


def after(value, *others):
    return lax.optimization_barrier((value,) + others)[0]


def per_device(spectra, src_block, quality):
    windows, channels, _, num_bins = spectra.shape
    tm = lax.axis_size("tm")
    chan = lax.axis_size("chan")
    me = lax.axis_index("chan")
    my_tm = lax.axis_index("tm")
    kept = channels // tm
    bit = lambda value, place: (value >> place) & 1
    swap = lambda value, place: lax.ppermute(
        value, "chan", [(i, i ^ (1 << place)) for i in range(chan)]
    )

    def cut(value, axis, start, size):
        at = [0] * value.ndim
        at[axis] = start
        sizes = list(value.shape)
        sizes[axis] = size
        return lax.dynamic_slice(value, at, sizes, allow_negative_indices=False)

    raw = lax.optimization_barrier(spectra.transpose(0, 2, 1, 3))
    half = num_bins // 2
    own_half = me & 1
    mine = cut(raw, 3, own_half * half, half)
    given = swap(cut(raw, 3, (own_half ^ 1) * half, half), 0)
    usable = quality.astype(jnp.float32)[None, :]
    wide = raw.astype(jnp.float32)
    power = jnp.mean(wide * wide, axis=(1, 3)) * usable
    scale = usable / jnp.sqrt(power + 1e-06)
    given_scale = swap(scale, 0)
    receivers = (wide * scale[:, None, :, None]).astype(jnp.bfloat16)
    table = lag_table(num_bins, LAG, windows * tm)

    steps = range(STEPS)
    apart = [src_block[step] ^ me for step in steps]

    def starts_of(size):
        out = []
        for place in (1, 2):
            own = bit(me, place)
            out.append([own * size, (1 - own) * size])
        return out

    def same_side(place):
        return [(apart[step] & (1 << place)) == 0 for step in steps]

    first_rows = [(1 - my_tm) * kept, my_tm * kept]
    same, starts = {0: same_side(0)}, {half // 2: starts_of(half // 2)}

    def later_scalars(value):
        late = ([same_side(place) for place in (1, 2, 3)], starts_of(half // 4))
        value, (sides, starts[half // 4]) = lax.optimization_barrier((value, late))
        same.update(zip((1, 2, 3), sides))
        return value

    def part_of(value, place, other):
        size = value.shape[-1] // 2
        return cut(value, value.ndim - 1, starts[size][place - 1][other], size)

    def chosen(step, part, place, other):
        here = same[0][step]
        factor = jnp.where(here, scale, given_scale)
        value = jnp.where(here, part_of(mine, place, other), part_of(given, place, other))
        value = value.astype(jnp.float32) * factor[:, None, :, None]
        value = cut(value.astype(jnp.bfloat16), 2, first_rows[part], kept)
        if chan > 16:
            groups = [list(range(i, chan, 16)) for i in range(16)]
            value = jnp.where(src_block[step] // 16 == me // 16, value, 0)
            value = lax.psum(value, "chan", axis_index_groups=groups)
        return value

    places = [(1, 2) if step % 2 == 0 else (2, 1) for step in steps]

    def broadcast(part, ahead=None):
        tie = lambda value, phase: after(value, *ahead[max(phase, 1)]) if ahead else value
        seen = []
        have = []
        for step in steps:
            first = places[step][0]
            have.append(tie(chosen(step, part, first, 1), 0))
        have = [
            swap(value, places[step][0])
            for step, value in zip(steps, lax.optimization_barrier(tuple(have)))
        ]
        if not ahead:
            have[0] = later_scalars(have[0])
        seen.append(tuple(have))
        for step in steps:
            first = places[step][0]
            have[step] = jnp.where(same[first][step], chosen(step, part, first, 0), have[step])
        come = []
        for step in steps:
            second = places[step][1]
            come.append(swap(tie(part_of(have[step], second, 1), 1), second))
        seen.append(tuple(come))
        for step in steps:
            second = places[step][1]
            own = part_of(have[step], second, 0)
            have[step] = jnp.where(same[second][step], own, come[step])
        stacked = tie(jnp.stack(have), 2)
        come = swap(stacked, 3)
        seen.append((come,))
        work = yield stacked
        come = after(come, *work[0])
        for step in steps:
            have[step] = jnp.where(same[3][step], have[step], come[step])[None]
        come = [swap(tie(have[step], 3), places[step][1]) for step in steps]
        seen.append(tuple(come))
        come = [after(value, *come, *work[1]) for value in come]
        have = [jnp.concatenate(pair, 0) for pair in zip(have, come)]
        come = [swap(tie(have[step], 4), places[step][0]) for step in steps]
        seen.append(tuple(come))
        yield have, come, seen

    def whole(have, come, behind, joined=False):
        come = after(come, *behind)
        pieces = [jnp.concatenate([have, come], 0)] if joined else [have, come]
        return pieces + [swap(piece, 0) for piece in pieces]

    def lags(cross):
        return jnp.dot(
            cross.reshape(kept * channels, 2 * num_bins),
            table,
            preferred_element_type=jnp.float32,
        )

    orders = [
        bit(me, 0) * 4 + bit(me, first) * 2 + bit(me, second) for first, second in places
    ]
    partners = [(i, i ^ 1) for i in range(tm)]
    send = broadcast(0)
    next(send)
    have, more, seen = send.send(((), ()))
    keep = broadcast(1, seen)
    work = []
    sent = []
    operand = next(keep)
    behind = []
    for step in steps:
        first, *rest = whole(have[step], more[step], behind, not step)
        work.append(cross_spectra(orders[step], (after(first, *sent), *rest), receivers))
        sent.append(lags(work[step]).astype(jnp.bfloat16))
        behind = work[:1]
    have, more, _ = keep.send((work[:1], sent[:1]))
    come = [lax.ppermute(value, "tm", partners) for value in sent]
    cross = []
    for step in steps:
        first, *rest = whole(have[step], more[step], work[1:])
        first = after(first, *sent, *cross, *come[:step])
        cross.append(cross_spectra(orders[step], (first, *rest), receivers))
    come = [after(value, cross[-1]) for value in come]
    outs = [lags(after(value, *come)) for value in cross]
    outs = [
        (out + got.astype(jnp.float32)).reshape(kept, channels, LAG)
        for out, got in zip(outs, come)
    ]
    return jnp.stack(outs, 1)


def solution(mesh):
    return jax.shard_map(
        per_device,
        mesh=mesh,
        in_specs=(P("tm", "chan", None, None), P(), P("chan")),
        out_specs=P("tm", None, "chan", None),
        check_vma=False,
    )
```
